32 devices in a mesh: groups: 2 (over y), row: 4 (over x, core), col: 4 (over z).
Axes of the slice: x: 2, y: 2, z: 4, core: 2. Of those that a mesh axis runs over, the one named last changes fastest.
Arguments:
- pair: bfloat16 [192, 96, 128], P(('groups', 'row'), 'col'), parts along dimension 0, may hold values from -6 to 6
- token_mask: int32 [192], P('groups'), parts along dimension 0, may hold values from 0 to 1, as said below
- in_gain: float32 [2, 128], replicated, may hold values from 0.25 to 1.75
- in_shift: float32 [2, 128], replicated, may hold values from -3 to 3
- w_in: bfloat16 [2, 128, 640], replicated, may hold values from -0.5 to 0.5
- bias_in: float32 [2, 640], replicated, may hold values from -3 to 3
- out_gain: float32 [2, 128], replicated, may hold values from 0.25 to 1.75
- out_shift: float32 [2, 128], replicated, may hold values from -3 to 3
- w_out: bfloat16 [2, 128, 128], replicated, may hold values from -0.5 to 0.5
- bias_out: float32 [2, 128], replicated, may hold values from -3 to 3
Outputs:
- pair_out: bfloat16 [192, 96, 128], P(('groups', 'row'), 'col'), parts along dimension 0
The draws below stay inside these ranges and needn't reach their ends.
There are 2 independent parts, one for each index of `groups`. The reference program is written for one: setup_inputs(seed, part) draws one part's arguments, and reference() takes and returns one part's arrays. A program takes and returns all parts, laid end to end along the dimension named above; an argument that names none is the same for every part. Nothing has to cross between parts.
Inputs may be any that keep to these rules, and one draw needn't show every extreme that they name: token_mask is 1 on the first L tokens and 0 on the rest, with 48 <= L < 96.
All inputs are finite; a program needn't handle non-finite values.
Results may differ from the reference program's by a relative error of at most 0.0085.
Values may be sent and summed in bfloat16 or wider, within the bound.
No kernel may reach another device: no remote copies, remote signals or barrier semaphores. Data moves between devices by JAX's collectives and lax.ppermute only.
A program may use at most 64 MiB of HBM per device.

```python
import jax
import jax.numpy as jnp
from jax import lax

C = 128
H = 128
N = 96


def draw_token_mask(key, part):
    key = jax.random.fold_in(key, 7)
    length = jax.random.randint(key, (), N // 2, N)
    return (jnp.arange(N) < length).astype(jnp.int32)


def block_scale(own_key, extent, pieces, smallest, high):
    level, own = 1.0, jax.random.fold_in(own_key, 6)
    for position, parts in pieces:
        heights = jnp.exp(jax.random.uniform(jax.random.fold_in(own, position), (parts,), jnp.float32, smallest / len(pieces), high / len(pieces)))
        level = level * jnp.repeat(heights, extent[position] // parts).reshape([-1 if axis == position else 1 for axis in range(len(extent))])
    return level


def normal_values(rng, extent, scale, reach, split=(), held_as=jnp.bfloat16):
    array = jax.random.normal(rng, extent, jnp.float32) * scale
    if len(split) > 0:
        array = block_scale(rng, extent, split, -0.22, 0.18) * array
    return jnp.clip(array, min=-reach, max=reach).astype(held_as)


def setup_inputs(seed: int = 0, part: int = 0) -> dict:
    keys = jax.random.split(jax.random.key(seed), 11)
    own_keys = jax.random.split(jax.random.fold_in(keys[10], part), 11)
    return {
        "pair": normal_values(own_keys[0], (N, N, C), 1.0, 6.0, ((0, 4), (1, 4))),
        "token_mask": draw_token_mask(jax.random.fold_in(jax.random.fold_in(keys[10], part), 71), part),
        "in_gain": jnp.clip(1.0 + 0.15 * jax.random.normal(keys[2], (2, C), jnp.float32), 0.25, 1.75),
        "in_shift": normal_values(keys[3], (2, C), 0.5, 3.0, (), jnp.float32),
        "w_in": normal_values(keys[4], (2, C, 4 * H + C), C ** -0.5, 0.5),
        "bias_in": normal_values(keys[5], (2, 4 * H + C), 0.5, 3.0, (), jnp.float32),
        "out_gain": jnp.clip(1.0 + 0.15 * jax.random.normal(keys[6], (2, H), jnp.float32), 0.25, 1.75),
        "out_shift": normal_values(keys[7], (2, H), 0.5, 3.0, (), jnp.float32),
        "w_out": normal_values(keys[8], (2, H, C), H ** -0.5, 0.5),
        "bias_out": normal_values(keys[9], (2, C), 0.5, 3.0, (), jnp.float32),
    }


def norm_rows(values, gain, shift):
    center = values - lax.optimization_barrier(jnp.mean(values, axis=-1, keepdims=True))
    spread = lax.optimization_barrier(jnp.mean(center * center, axis=-1, keepdims=True))
    return center * lax.rsqrt(spread + 1e-05) * gain + shift

def triangle(pair, grid, index, in_gain, in_shift, w_in, bias_in, out_gain, out_shift, w_out, bias_out, incoming):
    normed = norm_rows(pair.astype(jnp.float32), in_gain[index], in_shift[index]).astype(jnp.bfloat16)
    product = jnp.dot(normed, w_in[index], preferred_element_type=jnp.float32) + bias_in[index]
    left_side = (jax.nn.sigmoid(product[..., H:2 * H]) * product[..., :H] * grid[..., None]).astype(jnp.bfloat16)
    right_side = (jax.nn.sigmoid(product[..., 3 * H:4 * H]) * product[..., 2 * H:3 * H] * grid[..., None]).astype(jnp.bfloat16)
    gating = jax.nn.sigmoid(product[..., 4 * H:])
    if incoming:
        mixture = jnp.einsum('kih,kjh->ijh', left_side.astype(jnp.float32), right_side.astype(jnp.float32), precision=lax.Precision.HIGHEST)
    else:
        mixture = jnp.einsum('ikh,jkh->ijh', left_side.astype(jnp.float32), right_side.astype(jnp.float32), precision=lax.Precision.HIGHEST)
    normout = norm_rows(mixture, out_gain[index], out_shift[index]).astype(jnp.bfloat16)
    update = gating * (jnp.dot(normout, w_out[index], preferred_element_type=jnp.float32) + bias_out[index])
    return (pair.astype(jnp.float32) + update).astype(jnp.bfloat16)

def reference(pair, token_mask, in_gain, in_shift, w_in, bias_in, out_gain, out_shift, w_out, bias_out):
    present = token_mask.astype(jnp.float32)
    grid = present[:, None] * present[None, :]
    first = triangle(pair, grid, 0, in_gain, in_shift, w_in, bias_in, out_gain, out_shift, w_out, bias_out, False)
    return triangle(first, grid, 1, in_gain, in_shift, w_in, bias_in, out_gain, out_shift, w_out, bias_out, True)
```

```python
import jax
import jax.numpy as jnp
from jax import lax
from jax.sharding import PartitionSpec as P


def norm_rows(values, gain, shift):
    center = values - jnp.mean(values, axis=-1, keepdims=True)
    spread = jnp.mean(center * center, axis=-1, keepdims=True)
    return center * lax.rsqrt(spread + 1e-05) * gain + shift


def update(pair, grid, in_gain, in_shift, w_in, bias_in, out_gain, out_shift, w_out, bias_out, shape, incoming):
    rows, cols, _ = pair.shape
    peers_r, peers_c = shape
    peers = peers_r * peers_c
    hidden = w_out.shape[0]
    normed = norm_rows(pair.astype(jnp.float32), in_gain, in_shift).astype(jnp.bfloat16)
    product = jnp.dot(normed, w_in, preferred_element_type=jnp.float32) + bias_in
    values = product[..., : 4 * hidden].reshape(rows, cols, 2, 2, hidden)
    sides = (jax.nn.sigmoid(values[..., 1, :]) * values[..., 0, :] * grid[..., None, None]).astype(jnp.bfloat16)
    gating = jax.nn.sigmoid(product[..., 4 * hidden :])
    if hidden % peers == 0:
        part = hidden // peers
        sides = sides.reshape(rows * cols, 2, peers, part).transpose(2, 1, 3, 0).reshape(peers, 2 * part, rows * cols)
        sides = lax.all_to_all(sides, ("row", "col"), 0, 0, tiled=True)
        sides = sides.reshape(peers_r, peers_c, 2, part, rows, cols).transpose(2, 3, 0, 4, 1, 5)
        sides = sides.reshape(2, part, peers_r * rows, peers_c * cols)
        form = "hki,hkj->hij" if incoming else "hik,hjk->hij"
        mixed = jnp.einsum(form, sides[0], sides[1], preferred_element_type=jnp.float32).astype(jnp.bfloat16)
        mixed = mixed.reshape(part, peers_r, rows, peers_c, cols).transpose(1, 3, 0, 2, 4).reshape(peers, part, rows * cols)
        mixed = lax.all_to_all(mixed, ("row", "col"), 0, 0, tiled=True)
    else:
        part = hidden // peers_c
        sides = sides.reshape(rows, cols, 2, peers_c, part).transpose(3, 2, 4, 0, 1)
        sides = lax.all_to_all(sides, "col", 0, 0).transpose(1, 2, 3, 0, 4).reshape(2, part, rows, peers_c * cols)
        panel = lax.all_gather(sides, "row", axis=2, tiled=True)
        here = lax.axis_index("row") * rows
        if incoming:
            own = lax.dynamic_slice_in_dim(panel[0], here, rows, 2)
            mixed = jnp.einsum("hki,hkj->hij", own, panel[1], preferred_element_type=jnp.float32)
        else:
            mixed = jnp.einsum("hik,hjk->hij", sides[0], panel[1], preferred_element_type=jnp.float32)
        mixed = mixed.astype(jnp.bfloat16).reshape(part, rows, peers_c, cols).transpose(2, 0, 1, 3)
        mixed = lax.all_to_all(mixed, "col", 0, 0)
    mixed = mixed.reshape(hidden, rows * cols).T.reshape(rows, cols, hidden).astype(jnp.float32)
    normout = norm_rows(mixed, out_gain, out_shift).astype(jnp.bfloat16)
    result = gating * (jnp.dot(normout, w_out, preferred_element_type=jnp.float32) + bias_out)
    return (pair.astype(jnp.float32) + result).astype(jnp.bfloat16)


def solution(mesh):
    shape = (mesh.shape["row"], mesh.shape["col"])

    def per_device(pair, token_mask, in_gain, in_shift, w_in, bias_in, out_gain, out_shift, w_out, bias_out):
        rows, cols, _ = pair.shape
        present = token_mask.astype(jnp.float32)
        row_mask = lax.dynamic_slice_in_dim(present, lax.axis_index("row") * rows, rows)
        col_mask = lax.dynamic_slice_in_dim(present, lax.axis_index("col") * cols, cols)
        grid = row_mask[:, None] * col_mask[None, :]
        for index in range(2):
            pair = update(
                pair, grid, in_gain[index], in_shift[index], w_in[index], bias_in[index],
                out_gain[index], out_shift[index], w_out[index], bias_out[index], shape, index == 1,
            )
        return pair

    placed = (P(("groups", "row"), "col", None), P("groups")) + (P(),) * 8
    return jax.shard_map(
        per_device, mesh=mesh, in_specs=placed, out_specs=P(("groups", "row"), "col", None), check_vma=False
    )
```

```python
import jax
import jax.numpy as jnp
from jax import lax
from jax.sharding import PartitionSpec as P


def norm_rows(values, gain, shift):
    center = values - jnp.mean(values, axis=-1, keepdims=True)
    spread = jnp.mean(center * center, axis=-1, keepdims=True)
    return center * lax.rsqrt(spread + 1e-05) * gain + shift


def project(pair, grid, in_gain, in_shift, w_in, bias_in, hidden):
    normed = norm_rows(pair.astype(jnp.float32), in_gain, in_shift).astype(jnp.bfloat16)
    product = jnp.dot(normed, w_in, preferred_element_type=jnp.float32) + bias_in
    gates = jax.nn.sigmoid(product[..., hidden : 2 * hidden]), jax.nn.sigmoid(product[..., 3 * hidden : 4 * hidden])
    left = (gates[0] * product[..., :hidden] * grid[..., None]).astype(jnp.bfloat16)
    right = (gates[1] * product[..., 2 * hidden : 3 * hidden] * grid[..., None]).astype(jnp.bfloat16)
    return left, right, jax.nn.sigmoid(product[..., 4 * hidden :])


def finish(pair, mixed, gating, out_gain, out_shift, w_out, bias_out):
    normout = norm_rows(mixed, out_gain, out_shift).astype(jnp.bfloat16)
    result = gating * (jnp.dot(normout, w_out, preferred_element_type=jnp.float32) + bias_out)
    return (pair.astype(jnp.float32) + result).astype(jnp.bfloat16)


def solution(mesh):
    n = mesh.shape["col"]

    def along(block, axis, step):
        return lax.ppermute(block, axis, [(k, (k + step) % n) for k in range(n)]) if step else block

    def across(block, step):
        pairs = [(a * n + z, z * n + (a + step) % n) for a in range(n) for z in range(n)]
        return lax.ppermute(block, ("row", "col"), pairs)

    def matched(blocks):
        start = lax.rem(lax.axis_index("row") - lax.axis_index("col") + n, n)
        return lax.dynamic_slice_in_dim(jnp.concatenate([jnp.stack(blocks)] * 2), start, n)

    def per_device(pair, token_mask, in_gain, in_shift, w_in, bias_in, out_gain, out_shift, w_out, bias_out):
        rows, cols, _ = pair.shape
        hidden = w_out.shape[1]
        present = token_mask.astype(jnp.float32)
        row_mask = lax.dynamic_slice_in_dim(present, lax.axis_index("row") * rows, rows)
        col_mask = lax.dynamic_slice_in_dim(present, lax.axis_index("col") * cols, cols)
        grid = row_mask[:, None] * col_mask[None, :]
        left, right, gating = project(pair, grid, in_gain[0], in_shift[0], w_in[0], bias_in[0], hidden)
        mirrored = across(right, 0)
        lefts = jnp.stack([along(left, "col", step) for step in range(n)])
        rights = matched([along(mirrored, "row", step) for step in range(n)])
        mixed = jnp.einsum("sikh,sjkh->ijh", lefts, rights, preferred_element_type=jnp.float32)
        pair = finish(pair, mixed, gating, out_gain[0], out_shift[0], w_out[0], bias_out[0])
        left, right, gating = project(pair, grid, in_gain[1], in_shift[1], w_in[1], bias_in[1], hidden)
        lefts = jnp.stack([across(left, step) for step in range(n)])
        rights = matched([along(right, "row", step) for step in range(n)])
        mixed = jnp.einsum("skih,skjh->ijh", lefts, rights, preferred_element_type=jnp.float32)
        return finish(pair, mixed, gating, out_gain[1], out_shift[1], w_out[1], bias_out[1])

    placed = (P(("groups", "row"), "col", None), P("groups")) + (P(),) * 8
    return jax.shard_map(
        per_device, mesh=mesh, in_specs=placed, out_specs=P(("groups", "row"), "col", None), check_vma=False
    )
```

```python
import functools

import jax
import jax.numpy as jnp
from jax import lax
from jax.experimental import pallas as pl
from jax.experimental.pallas import tpu as pltpu
from jax.sharding import PartitionSpec as P

F32, BF16 = jnp.float32, jnp.bfloat16


def dot(a, b):
    return jnp.dot(a, b, preferred_element_type=F32)


def split(values):
    high = values.astype(BF16)
    return jnp.concatenate([high, (values - high.astype(F32)).astype(BF16)], axis=1)


def constants(width):
    rows = lax.broadcasted_iota(jnp.int32, (2 * width, width), 0)
    cols = lax.broadcasted_iota(jnp.int32, (2 * width, width), 1)
    mean = jnp.full((2 * width, width), 1.0 / width, F32)
    center = jnp.where((rows == cols) | (rows == cols + width), 1.0, 0.0) - mean
    return center.astype(BF16), mean.astype(BF16)


def scaled(center, mean, gain, shift):
    spread = dot(split(center * center), mean)
    return (center * lax.rsqrt(spread + 1e-05) * gain + shift).astype(BF16)


def norm_pair(values, consts, gain, shift):
    return scaled(dot(values, consts[0][: values.shape[1]]), consts[1], gain, shift)


def norm_mixed(values, consts, gain, shift):
    return scaled(dot(split(values), consts[0]), consts[1], gain, shift)


def gated(normed, weights, bias, width):
    product = dot(normed, weights) + bias
    return (jnp.tanh(product[:, width:]) + 1.0) * product[:, :width]


def gate(normed, weights, bias):
    return 0.5 * jnp.tanh(dot(normed, weights) + bias) + 0.5


def masked(values, outer, inner):
    t = outer.shape[0]
    grid = jnp.concatenate([outer[k : k + 1] * inner for k in range(t)], axis=0)
    return (values * grid).astype(BF16)


def mix(out_ref, left_ref, right_ref, slots, left_at, right_at, t):
    width = out_ref.shape[1]
    for base in range(0, t, 8):

        def slot(s, total):
            ls, rs = left_at(s), right_at(s)

            def step(q, total):
                for u in range(4):
                    first = pl.multiple_of((q * 4 + u) * t, 8)
                    right = right_ref[rs, pl.ds(first, t), :]
                    total = tuple(
                        total[i] + left_ref[ls, pl.ds(first + base + i, 1), :] * right for i in range(8)
                    )
                return total

            return lax.fori_loop(0, t // 4, step, total)

        total = lax.fori_loop(0, slots, slot, (jnp.zeros((t, width), F32),) * 8)
        for i in range(8):
            out_ref[pl.ds((base + i) * t, t), :] = total[i]


def finish(pair, mixed, gating, consts, gain, shift, weights, bias):
    normout = norm_mixed(mixed, consts, gain, shift)
    return (pair.astype(F32) + gating * (dot(normout, weights) + bias)).astype(BF16)


def first_kernel(n, t, *refs):
    row_refs, col_refs = refs[:n], refs[n : 2 * n]
    mask, in_gain, in_shift, w_in, bias_in, out_gain, out_shift, w_out, bias_out = refs[2 * n : 2 * n + 9]
    pair_ref, left_ref, right_ref, held, wide, lefts, rights, mixed = refs[2 * n + 9 :]
    width = pair_ref.shape[1]
    r, c = lax.axis_index("row"), lax.axis_index("col")
    half = n // 2
    consts = constants(width)
    weights = [w_in[u] * 0.5 for u in range(2)]
    biases = [bias_in[u : u + 1] * 0.5 for u in range(2)]
    for m, ref in enumerate(row_refs + col_refs):
        held[m] = ref[...]

    def prepare(m, _):
        along_row = m < n
        s = jnp.where(along_row, m, m - n)
        turned = lax.rem(r - s + n, n)
        outer = jnp.where(along_row, lax.rem(c - s + n, n), lax.rem(turned, half) * 2 + turned // half)
        inner = jnp.where(along_row, r, c)
        outer = mask[pl.ds(pl.multiple_of(outer * t, 8), t), :]
        inner = mask[pl.ds(pl.multiple_of(inner * t, 8), t), :]
        wide[...] = held[m].astype(F32)
        values = jnp.concatenate([wide[pl.ds(k, t, stride=t), :] for k in range(t)], axis=0).astype(BF16)
        normed = norm_pair(values, consts, in_gain[0:1], in_shift[0:1])
        for k, target in enumerate((lefts, rights)):
            span = slice(2 * k * width, 2 * (k + 1) * width)
            side = gated(normed, weights[0][:, span], biases[0][:, span], width)
            target[m] = masked(side, outer, inner).astype(F32)
        return 0

    lax.fori_loop(0, 2 * n, prepare, 0)

    def place(b):
        return b // 2 + lax.rem(b, 2) * half

    def col_slot(s):
        return n + lax.rem(r - place(lax.rem(c - s + n, n)) + n, n)

    mix(mixed.at[0], lefts, rights, n, lambda s: s, col_slot, t)
    mix(mixed.at[1], lefts, rights, n, col_slot, lambda s: s, t)
    here = mask[pl.ds(pl.multiple_of(r * t, 8), t), :]
    there = mask[pl.ds(pl.multiple_of(c * t, 8), t), :]
    own = (0, n + lax.rem(r - place(r) + n, n))
    for k in range(2):
        pair = held[own[k]]
        normed = norm_pair(pair, consts, in_gain[0:1], in_shift[0:1])
        gating = gate(normed, weights[0][:, 4 * width :], biases[0][:, 4 * width :])
        updated = finish(
            pair, mixed[k], gating, consts, out_gain[0:1], out_shift[0:1], w_out[0], bias_out[0:1]
        )
        normed = norm_pair(updated, consts, in_gain[1:2], in_shift[1:2])
        if k == 0:
            pair_ref[...] = updated
            span = slice(2 * width, 4 * width)
            side = gated(normed, weights[1][:, span], biases[1][:, span], width)
            right_ref[...] = masked(side, here, there)
        else:
            side = gated(normed, weights[1][:, : 2 * width], biases[1][:, : 2 * width], width)
            left_ref[...] = masked(side, there, here)


def second_kernel(n, t, *refs):
    left_refs, right_refs = refs[:n], refs[n : 2 * n]
    pair, in_gain, in_shift, w_in, bias_in, out_gain, out_shift, w_out, bias_out = refs[2 * n : 2 * n + 9]
    out_ref, lefts, rights, mixed = refs[2 * n + 9 :]
    width = out_ref.shape[1]
    r, c = lax.axis_index("row"), lax.axis_index("col")
    consts = constants(width)
    for s in range(n):
        lefts[s] = left_refs[s][...].astype(F32)
        rights[s] = right_refs[s][...].astype(F32)
    mix(mixed, lefts, rights, n, lambda s: s, lambda s: lax.rem(r - c + s + n, n), t)
    normed = norm_pair(pair[...], consts, in_gain[1:2], in_shift[1:2])
    gating = gate(normed, w_in[1, :, 4 * width :] * 0.5, bias_in[1:2, 4 * width :] * 0.5)
    out_ref[...] = finish(
        pair[...], mixed[...], gating, consts, out_gain[1:2], out_shift[1:2], w_out[1], bias_out[1:2]
    )


def solution(mesh):
    n = mesh.shape["col"]
    half = n // 2

    def along(block, axis, step):
        return lax.ppermute(block, axis, [(k, (k + step) % n) for k in range(n)]) if step else block

    def mirrored(block):
        pairs = [(a * n + z, (z // 2 + z % 2 * half) * n + a) for a in range(n) for z in range(n)]
        return lax.ppermute(block, ("row", "col"), pairs)

    def per_device(pair, token_mask, in_gain, in_shift, w_in, bias_in, out_gain, out_shift, w_out, bias_out):
        t, _, width = pair.shape
        area = (t * t, width)
        block = jax.ShapeDtypeStruct(area, BF16)
        params = pltpu.CompilerParams(vmem_limit_bytes=48 * 1024 * 1024)
        mask = jnp.broadcast_to(token_mask.astype(F32)[:, None], (n * t, width))
        tensors = (in_gain, in_shift, w_in, bias_in, out_gain, out_shift, w_out, bias_out)
        pair = pair.reshape(area)
        col_block = mirrored(pair)
        rows = [along(pair, "col", step) for step in range(n)]
        cols = [along(col_block, "row", step) for step in range(n)]
        pair, left, right = pl.pallas_call(
            functools.partial(first_kernel, n, t),
            out_shape=(block,) * 3,
            scratch_shapes=[
                pltpu.VMEM((2 * n,) + area, BF16),
                pltpu.VMEM(area, F32),
                pltpu.VMEM((2 * n,) + area, F32),
                pltpu.VMEM((2 * n,) + area, F32),
                pltpu.VMEM((2,) + area, F32),
            ],
            compiler_params=params,
            name="first_update",
        )(*rows, *cols, mask, *tensors)
        lefts = [along(left, "col", step) for step in range(n)]
        rights = [along(right, "row", step) for step in range(n)]
        out = pl.pallas_call(
            functools.partial(second_kernel, n, t),
            out_shape=block,
            scratch_shapes=[
                pltpu.VMEM((n,) + area, F32),
                pltpu.VMEM((n,) + area, F32),
                pltpu.VMEM(area, F32),
            ],
            compiler_params=params,
            name="second_update",
        )(*lefts, *rights, pair, *tensors)
        return out.reshape(t, t, width)

    placed = (P(("groups", "row"), "col", None), P("groups")) + (P(),) * 8
    return jax.shard_map(
        per_device, mesh=mesh, in_specs=placed, out_specs=P(("groups", "row"), "col", None), check_vma=False
    )
```

```python
import functools

import jax
import jax.numpy as jnp
from jax import lax
from jax.experimental import pallas as pl
from jax.experimental.pallas import tpu as pltpu
from jax.sharding import PartitionSpec as P

F32, BF16 = jnp.float32, jnp.bfloat16


def dot(a, b):
    return jnp.dot(a, b, preferred_element_type=F32)


def split(values):
    high = values.astype(BF16)
    return jnp.concatenate([high, (values - high.astype(F32)).astype(BF16)], axis=1)


def constants(width):
    rows = lax.broadcasted_iota(jnp.int32, (2 * width, width), 0)
    cols = lax.broadcasted_iota(jnp.int32, (2 * width, width), 1)
    mean = jnp.full((2 * width, width), 1.0 / width, F32)
    center = jnp.where((rows == cols) | (rows == cols + width), 1.0, 0.0) - mean
    return center.astype(BF16), mean.astype(BF16)


def scaled(center, mean, gain, shift):
    spread = dot(split(center * center), mean)
    return (center * lax.rsqrt(spread + 1e-05) * gain + shift).astype(BF16)


def norm_pair(values, consts, gain, shift):
    return scaled(dot(values, consts[0][: values.shape[1]]), consts[1], gain, shift)


def norm_mixed(values, consts, gain, shift):
    return scaled(dot(split(values), consts[0]), consts[1], gain, shift)


def gated(normed, weights, bias, width):
    product = dot(normed, weights) + bias
    return (jnp.tanh(product[:, width:]) + 1.0) * product[:, :width]


def gate(normed, weights, bias):
    return 0.5 * jnp.tanh(dot(normed, weights) + bias) + 0.5


def masked(values, outer, inner):
    t = outer.shape[0]
    grid = jnp.concatenate([outer[k : k + 1] * inner for k in range(t)], axis=0)
    return (values * grid).astype(BF16)


def mix(out_ref, old_ref, left, right, t):
    width = out_ref.shape[1]
    for base in range(0, t, 8):
        if old_ref is None:
            total = (jnp.zeros((t, width), F32),) * 8
        else:
            total = tuple(old_ref[pl.ds((base + i) * t, t), :] for i in range(8))

        def step(q, total):
            for u in range(4):
                first = pl.multiple_of((q * 4 + u) * t, 8)
                row = right(first)
                total = tuple(total[i] + left(first + base + i) * row for i in range(8))
            return total

        total = lax.fori_loop(0, t // 4, step, total)
        for i in range(8):
            out_ref[pl.ds((base + i) * t, t), :] = total[i]


def finish(pair, mixed, gating, consts, gain, shift, weights, bias):
    normout = norm_mixed(mixed, consts, gain, shift)
    return (pair.astype(F32) + gating * (dot(normout, weights) + bias)).astype(BF16)


def row_of(ref, *lead):
    return lambda at: ref[(*lead, pl.ds(at, 1), slice(None))]


def rows_of(ref, t, *lead):
    return lambda at: ref[(*lead, pl.ds(at, t), slice(None))]


def place(b, n):
    return b // 2 + lax.rem(b, 2) * (n // 2)


def mask_of(mask, b, t):
    return mask[pl.ds(pl.multiple_of(b * t, 8), t), :]


def sides(values_ref, wide, left_at, right_at, outer, inner, consts, in_gain, in_shift, weights, bias):
    t, width = outer.shape
    wide[...] = values_ref[...].astype(F32)
    values = jnp.concatenate([wide[pl.ds(k, t, stride=t), :] for k in range(t)], axis=0).astype(BF16)
    normed = norm_pair(values, consts, in_gain[0:1], in_shift[0:1])
    for k, target in enumerate((left_at, right_at)):
        span = slice(2 * k * width, 2 * (k + 1) * width)
        side = gated(normed, weights[:, span], bias[:, span], width)
        target[...] = masked(side, outer, inner).astype(F32)


def own_kernel(n, t, pair, mask, in_gain, in_shift, w_in, bias_in, left, right, gating, wide):
    width = pair.shape[1]
    r, c = lax.axis_index("row"), lax.axis_index("col")
    consts = constants(width)
    weights, bias = w_in[0] * 0.5, bias_in[0:1] * 0.5
    outer, inner = mask_of(mask, c, t), mask_of(mask, r, t)
    sides(pair, wide, left, right, outer, inner, consts, in_gain, in_shift, weights, bias)
    normed = norm_pair(pair[...], consts, in_gain[0:1], in_shift[0:1])
    gating[...] = gate(normed, weights[:, 4 * width :], bias[:, 4 * width :])


def column_kernel(n, t, *refs):
    blocks = refs[:n]
    mask, in_gain, in_shift, w_in, bias_in, own_left, own_right = refs[n : n + 7]
    lefts, rights, pair, gating, mixed, held, wide = refs[n + 7 :]
    width = wide.shape[1]
    r, c = lax.axis_index("row"), lax.axis_index("col")
    consts = constants(width)
    weights, bias = w_in[0] * 0.5, bias_in[0:1] * 0.5
    for s in range(n):
        held[s] = blocks[s][...]

    def prepare(b, _):
        s = r ^ place(b, n)
        outer, inner = mask_of(mask, b, t), mask_of(mask, c, t)
        sides(
            held.at[s], wide, lefts.at[b], rights.at[b], outer, inner, consts, in_gain, in_shift, weights, bias
        )
        return 0

    lax.fori_loop(0, n, prepare, 0)
    own = held[r ^ place(r, n)]
    pair[...] = own
    normed = norm_pair(own, consts, in_gain[0:1], in_shift[0:1])
    gating[...] = gate(normed, weights[:, 4 * width :], bias[:, 4 * width :])
    mix(mixed.at[0], None, row_of(own_left), rows_of(rights, t, c), t)
    mix(mixed.at[1], None, row_of(lefts, c), rows_of(own_right, t), t)


def slot_sum(n, t, slot, block, mask, in_gain, in_shift, w_in, bias_in, lefts, rights, old, mixed, wide, left, right):
    r, c = lax.axis_index("row"), lax.axis_index("col")
    consts = constants(wide.shape[1])
    weights, bias = w_in[0] * 0.5, bias_in[0:1] * 0.5
    b = c ^ slot
    outer, inner = mask_of(mask, b, t), mask_of(mask, r, t)
    sides(block, wide, left, right, outer, inner, consts, in_gain, in_shift, weights, bias)
    mix(mixed.at[0], old.at[0], row_of(left), rows_of(rights, t, b), t)
    mix(mixed.at[1], old.at[1], row_of(lefts, b), rows_of(right, t), t)


def slot_kernel(n, t, slot, *refs):
    slot_sum(n, t, slot, *refs)


def last_kernel(n, t, slot, *refs):
    block, mask, in_gain, in_shift, w_in, bias_in, lefts, rights, old = refs[:9]
    out_gain, out_shift, w_out, bias_out, pair, gating, col_pair, col_gating = refs[9:17]
    pair_ref, left_ref, right_ref, mixed, wide, left, right = refs[17:]
    slot_sum(
        n, t, slot, block, mask, in_gain, in_shift, w_in, bias_in, lefts, rights, old, mixed, wide, left, right
    )
    width = wide.shape[1]
    r, c = lax.axis_index("row"), lax.axis_index("col")
    consts = constants(width)
    weights, bias = w_in[1] * 0.5, bias_in[1:2] * 0.5
    here, there = mask_of(mask, r, t), mask_of(mask, c, t)
    for k, (base, factor) in enumerate(((pair, gating), (col_pair, col_gating))):
        updated = finish(
            base[...], mixed[k], factor[...], consts, out_gain[0:1], out_shift[0:1], w_out[0], bias_out[0:1]
        )
        normed = norm_pair(updated, consts, in_gain[1:2], in_shift[1:2])
        if k == 0:
            pair_ref[...] = updated
            span = slice(2 * width, 4 * width)
            right_ref[...] = masked(gated(normed, weights[:, span], bias[:, span], width), here, there)
        else:
            span = slice(0, 2 * width)
            left_ref[...] = masked(gated(normed, weights[:, span], bias[:, span], width), there, here)


def gate_kernel(pair, in_gain, in_shift, w_in, bias_in, gating):
    width = pair.shape[1]
    normed = norm_pair(pair[...], constants(width), in_gain[1:2], in_shift[1:2])
    gating[...] = gate(normed, w_in[1, :, 4 * width :] * 0.5, bias_in[1:2, 4 * width :] * 0.5)


def right_kernel(n, t, *refs):
    blocks, left = refs[:n], refs[n]
    rights, mixed, wide = refs[n + 1 :]
    r, c = lax.axis_index("row"), lax.axis_index("col")
    for s in range(n):
        rights[s] = blocks[s][...].astype(F32)
    wide[...] = left[...].astype(F32)
    mix(mixed, None, row_of(wide), rows_of(rights, t, r ^ c), t)


def left_sum(n, t, slot, left, rights, old, mixed, wide):
    r, c = lax.axis_index("row"), lax.axis_index("col")
    wide[...] = left[...].astype(F32)
    mix(mixed, old, row_of(wide), rows_of(rights, t, r ^ c ^ slot), t)


def left_kernel(n, t, slot, *refs):
    left_sum(n, t, slot, *refs)


def end_kernel(n, t, slot, left, rights, old, pair, gating, out_gain, out_shift, w_out, bias_out, out, mixed, wide):
    left_sum(n, t, slot, left, rights, old, mixed, wide)
    consts = constants(wide.shape[1])
    out[...] = finish(
        pair[...], mixed[...], gating[...], consts, out_gain[1:2], out_shift[1:2], w_out[1], bias_out[1:2]
    )


def solution(mesh):
    n = mesh.shape["col"]
    half = n // 2

    def along(block, axis, step):
        return lax.ppermute(block, axis, [(k, k ^ step) for k in range(n)])

    def mirrored(block):
        pairs = [(a * n + z, (z // 2 + z % 2 * half) * n + a) for a in range(n) for z in range(n)]
        return lax.ppermute(block, ("row", "col"), pairs)

    def plane(block):
        return [block] + [along(block, "row", step) for step in range(1, n)]

    def per_device(pair, token_mask, in_gain, in_shift, w_in, bias_in, out_gain, out_shift, w_out, bias_out):
        t, _, width = pair.shape
        area = (t * t, width)
        narrow, broad = jax.ShapeDtypeStruct(area, BF16), jax.ShapeDtypeStruct(area, F32)
        stacked = jax.ShapeDtypeStruct((n,) + area, F32)
        twice = jax.ShapeDtypeStruct((2,) + area, F32)
        scratch = pltpu.VMEM(area, F32)

        def call(kernel, name, outs, scratches, ops, *operands, alias=None):
            return pl.pallas_call(
                kernel,
                out_shape=outs,
                scratch_shapes=scratches,
                input_output_aliases=alias or {},

                compiler_params=pltpu.CompilerParams(vmem_limit_bytes=(16 + n) * 1024 * 1024),
                name=name,
            )(*operands)

        work = 2 * t**4 * width
        mask = jnp.broadcast_to(token_mask.astype(F32)[:, None], (n * t, width))
        ins = (mask, in_gain, in_shift, w_in, bias_in)
        outs = (out_gain, out_shift, w_out, bias_out)
        pair = pair.reshape(area)
        col_block = mirrored(pair)
        steps = [step for step in range(1, n) if step != half] + [half]
        rows = [along(pair, "col", step) for step in steps]
        own_left, own_right, gating = call(
            functools.partial(own_kernel, n, t), "own_sides", (broad,) * 3, [scratch], work, pair, *ins
        )
        lefts, rights, col_pair, col_gating, mixed = call(
            functools.partial(column_kernel, n, t),
            "column_sides",
            (stacked, stacked, narrow, broad, twice),
            [pltpu.VMEM((n,) + area, BF16), scratch],
            n * work,
            *plane(col_block),
            *ins,
            own_left,
            own_right,
        )
        for step, block in zip(steps[:-1], rows[:-1]):
            mixed = call(
                functools.partial(slot_kernel, n, t, step),
                "row_slot",
                twice,
                [scratch] * 3,
                work,
                block,
                *ins,
                lefts,
                rights,
                mixed,
                alias={8: 0},
            )
        pair, left, right = call(
            functools.partial(last_kernel, n, t, steps[-1]),
            "last_slot",
            (narrow,) * 3,
            [pltpu.VMEM((2,) + area, F32)] + [scratch] * 3,
            work,
            rows[-1],
            *ins,
            lefts,
            rights,
            mixed,
            *outs,
            pair,
            gating,
            col_pair,
            col_gating,
        )
        blocks = [along(left, "col", step) for step in steps]
        gating = call(gate_kernel, "gate", broad, [], work, pair, *ins[1:])
        rights, mixed = call(
            functools.partial(right_kernel, n, t), "right_slots", (stacked, broad), [scratch], work, *plane(right), left
        )
        for step, block in zip(steps[:-1], blocks[:-1]):
            mixed = call(
                functools.partial(left_kernel, n, t, step),
                "left_slot",
                broad,
                [scratch],
                work,
                block,
                rights,
                mixed,
                alias={2: 0},
            )
        out = call(
            functools.partial(end_kernel, n, t, steps[-1]),
            "end",
            narrow,
            [scratch] * 2,
            work,
            blocks[-1],
            rights,
            mixed,
            pair,
            gating,
            *outs,
        )
        return out.reshape(t, t, width)

    placed = (P(("groups", "row"), "col", None), P("groups")) + (P(),) * 8
    return jax.shard_map(
        per_device, mesh=mesh, in_specs=placed, out_specs=P(("groups", "row"), "col", None), check_vma=False
    )
```

```python
import functools

import jax
import jax.numpy as jnp
from jax import lax
from jax.experimental import pallas as pl
from jax.experimental.pallas import tpu as pltpu
from jax.sharding import PartitionSpec as P

F32, BF16 = jnp.float32, jnp.bfloat16


def dot(a, b):
    return jnp.dot(a, b, preferred_element_type=F32)


def split(values):
    high = values.astype(BF16)
    return jnp.concatenate([high, (values - high.astype(F32)).astype(BF16)], axis=1)


def constants(width):
    rows = lax.broadcasted_iota(jnp.int32, (2 * width, width), 0)
    cols = lax.broadcasted_iota(jnp.int32, (2 * width, width), 1)
    mean = jnp.full((2 * width, width), 1.0 / width, F32)
    center = jnp.where((rows == cols) | (rows == cols + width), 1.0, 0.0) - mean
    return center.astype(BF16), mean.astype(BF16)


def scaled(center, mean, gain, shift):
    spread = dot(split(center * center), mean)
    return (center * lax.rsqrt(spread + 1e-05) * gain + shift).astype(BF16)


def norm_pair(values, consts, gain, shift):
    return scaled(dot(values, consts[0][: values.shape[1]]), consts[1], gain, shift)


def norm_mixed(values, consts, gain, shift):
    return scaled(dot(split(values), consts[0]), consts[1], gain, shift)


def gated(normed, weights, bias, width):
    product = dot(normed, weights) + bias
    return (jnp.tanh(product[:, width:]) + 1.0) * product[:, :width]


def gate(normed, weights, bias):
    return 0.5 * jnp.tanh(dot(normed, weights) + bias) + 0.5


def masked(values, outer, inner):
    t = outer.shape[0]
    grid = jnp.concatenate([outer[k : k + 1] * inner for k in range(t)], axis=0)
    return (values * grid).astype(BF16)


def mix(out_ref, old_ref, left, right, t):
    width = out_ref.shape[1]
    for base in range(0, t, 8):
        if old_ref is None:
            total = (jnp.zeros((t, width), F32),) * 8
        else:
            total = tuple(old_ref[pl.ds((base + i) * t, t), :] for i in range(8))

        def step(q, total):
            for u in range(4):
                first = pl.multiple_of((q * 4 + u) * t, 8)
                row = right(first)
                total = tuple(total[i] + left(first + base + i) * row for i in range(8))
            return total

        total = lax.fori_loop(0, t // 4, step, total)
        for i in range(8):
            out_ref[pl.ds((base + i) * t, t), :] = total[i]


def finish(pair, mixed, gating, consts, gain, shift, weights, bias):
    normout = norm_mixed(mixed, consts, gain, shift)
    return (pair.astype(F32) + gating * (dot(normout, weights) + bias)).astype(BF16)


def row_of(ref, *lead):
    return lambda at: ref[(*lead, pl.ds(at, 1), slice(None))]


def rows_of(ref, t, *lead):
    return lambda at: ref[(*lead, pl.ds(at, t), slice(None))]


def place(b, n):
    return b // 2 + lax.rem(b, 2) * (n // 2)


def mask_of(mask, b, t):
    return mask[pl.ds(pl.multiple_of(b * t, 8), t), :]


def sides(values_ref, wide, left_at, right_at, outer, inner, consts, in_gain, in_shift, weights, bias):
    t, width = outer.shape
    wide[...] = values_ref[...].astype(F32)
    values = jnp.concatenate([wide[pl.ds(k, t, stride=t), :] for k in range(t)], axis=0).astype(BF16)
    normed = norm_pair(values, consts, in_gain[0:1], in_shift[0:1])
    for k, target in enumerate((left_at, right_at)):
        span = slice(2 * k * width, 2 * (k + 1) * width)
        side = gated(normed, weights[:, span], bias[:, span], width)
        target[...] = masked(side, outer, inner).astype(F32)


def own_kernel(n, t, count, *refs):
    sources, copies = refs[:count], refs[count : 2 * count - 3]
    weights, bias, mask, left, right, gating = refs[2 * count - 3 : 2 * count + 3]
    tokens, raw_weights, raw_bias, wide, arrived = refs[2 * count + 3 :]
    pair, in_gain, in_shift = copies[:3]
    width = pair.shape[1]
    targets = (tokens, raw_weights, raw_bias, *copies)
    moves = [pltpu.make_async_copy(s, d, arrived.at[k]) for k, (s, d) in enumerate(zip(sources, targets))]
    for move in moves:
        move.start()
    for move in moves:
        move.wait()
    r, c = lax.axis_index("row"), lax.axis_index("col")
    rows = lax.broadcasted_iota(jnp.int32, (n * t, n * t), 0)
    cols = lax.broadcasted_iota(jnp.int32, (n * t, n * t), 1)
    spread = jnp.where(rows == cols, tokens[...].astype(F32), 0.0).astype(BF16)
    mask[...] = dot(spread, jnp.ones((n * t, width), BF16))
    weights[...] = raw_weights[...] * 0.5
    bias[...] = raw_bias[...] * 0.5
    consts = constants(width)
    outer, inner = mask_of(mask, c, t), mask_of(mask, r, t)
    sides(pair, wide, left, right, outer, inner, consts, in_gain, in_shift, weights[0], bias[0:1])
    normed = norm_pair(pair[...], consts, in_gain[0:1], in_shift[0:1])
    gating[...] = gate(normed, weights[0, :, 4 * width :], bias[0:1, 4 * width :])


def column_kernel(n, t, steps, *refs):
    blocks, rows = refs[:n], refs[n : 2 * n - 2]
    mask, in_gain, in_shift, w_in, bias_in, own_left, own_right = refs[2 * n - 2 : 2 * n + 5]
    lefts, rights, pair, gating, mixed, held, wide, left, right = refs[2 * n + 5 :]
    width = wide.shape[1]
    r, c = lax.axis_index("row"), lax.axis_index("col")
    consts = constants(width)
    weights, bias = w_in[0], bias_in[0:1]
    for s in range(n):
        held[s] = blocks[s][...]

    def prepare(b, _):
        s = r ^ place(b, n)
        outer, inner = mask_of(mask, b, t), mask_of(mask, c, t)
        sides(
            held.at[s], wide, lefts.at[b], rights.at[b], outer, inner, consts, in_gain, in_shift, weights, bias
        )
        return 0

    lax.fori_loop(0, n, prepare, 0)
    own = held[r ^ place(r, n)]
    pair[...] = own
    normed = norm_pair(own, consts, in_gain[0:1], in_shift[0:1])
    gating[...] = gate(normed, weights[:, 4 * width :], bias[:, 4 * width :])
    mix(mixed.at[0], None, row_of(own_left), rows_of(rights, t, c), t)
    mix(mixed.at[1], None, row_of(lefts, c), rows_of(own_right, t), t)
    for step, block in zip(steps, rows):
        slot_sum(
            n, t, step, block, mask, in_gain, in_shift, w_in, bias_in, lefts, rights, mixed, mixed, wide, left, right
        )


def slot_sum(n, t, slot, block, mask, in_gain, in_shift, w_in, bias_in, lefts, rights, old, mixed, wide, left, right):
    r, c = lax.axis_index("row"), lax.axis_index("col")
    consts = constants(wide.shape[1])
    weights, bias = w_in[0], bias_in[0:1]
    b = c ^ slot
    outer, inner = mask_of(mask, b, t), mask_of(mask, r, t)
    sides(block, wide, left, right, outer, inner, consts, in_gain, in_shift, weights, bias)
    mix(mixed.at[0], old.at[0], row_of(left), rows_of(rights, t, b), t)
    mix(mixed.at[1], old.at[1], row_of(lefts, b), rows_of(right, t), t)


def last_kernel(n, t, slot, *refs):
    block, mask, in_gain, in_shift, w_in, bias_in, lefts, rights, old = refs[:9]
    out_gain, out_shift, w_out, bias_out, pair, gating, col_pair, col_gating = refs[9:17]
    pair_ref, left_ref, right_ref, mixed, wide, left, right = refs[17:]
    slot_sum(
        n, t, slot, block, mask, in_gain, in_shift, w_in, bias_in, lefts, rights, old, mixed, wide, left, right
    )
    width = wide.shape[1]
    r, c = lax.axis_index("row"), lax.axis_index("col")
    consts = constants(width)
    weights, bias = w_in[1], bias_in[1:2]
    here, there = mask_of(mask, r, t), mask_of(mask, c, t)
    for k, (base, factor) in enumerate(((pair, gating), (col_pair, col_gating))):
        updated = finish(
            base[...], mixed[k], factor[...], consts, out_gain[0:1], out_shift[0:1], w_out[0], bias_out[0:1]
        )
        normed = norm_pair(updated, consts, in_gain[1:2], in_shift[1:2])
        if k == 0:
            pair_ref[...] = updated
            span = slice(2 * width, 4 * width)
            right_ref[...] = masked(gated(normed, weights[:, span], bias[:, span], width), here, there)
        else:
            span = slice(0, 2 * width)
            left_ref[...] = masked(gated(normed, weights[:, span], bias[:, span], width), there, here)


def gate_kernel(pair, in_gain, in_shift, w_in, bias_in, gating):
    width = pair.shape[1]
    normed = norm_pair(pair[...], constants(width), in_gain[1:2], in_shift[1:2])
    gating[...] = gate(normed, w_in[1, :, 4 * width :], bias_in[1:2, 4 * width :])


def right_kernel(n, t, *refs):
    blocks, left = refs[:n], refs[n]
    rights, mixed, wide = refs[n + 1 :]
    r, c = lax.axis_index("row"), lax.axis_index("col")
    for s in range(n):
        rights[s] = blocks[s][...].astype(F32)
    wide[...] = left[...].astype(F32)
    mix(mixed, None, row_of(wide), rows_of(rights, t, r ^ c), t)


def left_sum(n, t, slot, left, rights, old, mixed, wide):
    r, c = lax.axis_index("row"), lax.axis_index("col")
    wide[...] = left[...].astype(F32)
    mix(mixed, old, row_of(wide), rows_of(rights, t, r ^ c ^ slot), t)


def left_kernel(n, t, slot, *refs):
    left_sum(n, t, slot, *refs)


def end_kernel(n, t, slot, left, rights, old, pair, gating, out_gain, out_shift, w_out, bias_out, out, mixed, wide):
    left_sum(n, t, slot, left, rights, old, mixed, wide)
    consts = constants(wide.shape[1])
    out[...] = finish(
        pair[...], mixed[...], gating[...], consts, out_gain[1:2], out_shift[1:2], w_out[1], bias_out[1:2]
    )


def solution(mesh):
    n = mesh.shape["col"]
    half = n // 2

    def along(block, axis, step):
        return lax.ppermute(block, axis, [(k, k ^ step) for k in range(n)])

    def mirrored(block):
        pairs = [(a * n + z, (z // 2 + z % 2 * half) * n + a) for a in range(n) for z in range(n)]
        return lax.ppermute(block, ("row", "col"), pairs)

    def plane(block):
        return [block] + [along(block, "row", step) for step in range(1, n)]

    def per_device(pair, token_mask, in_gain, in_shift, w_in, bias_in, out_gain, out_shift, w_out, bias_out):
        t, _, width = pair.shape
        area = (t * t, width)
        narrow, broad = jax.ShapeDtypeStruct(area, BF16), jax.ShapeDtypeStruct(area, F32)
        stacked = jax.ShapeDtypeStruct((n,) + area, F32)
        twice = jax.ShapeDtypeStruct((2,) + area, F32)
        scratch = pltpu.VMEM(area, F32)

        def call(kernel, name, outs, scratches, *operands, alias=None, **specs):
            return pl.pallas_call(
                kernel,
                out_shape=outs,
                **specs,
                scratch_shapes=scratches,
                input_output_aliases=alias or {},

                compiler_params=pltpu.CompilerParams(vmem_limit_bytes=(16 + n) * 1024 * 1024),
                name=name,
            )(*operands)

        pair = pair.reshape(area)
        col_block = mirrored(pair)
        steps = [step for step in range(1, n) if step != half] + [half]
        rows = [along(pair, "col", step) for step in steps]
        tokens = token_mask.reshape(1, n * t)
        raw = (tokens, w_in, bias_in, pair, in_gain, in_shift, out_gain, out_shift, w_out, bias_out)
        like = [jax.ShapeDtypeStruct(array.shape, array.dtype) for array in raw]
        mask = jax.ShapeDtypeStruct((n * t, width), F32)
        pair, in_gain, in_shift, *outs, w_in, bias_in, mask, own_left, own_right, gating = call(
            functools.partial(own_kernel, n, t, len(raw)),
            "own_sides",
            (*like[3:], like[1], like[2], mask, broad, broad, broad),
            [
                *(pltpu.VMEM(array.shape, array.dtype) for array in raw[:3]),
                scratch,
                pltpu.SemaphoreType.DMA((len(raw),)),
            ],
            *raw,
            in_specs=[pl.BlockSpec(memory_space=pltpu.MemorySpace.HBM)] * len(raw),
        )
        ins = (mask, in_gain, in_shift, w_in, bias_in)
        lefts, rights, col_pair, col_gating, mixed = call(
            functools.partial(column_kernel, n, t, steps[:-1]),
            "column_sides",
            (stacked, stacked, narrow, broad, twice),
            [pltpu.VMEM((n,) + area, BF16)] + [scratch] * 3,
            *plane(col_block),
            *rows[:-1],
            *ins,
            own_left,
            own_right,
        )
        pair, left, right = call(
            functools.partial(last_kernel, n, t, steps[-1]),
            "last_slot",
            (narrow,) * 3,
            [pltpu.VMEM((2,) + area, F32)] + [scratch] * 3,
            rows[-1],
            *ins,
            lefts,
            rights,
            mixed,
            *outs,
            pair,
            gating,
            col_pair,
            col_gating,
        )
        blocks = [along(left, "col", step) for step in steps]
        gating = call(gate_kernel, "gate", broad, [], pair, *ins[1:])
        rights, mixed = call(
            functools.partial(right_kernel, n, t), "right_slots", (stacked, broad), [scratch], *plane(right), left
        )
        for step, block in zip(steps[:-1], blocks[:-1]):
            mixed = call(
                functools.partial(left_kernel, n, t, step),
                "left_slot",
                broad,
                [scratch],
                block,
                rights,
                mixed,
                alias={2: 0},
            )
        out = call(
            functools.partial(end_kernel, n, t, steps[-1]),
            "end",
            narrow,
            [scratch] * 2,
            blocks[-1],
            rights,
            mixed,
            pair,
            gating,
            *outs,
        )
        return out.reshape(t, t, width)

    placed = (P(("groups", "row"), "col", None), P("groups")) + (P(),) * 8
    return jax.shard_map(
        per_device, mesh=mesh, in_specs=placed, out_specs=P(("groups", "row"), "col", None), check_vma=False
    )
```

```python
import functools

import jax
import jax.numpy as jnp
from jax import lax
from jax.experimental import pallas as pl
from jax.experimental.pallas import tpu as pltpu
from jax.sharding import PartitionSpec as P

F32, BF16 = jnp.float32, jnp.bfloat16


def dot(a, b):
    return jnp.dot(a, b, preferred_element_type=F32)


def split(values):
    high = values.astype(BF16)
    return jnp.concatenate([high, (values - high.astype(F32)).astype(BF16)], axis=1)


def constants(width):
    rows = lax.broadcasted_iota(jnp.int32, (2 * width, width), 0)
    cols = lax.broadcasted_iota(jnp.int32, (2 * width, width), 1)
    mean = jnp.full((2 * width, width), 1.0 / width, F32)
    center = jnp.where((rows == cols) | (rows == cols + width), 1.0, 0.0) - mean
    return center.astype(BF16), mean.astype(BF16)


def scaled(center, mean, gain, shift):
    spread = dot(split(center * center), mean)
    return (center * lax.rsqrt(spread + 1e-05) * gain + shift).astype(BF16)


def norm_pair(values, consts, gain, shift):
    return scaled(dot(values, consts[0][: values.shape[1]]), consts[1], gain, shift)


def norm_mixed(values, consts, gain, shift):
    return scaled(dot(split(values), consts[0]), consts[1], gain, shift)


def gated(normed, weights, bias, width):
    product = dot(normed, weights) + bias
    return (jnp.tanh(product[:, width:]) + 1.0) * product[:, :width]


def gate(normed, weights, bias):
    return 0.5 * jnp.tanh(dot(normed, weights) + bias) + 0.5


def masked(values, outer, inner):
    t = outer.shape[0]
    grid = jnp.concatenate([outer[k : k + 1] * inner for k in range(t)], axis=0)
    return (values * grid).astype(BF16)


def mix(out_ref, old_ref, left, right, t):
    width = out_ref.shape[1]
    for base in range(0, t, 8):
        if old_ref is None:
            total = (jnp.zeros((t, width), F32),) * 8
        else:
            total = tuple(old_ref[pl.ds((base + i) * t, t), :] for i in range(8))

        def step(q, total):
            for u in range(4):
                first = pl.multiple_of((q * 4 + u) * t, 8)
                row = right(first)
                total = tuple(total[i] + left(first + base + i) * row for i in range(8))
            return total

        total = lax.fori_loop(0, t // 4, step, total)
        for i in range(8):
            out_ref[pl.ds((base + i) * t, t), :] = total[i]


def finish(pair, mixed, gating, consts, gain, shift, weights, bias):
    normout = norm_mixed(mixed, consts, gain, shift)
    return (pair.astype(F32) + gating * (dot(normout, weights) + bias)).astype(BF16)


def row_of(ref, *lead):
    return lambda at: ref[(*lead, pl.ds(at, 1), slice(None))]


def rows_of(ref, t, *lead):
    return lambda at: ref[(*lead, pl.ds(at, t), slice(None))]


def place(b, n):
    return b // 2 + lax.rem(b, 2) * (n // 2)


TABLE_MASK = 24


def in_norm(table, u):
    return table[u : u + 1], table[2 + u : 3 + u]


def out_norm(table, u):
    return table[4 + u : 5 + u], table[6 + u : 7 + u]


def half_bias(table, u, first, last):
    return jnp.concatenate([table[k : k + 1] for k in range(10 + 5 * u + first, 10 + 5 * u + last)], axis=1) * 0.5


def mask_of(table, b, t):
    return table[pl.ds(pl.multiple_of(TABLE_MASK + b * t, 8), t), :]


def sides(values_ref, wide, left_at, right_at, outer, inner, consts, table, weights):
    t, width = outer.shape
    wide[...] = values_ref[...].astype(F32)
    values = jnp.concatenate([wide[pl.ds(k, t, stride=t), :] for k in range(t)], axis=0).astype(BF16)
    normed = norm_pair(values, consts, *in_norm(table, 0))
    for k, target in enumerate((left_at, right_at)):
        span = slice(2 * k * width, 2 * (k + 1) * width)
        side = gated(normed, weights[0, :, span], half_bias(table, 0, 2 * k, 2 * k + 2), width)
        target[...] = masked(side, outer, inner).astype(F32)


def gate_of(values, consts, table, weights, u):
    normed = norm_pair(values, consts, *in_norm(table, u))
    return gate(normed, weights[u, :, 4 * values.shape[1] :], half_bias(table, u, 4, 5))


def own_kernel(n, t, pair, table, w_in, weights, left, right, gating, wide):
    r, c = lax.axis_index("row"), lax.axis_index("col")
    consts = constants(wide.shape[1])
    weights[...] = w_in[...] * 0.5
    outer, inner = mask_of(table, c, t), mask_of(table, r, t)
    sides(pair, wide, left, right, outer, inner, consts, table, weights)
    gating[...] = gate_of(pair[...], consts, table, weights, 0)


def slot_sum(t, step, block, table, weights, lefts, rights, old, mixed, wide, left, right):
    r, c = lax.axis_index("row"), lax.axis_index("col")
    b = c ^ step
    outer, inner = mask_of(table, b, t), mask_of(table, r, t)
    sides(block, wide, left, right, outer, inner, constants(wide.shape[1]), table, weights)
    mix(mixed.at[0], old.at[0], row_of(left), rows_of(rights, t, b), t)
    mix(mixed.at[1], old.at[1], row_of(lefts, b), rows_of(right, t), t)


def column_kernel(n, t, steps, *refs):
    blocks, rows = refs[:n], refs[n : 2 * n - 2]
    table, weights, own_left, own_right = refs[2 * n - 2 : 2 * n + 2]
    lefts, rights, pair, gating, mixed, held, wide, left, right = refs[2 * n + 2 :]
    r, c = lax.axis_index("row"), lax.axis_index("col")
    consts = constants(wide.shape[1])
    for s in range(n):
        held[s] = blocks[s][...]

    def prepare(b, _):
        outer, inner = mask_of(table, b, t), mask_of(table, c, t)
        sides(held.at[r ^ place(b, n)], wide, lefts.at[b], rights.at[b], outer, inner, consts, table, weights)
        return 0

    lax.fori_loop(0, n, prepare, 0)
    own = held[r ^ place(r, n)]
    pair[...] = own
    gating[...] = gate_of(own, consts, table, weights, 0)
    mix(mixed.at[0], None, row_of(own_left), rows_of(rights, t, c), t)
    mix(mixed.at[1], None, row_of(lefts, c), rows_of(own_right, t), t)
    for step, block in zip(steps, rows):
        slot_sum(t, step, block, table, weights, lefts, rights, mixed, mixed, wide, left, right)


def last_kernel(n, t, step, *refs):
    block, table, weights, lefts, rights, old, w_out, pair, gating, col_pair, col_gating = refs[:11]
    pair_ref, left_ref, right_ref, mixed, wide, left, right = refs[11:]
    slot_sum(t, step, block, table, weights, lefts, rights, old, mixed, wide, left, right)
    width = wide.shape[1]
    r, c = lax.axis_index("row"), lax.axis_index("col")
    consts = constants(width)
    here, there = mask_of(table, r, t), mask_of(table, c, t)
    for k, (base, factor) in enumerate(((pair, gating), (col_pair, col_gating))):
        updated = finish(base[...], mixed[k], factor[...], consts, *out_norm(table, 0), w_out[0], table[8:9])
        normed = norm_pair(updated, consts, *in_norm(table, 1))
        if k == 0:
            pair_ref[...] = updated
            side = gated(normed, weights[1, :, 2 * width : 4 * width], half_bias(table, 1, 2, 4), width)
            right_ref[...] = masked(side, here, there)
        else:
            side = gated(normed, weights[1, :, : 2 * width], half_bias(table, 1, 0, 2), width)
            left_ref[...] = masked(side, there, here)


def gate_kernel(pair, table, weights, gating):
    gating[...] = gate_of(pair[...], constants(pair.shape[1]), table, weights, 1)


def right_kernel(n, t, *refs):
    blocks, left = refs[:n], refs[n]
    rights, mixed, wide = refs[n + 1 :]
    r, c = lax.axis_index("row"), lax.axis_index("col")
    for s in range(n):
        rights[s] = blocks[s][...].astype(F32)
    wide[...] = left[...].astype(F32)
    mix(mixed, None, row_of(wide), rows_of(rights, t, r ^ c), t)


def left_sum(n, t, slot, left, rights, old, mixed, wide):
    r, c = lax.axis_index("row"), lax.axis_index("col")
    wide[...] = left[...].astype(F32)
    mix(mixed, old, row_of(wide), rows_of(rights, t, r ^ c ^ slot), t)


def left_kernel(n, t, slot, *refs):
    left_sum(n, t, slot, *refs)


def end_kernel(n, t, slot, left, rights, old, pair, gating, table, w_out, out, mixed, wide):
    left_sum(n, t, slot, left, rights, old, mixed, wide)
    consts = constants(wide.shape[1])
    out[...] = finish(pair[...], mixed[...], gating[...], consts, *out_norm(table, 1), w_out[1], table[9:10])


def solution(mesh):
    n = mesh.shape["col"]
    half = n // 2

    def along(block, axis, step):
        return lax.ppermute(block, axis, [(k, k ^ step) for k in range(n)])

    def mirrored(block):
        pairs = [(a * n + z, (z // 2 + z % 2 * half) * n + a) for a in range(n) for z in range(n)]
        return lax.ppermute(block, ("row", "col"), pairs)

    def plane(block):
        return [block] + [along(block, "row", step) for step in range(1, n)]

    def per_device(pair, token_mask, in_gain, in_shift, w_in, bias_in, out_gain, out_shift, w_out, bias_out):
        t, _, width = pair.shape
        area = (t * t, width)
        narrow, broad = jax.ShapeDtypeStruct(area, BF16), jax.ShapeDtypeStruct(area, F32)
        stacked = jax.ShapeDtypeStruct((n,) + area, F32)
        twice = jax.ShapeDtypeStruct((2,) + area, F32)
        scratch = pltpu.VMEM(area, F32)

        def call(kernel, name, outs, scratches, *operands, alias=None, **specs):
            return pl.pallas_call(
                kernel,
                out_shape=outs,
                **specs,
                scratch_shapes=scratches,
                input_output_aliases=alias or {},

                compiler_params=pltpu.CompilerParams(vmem_limit_bytes=(16 + n) * 1024 * 1024),
                name=name,
            )(*operands)

        pair = pair.reshape(area)
        col_block = mirrored(pair)
        steps = [step for step in range(1, n) if step != half] + [half]
        rows = [along(pair, "col", step) for step in steps]
        mask = jnp.broadcast_to(token_mask.astype(F32)[:, None], (n * t, width))
        vectors = [in_gain, in_shift, out_gain, out_shift, bias_out, bias_in.reshape(-1, width)]
        table = jnp.concatenate(vectors + [jnp.zeros((TABLE_MASK - 20, width), F32), mask])
        weights, own_left, own_right, gating = call(
            functools.partial(own_kernel, n, t),
            "own_sides",
            (jax.ShapeDtypeStruct(w_in.shape, BF16), broad, broad, broad),
            [scratch],
            pair,
            table,
            w_in,
        )
        col_block, own_left = lax.optimization_barrier((col_block, own_left))
        lefts, rights, col_pair, col_gating, mixed = call(
            functools.partial(column_kernel, n, t, steps[:-1]),
            "column_sides",
            (stacked, stacked, narrow, broad, twice),
            [pltpu.VMEM((n,) + area, BF16)] + [scratch] * 3,
            *plane(col_block),
            *rows[:-1],
            table,
            weights,
            own_left,
            own_right,
        )
        pair, left, right = call(
            functools.partial(last_kernel, n, t, steps[-1]),
            "last_slot",
            (narrow,) * 3,
            [pltpu.VMEM((2,) + area, F32)] + [scratch] * 3,
            rows[-1],
            table,
            weights,
            lefts,
            rights,
            mixed,
            w_out,
            pair,
            gating,
            col_pair,
            col_gating,
        )
        blocks = [along(left, "col", step) for step in steps]
        gating = call(gate_kernel, "gate", broad, [], pair, table, weights)
        rights, mixed = call(
            functools.partial(right_kernel, n, t), "right_slots", (stacked, broad), [scratch], *plane(right), left
        )
        for step, block in zip(steps[:-1], blocks[:-1]):
            mixed = call(
                functools.partial(left_kernel, n, t, step),
                "left_slot",
                broad,
                [scratch],
                block,
                rights,
                mixed,
                alias={2: 0},
            )
        out = call(
            functools.partial(end_kernel, n, t, steps[-1]),
            "end",
            narrow,
            [scratch] * 2,
            blocks[-1],
            rights,
            mixed,
            pair,
            gating,
            table,
            w_out,
        )
        return out.reshape(t, t, width)

    placed = (P(("groups", "row"), "col", None), P("groups")) + (P(),) * 8
    return jax.shard_map(
        per_device, mesh=mesh, in_specs=placed, out_specs=P(("groups", "row"), "col", None), check_vma=False
    )
```

```python
import functools

import jax
import jax.numpy as jnp
from jax import lax
from jax.experimental import pallas as pl
from jax.experimental.pallas import tpu as pltpu
from jax.sharding import PartitionSpec as P

F32, BF16 = jnp.float32, jnp.bfloat16


def dot(a, b):
    return jnp.dot(a, b, preferred_element_type=F32)


def split(values):
    high = values.astype(BF16)
    return jnp.concatenate([high, (values - high.astype(F32)).astype(BF16)], axis=1)


def constants(width):
    rows = lax.broadcasted_iota(jnp.int32, (2 * width, width), 0)
    cols = lax.broadcasted_iota(jnp.int32, (2 * width, width), 1)
    mean = jnp.full((2 * width, width), 1.0 / width, F32)
    center = jnp.where((rows == cols) | (rows == cols + width), 1.0, 0.0) - mean
    return center.astype(BF16), mean.astype(BF16)


def scaled(center, mean, gain, shift):
    spread = dot(split(center * center), mean)
    return (center * lax.rsqrt(spread + 1e-05) * gain + shift).astype(BF16)


def norm_pair(values, consts, gain, shift):
    return scaled(dot(values, consts[0][: values.shape[1]]), consts[1], gain, shift)


def norm_mixed(values, consts, gain, shift):
    return scaled(dot(split(values), consts[0]), consts[1], gain, shift)


def gated(normed, weights, bias, width):
    product = dot(normed, weights) + bias
    return (jnp.tanh(product[:, width:]) + 1.0) * product[:, :width]


def gate(normed, weights, bias):
    return 0.5 * jnp.tanh(dot(normed, weights) + bias) + 0.5


def masked(values, outer, inner):
    t = outer.shape[0]
    grid = jnp.concatenate([outer[k : k + 1] * inner for k in range(t)], axis=0)
    return (values * grid).astype(BF16)


def mix(out_ref, old_ref, lefts, rights, first, last, left_at, right_at, t):
    width = out_ref.shape[1]
    for base in range(0, t, 8):
        if old_ref is None:
            total = (jnp.zeros((t, width), F32),) * 8
        else:
            total = tuple(old_ref[pl.ds((base + i) * t, t), :] for i in range(8))

        def slot(s, total):
            ls, rs = left_at(s), right_at(s)

            def step(q, total):
                for u in range(4):
                    at = pl.multiple_of((q * 4 + u) * t, 8)
                    row = rights[rs, pl.ds(at, t), :]
                    total = tuple(total[i] + lefts[ls, pl.ds(at + base + i, 1), :] * row for i in range(8))
                return total

            return lax.fori_loop(0, t // 4, step, total)

        total = lax.fori_loop(first, last, slot, total)
        for i in range(8):
            out_ref[pl.ds((base + i) * t, t), :] = total[i]


def finish(pair, mixed, gating, consts, gain, shift, weights, bias):
    normout = norm_mixed(mixed, consts, gain, shift)
    return (pair.astype(F32) + gating * (dot(normout, weights) + bias)).astype(BF16)


TABLE_MASK = 24


def in_norm(table, u):
    return table[u : u + 1], table[2 + u : 3 + u]


def out_norm(table, u):
    return table[4 + u : 5 + u], table[6 + u : 7 + u]


def half_bias(table, u, first, last):
    return jnp.concatenate([table[k : k + 1] for k in range(10 + 5 * u + first, 10 + 5 * u + last)], axis=1) * 0.5


def mask_of(table, b, t):
    return table[pl.ds(pl.multiple_of(TABLE_MASK + b * t, 8), t), :]


def sides(values_ref, wide, left_at, right_at, outer, inner, consts, table, weights):
    t, width = outer.shape
    wide[...] = values_ref[...].astype(F32)
    values = jnp.concatenate([wide[pl.ds(k, t, stride=t), :] for k in range(t)], axis=0).astype(BF16)
    normed = norm_pair(values, consts, *in_norm(table, 0))
    for k, target in enumerate((left_at, right_at)):
        span = slice(2 * k * width, 2 * (k + 1) * width)
        side = gated(normed, weights[0, :, span], half_bias(table, 0, 2 * k, 2 * k + 2), width)
        target[...] = masked(side, outer, inner).astype(F32)


def gate_of(values, consts, table, weights, u):
    normed = norm_pair(values, consts, *in_norm(table, u))
    return gate(normed, weights[u, :, 4 * values.shape[1] :], half_bias(table, u, 4, 5))


def own_kernel(t, pair, table, w_in, weights, row_l, row_r, gating, wide):
    r, c = lax.axis_index("row"), lax.axis_index("col")
    consts = constants(wide.shape[1])
    weights[...] = w_in[...] * 0.5
    outer, inner = mask_of(table, c, t), mask_of(table, r, t)
    sides(pair, wide, row_l.at[0], row_r.at[0], outer, inner, consts, table, weights)
    gating[...] = gate_of(pair[...], consts, table, weights, 0)


def rows_kernel(t, count, *refs):
    blocks, (col_pair, table, weights) = refs[:count], refs[count : count + 3]
    row_l, row_r, col_l, col_r, col_gating, wide = refs[count + 5 :]
    r, c = lax.axis_index("row"), lax.axis_index("col")
    consts = constants(wide.shape[1])
    here, there = mask_of(table, r, t), mask_of(table, c, t)
    sides(col_pair, wide, col_l.at[0], col_r.at[0], here, there, consts, table, weights)
    col_gating[...] = gate_of(col_pair[...], consts, table, weights, 0)
    for s, block in enumerate(blocks, 1):
        outer = mask_of(table, c ^ s, t)
        sides(block, wide, row_l.at[s], row_r.at[s], outer, here, consts, table, weights)


def columns_kernel(n, t, *refs):
    blocks, (table, weights, row_l, row_r) = refs[: n - 1], refs[n - 1 : n + 3]
    col_l, col_r, mixed, wide = refs[n + 5 :]
    r, c = lax.axis_index("row"), lax.axis_index("col")
    consts = constants(wide.shape[1])
    for s, block in enumerate(blocks, 1):
        outer, inner = mask_of(table, r ^ s, t), mask_of(table, c, t)
        sides(block, wide, col_l.at[s], col_r.at[s], outer, inner, consts, table, weights)
    mix(mixed.at[0], None, row_l, col_r, 0, n - 1, lambda s: s, lambda s: r ^ c ^ s, t)
    mix(mixed.at[1], None, col_l, row_r, 0, n - 1, lambda s: r ^ c ^ s, lambda s: s, t)


def last_kernel(n, t, *refs):
    block, table, weights, col_l, col_r, old, w_out, pair, gating, col_pair, col_gating = refs[:11]
    pair_ref, left_ref, right_ref, mixed, wide, left, right = refs[11:]
    width = wide.shape[1]
    r, c = lax.axis_index("row"), lax.axis_index("col")
    consts = constants(width)
    here, there = mask_of(table, r, t), mask_of(table, c, t)
    outer = mask_of(table, c ^ (n - 1), t)
    sides(block, wide, left.at[0], right.at[0], outer, here, consts, table, weights)
    source = r ^ c ^ (n - 1)
    mix(mixed.at[0], old.at[0], left, col_r, 0, 1, lambda s: s, lambda s: source, t)
    mix(mixed.at[1], old.at[1], col_l, right, 0, 1, lambda s: source, lambda s: s, t)
    for k, (base, factor) in enumerate(((pair, gating), (col_pair, col_gating))):
        updated = finish(base[...], mixed[k], factor[...], consts, *out_norm(table, 0), w_out[0], table[8:9])
        normed = norm_pair(updated, consts, *in_norm(table, 1))
        if k == 0:
            pair_ref[...] = updated
            side = gated(normed, weights[1, :, 2 * width : 4 * width], half_bias(table, 1, 2, 4), width)
            right_ref[...] = masked(side, here, there)
        else:
            side = gated(normed, weights[1, :, : 2 * width], half_bias(table, 1, 0, 2), width)
            left_ref[...] = masked(side, there, here)


def gate_kernel(pair, table, weights, gating):
    gating[...] = gate_of(pair[...], constants(pair.shape[1]), table, weights, 1)


def middle_kernel(n, t, *refs):
    blocks, sources = refs[: n - 1], refs[n - 1 : 2 * n - 1]
    rights, mixed, lefts = refs[2 * n - 1 :]
    r, c = lax.axis_index("row"), lax.axis_index("col")
    for s in range(n - 1):
        lefts[s] = blocks[s][...].astype(F32)
    for s in range(n):
        rights[s] = sources[s][...].astype(F32)
    mix(mixed, None, lefts, rights, 0, n - 1, lambda s: s, lambda s: r ^ c ^ s, t)


def end_kernel(n, t, block, rights, old, pair, gating, table, w_out, out, mixed, left):
    r, c = lax.axis_index("row"), lax.axis_index("col")
    left[0] = block[...].astype(F32)
    mix(mixed, old, left, rights, 0, 1, lambda s: s, lambda s: r ^ c ^ (n - 1), t)
    consts = constants(mixed.shape[1])
    out[...] = finish(pair[...], mixed[...], gating[...], consts, *out_norm(table, 1), w_out[1], table[9:10])


def solution(mesh):
    n = mesh.shape["col"]

    def gather(block, axis, after=lambda block: block):
        held, step = {0: block}, n // 2
        while step:
            for s, part in list(held.items()):
                part = after(part) if s else part
                held[s ^ step] = lax.ppermute(part, axis, [(k, k ^ step) for k in range(n)])
            step //= 2
        return [held[s] for s in range(n)]

    def mirrored(block):
        return lax.ppermute(block, ("row", "col"), [(a * n + z, z * n + a) for a in range(n) for z in range(n)])

    def per_device(pair, token_mask, in_gain, in_shift, w_in, bias_in, out_gain, out_shift, w_out, bias_out):
        t, _, width = pair.shape
        area = (t * t, width)
        narrow, broad = jax.ShapeDtypeStruct(area, BF16), jax.ShapeDtypeStruct(area, F32)
        row_like = jax.ShapeDtypeStruct((n - 1,) + area, F32)
        col_like = jax.ShapeDtypeStruct((n,) + area, F32)
        twice = jax.ShapeDtypeStruct((2,) + area, F32)
        scratch = pltpu.VMEM(area, F32)

        def call(kernel, name, outs, scratches, *operands, alias=None, **specs):
            return pl.pallas_call(
                kernel,
                out_shape=outs,
                scratch_shapes=scratches,
                input_output_aliases=alias or {},

                compiler_params=pltpu.CompilerParams(vmem_limit_bytes=(16 + n) * 1024 * 1024),
                name=name,
            )(*operands)

        pair = pair.reshape(area)
        col_pair = mirrored(pair)
        mask = jnp.broadcast_to(token_mask.astype(F32)[:, None], (n * t, width))
        vectors = [in_gain, in_shift, out_gain, out_shift, bias_out, bias_in.reshape(-1, width)]
        table = jnp.concatenate(vectors + [jnp.zeros((TABLE_MASK - 20, width), F32), mask])
        weights, row_l, row_r, gating = call(
            functools.partial(own_kernel, t),
            "own_sides",
            (jax.ShapeDtypeStruct(w_in.shape, BF16), row_like, row_like, broad),
            [scratch],
            pair,
            table,
            w_in,
        )
        after = lambda block: lax.optimization_barrier((block, row_l))[0]
        rows, cols = gather(pair, "col", after), gather(after(col_pair), "row")
        row_l, row_r, col_l, col_r, col_gating = call(
            functools.partial(rows_kernel, t, n - 2),
            "row_sides",
            (row_like, row_like, col_like, col_like, broad),
            [scratch],
            *rows[1:-1],
            col_pair,
            table,
            weights,
            row_l,
            row_r,
            alias={n + 1: 0, n + 2: 1},
        )
        col_l, col_r, mixed = call(
            functools.partial(columns_kernel, n, t),
            "column_sides",
            (col_like, col_like, twice),
            [scratch],
            *cols[1:],
            table,
            weights,
            row_l,
            row_r,
            col_l,
            col_r,
            alias={n + 3: 0, n + 4: 1},
        )
        pair, left, right = call(
            functools.partial(last_kernel, n, t),
            "last_slot",
            (narrow,) * 3,
            [pltpu.VMEM((2,) + area, F32), scratch] + [pltpu.VMEM((1,) + area, F32)] * 2,
            rows[-1],
            table,
            weights,
            col_l,
            col_r,
            mixed,
            w_out,
            pair,
            gating,
            col_pair,
            col_gating,
        )
        lefts, rights = gather(left, "col"), gather(right, "row")
        gating = call(gate_kernel, "gate", broad, [], pair, table, weights)
        rights, mixed = call(
            functools.partial(middle_kernel, n, t),
            "middle_slots",
            (col_like, broad),
            [pltpu.VMEM((n - 1,) + area, F32)],
            *lefts[:-1],
            *rights,
        )
        out = call(
            functools.partial(end_kernel, n, t),
            "end",
            narrow,
            [scratch, pltpu.VMEM((1,) + area, F32)],
            lefts[-1],
            rights,
            mixed,
            pair,
            gating,
            table,
            w_out,
        )
        return out.reshape(t, t, width)

    placed = (P(("groups", "row"), "col", None), P("groups")) + (P(),) * 8
    return jax.shard_map(
        per_device, mesh=mesh, in_specs=placed, out_specs=P(("groups", "row"), "col", None), check_vma=False
    )
```

```python
import functools

import jax
import jax.numpy as jnp
from jax import lax
from jax.experimental import pallas as pl
from jax.experimental.pallas import tpu as pltpu
from jax.sharding import PartitionSpec as P

F32, BF16 = jnp.float32, jnp.bfloat16


def dot(a, b):
    return jnp.dot(a, b, preferred_element_type=F32)


def split(values):
    high = values.astype(BF16)
    return jnp.concatenate([high, (values - high.astype(F32)).astype(BF16)], axis=1)


def constants(width):
    rows = lax.broadcasted_iota(jnp.int32, (2 * width, width), 0)
    cols = lax.broadcasted_iota(jnp.int32, (2 * width, width), 1)
    mean = jnp.full((2 * width, width), 1.0 / width, F32)
    center = jnp.where((rows == cols) | (rows == cols + width), 1.0, 0.0) - mean
    return center.astype(BF16), mean.astype(BF16)


def scaled(center, mean, gain, shift):
    spread = dot(split(center * center), mean)
    return (center * lax.rsqrt(spread + 1e-05) * gain + shift).astype(BF16)


def norm_pair(values, consts, gain, shift):
    return scaled(dot(values, consts[0][: values.shape[1]]), consts[1], gain, shift)


def norm_mixed(values, consts, gain, shift):
    return scaled(dot(split(values), consts[0]), consts[1], gain, shift)


def gated(normed, weights, bias, width):
    product = dot(normed, weights) + bias
    return (jnp.tanh(product[:, width:]) + 1.0) * product[:, :width]


def gate(normed, weights, bias):
    return 0.5 * jnp.tanh(dot(normed, weights) + bias) + 0.5


def masked(values, outer, inner):
    t = outer.shape[0]
    grid = jnp.concatenate([outer[k : k + 1] * inner for k in range(t)], axis=0)
    return (values * grid).astype(BF16)


def mix(out_ref, old_ref, lefts, rights, first, last, left_at, right_at, t):
    width = out_ref.shape[1]
    for base in range(0, t, 8):
        if old_ref is None:
            total = (jnp.zeros((t, width), F32),) * 8
        else:
            total = tuple(old_ref[pl.ds((base + i) * t, t), :] for i in range(8))

        def slot(s, total):
            ls, rs = left_at(s), right_at(s)

            def step(q, total):
                for u in range(4):
                    at = pl.multiple_of((q * 4 + u) * t, 8)
                    row = rights[rs, pl.ds(at, t), :]
                    total = tuple(total[i] + lefts[ls, pl.ds(at + base + i, 1), :] * row for i in range(8))
                return total

            return lax.fori_loop(0, t // 4, step, total)

        total = lax.fori_loop(first, last, slot, total)
        for i in range(8):
            out_ref[pl.ds((base + i) * t, t), :] = total[i]


def finish(pair, mixed, gating, consts, gain, shift, weights, bias):
    normout = norm_mixed(mixed, consts, gain, shift)
    return (pair.astype(F32) + gating * (dot(normout, weights) + bias)).astype(BF16)


TABLE_MASK = 24


def in_norm(table, u):
    return table[u : u + 1], table[2 + u : 3 + u]


def out_norm(table, u):
    return table[4 + u : 5 + u], table[6 + u : 7 + u]


def half_bias(table, u, first, last):
    return jnp.concatenate([table[k : k + 1] for k in range(10 + 5 * u + first, 10 + 5 * u + last)], axis=1) * 0.5


def mask_of(table, b, t):
    return table[pl.ds(pl.multiple_of(TABLE_MASK + b * t, 8), t), :]


def sides(values_ref, wide, left_at, right_at, outer, inner, consts, table, weights):
    t, width = outer.shape
    wide[...] = values_ref[...].astype(F32)
    values = jnp.concatenate([wide[pl.ds(k, t, stride=t), :] for k in range(t)], axis=0).astype(BF16)
    normed = norm_pair(values, consts, *in_norm(table, 0))
    for k, target in enumerate((left_at, right_at)):
        span = slice(2 * k * width, 2 * (k + 1) * width)
        side = gated(normed, weights[0, :, span], half_bias(table, 0, 2 * k, 2 * k + 2), width)
        target[...] = masked(side, outer, inner).astype(F32)


def gate_of(values, consts, table, weights, u):
    normed = norm_pair(values, consts, *in_norm(table, u))
    return gate(normed, weights[u, :, 4 * values.shape[1] :], half_bias(table, u, 4, 5))


def own_kernel(t, pair, table, w_in, weights, row_l, row_r, gating, wide):
    r, c = lax.axis_index("row"), lax.axis_index("col")
    consts = constants(wide.shape[1])
    weights[...] = w_in[...] * 0.5
    outer, inner = mask_of(table, c, t), mask_of(table, r, t)
    sides(pair, wide, row_l.at[0], row_r.at[0], outer, inner, consts, table, weights)
    gating[...] = gate_of(pair[...], consts, table, weights, 0)


def rows_kernel(t, count, *refs):
    blocks, (col_pair, table, weights) = refs[:count], refs[count : count + 3]
    row_l, row_r, col_l, col_r, col_gating, wide = refs[count + 5 :]
    r, c = lax.axis_index("row"), lax.axis_index("col")
    consts = constants(wide.shape[1])
    here, there = mask_of(table, r, t), mask_of(table, c, t)
    sides(col_pair, wide, col_l.at[0], col_r.at[0], here, there, consts, table, weights)
    col_gating[...] = gate_of(col_pair[...], consts, table, weights, 0)
    for s, block in enumerate(blocks, 1):
        outer = mask_of(table, c ^ s, t)
        sides(block, wide, row_l.at[s], row_r.at[s], outer, here, consts, table, weights)


def columns_kernel(t, count, *refs):
    blocks, (table, weights) = refs[:count], refs[count : count + 2]
    col_l, col_r, wide = refs[count + 4 :]
    r, c = lax.axis_index("row"), lax.axis_index("col")
    consts = constants(wide.shape[1])
    for s, block in enumerate(blocks, 1):
        outer, inner = mask_of(table, r ^ s, t), mask_of(table, c, t)
        sides(block, wide, col_l.at[s], col_r.at[s], outer, inner, consts, table, weights)


def mirror_kernel(n, t, *refs):
    row, col, table, weights, pair, gating, w_out = refs[:7]
    left_ref, row_l, row_r, col_l, col_r, mixed, wide = refs[11:]
    width = wide.shape[1]
    r, c = lax.axis_index("row"), lax.axis_index("col")
    consts = constants(width)
    here, there = mask_of(table, r, t), mask_of(table, c, t)
    for block, left, right, outer, inner in (
        (row, row_l, row_r, c ^ (n - 1), here),
        (col, col_l, col_r, r ^ (n - 1), there),
    ):
        outer = mask_of(table, outer, t)
        sides(block, wide, left.at[n - 1], right.at[n - 1], outer, inner, consts, table, weights)
    mix(mixed, None, col_l, row_r, 0, n, lambda s: r ^ c ^ s, lambda s: s, t)
    updated = finish(pair[...], mixed[...], gating[...], consts, *out_norm(table, 0), w_out[0], table[8:9])
    normed = norm_pair(updated, consts, *in_norm(table, 1))
    side = gated(normed, weights[1, :, : 2 * width], half_bias(table, 1, 0, 2), width)
    left_ref[...] = masked(side, there, here)


def own_end_kernel(n, t, row_l, col_r, table, weights, pair, gating, w_out, pair_ref, right_ref, mixed):
    width = mixed.shape[1]
    r, c = lax.axis_index("row"), lax.axis_index("col")
    consts = constants(width)
    mix(mixed, None, row_l, col_r, 0, n, lambda s: s, lambda s: r ^ c ^ s, t)
    updated = finish(pair[...], mixed[...], gating[...], consts, *out_norm(table, 0), w_out[0], table[8:9])
    pair_ref[...] = updated
    normed = norm_pair(updated, consts, *in_norm(table, 1))
    side = gated(normed, weights[1, :, 2 * width : 4 * width], half_bias(table, 1, 2, 4), width)
    right_ref[...] = masked(side, mask_of(table, r, t), mask_of(table, c, t))


def gate_kernel(pair, table, weights, gating):
    gating[...] = gate_of(pair[...], constants(pair.shape[1]), table, weights, 1)


def middle_kernel(n, t, *refs):
    blocks, sources = refs[: n - 1], refs[n - 1 : 2 * n - 1]
    rights, mixed, lefts = refs[2 * n - 1 :]
    r, c = lax.axis_index("row"), lax.axis_index("col")
    for s in range(n - 1):
        lefts[s] = blocks[s][...].astype(F32)
    for s in range(n):
        rights[s] = sources[s][...].astype(F32)
    mix(mixed, None, lefts, rights, 0, n - 1, lambda s: s, lambda s: r ^ c ^ s, t)


def end_kernel(n, t, block, rights, old, pair, gating, table, w_out, out, mixed, left):
    r, c = lax.axis_index("row"), lax.axis_index("col")
    left[0] = block[...].astype(F32)
    mix(mixed, old, left, rights, 0, 1, lambda s: s, lambda s: r ^ c ^ (n - 1), t)
    consts = constants(mixed.shape[1])
    out[...] = finish(pair[...], mixed[...], gating[...], consts, *out_norm(table, 1), w_out[1], table[9:10])


def solution(mesh):
    n = mesh.shape["col"]

    def gather(block, axis, after=lambda block: block):
        held, step = {0: block}, n // 2
        while step:
            for s, part in list(held.items()):
                part = after(part) if s else part
                held[s ^ step] = lax.ppermute(part, axis, [(k, k ^ step) for k in range(n)])
            step //= 2
        return [held[s] for s in range(n)]

    def mirrored(block):
        return lax.ppermute(block, ("row", "col"), [(a * n + z, z * n + a) for a in range(n) for z in range(n)])

    def per_device(pair, token_mask, in_gain, in_shift, w_in, bias_in, out_gain, out_shift, w_out, bias_out):
        t, _, width = pair.shape
        area = (t * t, width)
        narrow, broad = jax.ShapeDtypeStruct(area, BF16), jax.ShapeDtypeStruct(area, F32)
        slots = jax.ShapeDtypeStruct((n,) + area, F32)
        scratch = pltpu.VMEM(area, F32)

        def call(kernel, name, outs, scratches, *operands, alias=None, **specs):
            return pl.pallas_call(
                kernel,
                out_shape=outs,
                scratch_shapes=scratches,
                input_output_aliases=alias or {},

                compiler_params=pltpu.CompilerParams(vmem_limit_bytes=(16 + n) * 1024 * 1024),
                name=name,
            )(*operands)

        pair = pair.reshape(area)
        col_pair = mirrored(pair)
        mask = jnp.broadcast_to(token_mask.astype(F32)[:, None], (n * t, width))
        vectors = [in_gain, in_shift, out_gain, out_shift, bias_out, bias_in.reshape(-1, width)]
        table = jnp.concatenate(vectors + [jnp.zeros((TABLE_MASK - 20, width), F32), mask])
        weights, row_l, row_r, gating = call(
            functools.partial(own_kernel, t),
            "own_sides",
            (jax.ShapeDtypeStruct(w_in.shape, BF16), slots, slots, broad),
            [scratch],
            pair,
            table,
            w_in,
        )
        after = lambda block: lax.optimization_barrier((block, row_l))[0]
        rows = gather(pair, "col", after)
        cols = gather(lax.optimization_barrier((col_pair, rows[n // 2], row_l))[0], "row")
        row_l, row_r, col_l, col_r, col_gating = call(
            functools.partial(rows_kernel, t, n - 2),
            "row_sides",
            (slots, slots, slots, slots, broad),
            [scratch],
            *rows[1:-1],
            col_pair,
            table,
            weights,
            row_l,
            row_r,
            alias={n + 1: 0, n + 2: 1},
        )
        col_l, col_r = call(
            functools.partial(columns_kernel, t, n - 2),
            "column_sides",
            (slots, slots),
            [scratch],
            *cols[1:-1],
            table,
            weights,
            col_l,
            col_r,
            alias={n: 0, n + 1: 1},
        )
        left, row_l, _, _, col_r = call(
            functools.partial(mirror_kernel, n, t),
            "mirror_end",
            (narrow, slots, slots, slots, slots),
            [scratch] * 2,
            rows[-1],
            cols[-1],
            table,
            weights,
            col_pair,
            col_gating,
            w_out,
            row_l,
            row_r,
            col_l,
            col_r,
            alias={7: 1, 8: 2, 9: 3, 10: 4},
        )
        pair, right = call(
            functools.partial(own_end_kernel, n, t),
            "own_end",
            (narrow, narrow),
            [scratch],
            row_l,
            col_r,
            table,
            weights,
            pair,
            gating,
            w_out,
        )
        lefts = gather(left, "col")
        rights = [right] + [lax.ppermute(right, "row", [(k, k ^ s) for k in range(n)]) for s in range(1, n)]
        gating = call(gate_kernel, "gate", broad, [], pair, table, weights)
        rights, mixed = call(
            functools.partial(middle_kernel, n, t),
            "middle_slots",
            (slots, broad),
            [pltpu.VMEM((n - 1,) + area, F32)],
            *lefts[:-1],
            *rights,
        )
        out = call(
            functools.partial(end_kernel, n, t),
            "end",
            narrow,
            [scratch, pltpu.VMEM((1,) + area, F32)],
            lefts[-1],
            rights,
            mixed,
            pair,
            gating,
            table,
            w_out,
        )
        return out.reshape(t, t, width)

    placed = (P(("groups", "row"), "col", None), P("groups")) + (P(),) * 8
    return jax.shard_map(
        per_device, mesh=mesh, in_specs=placed, out_specs=P(("groups", "row"), "col", None), check_vma=False
    )
```

```python
import functools

import jax
import jax.numpy as jnp
from jax import lax
from jax.experimental import pallas as pl
from jax.experimental.pallas import tpu as pltpu
from jax.sharding import PartitionSpec as P

F32, BF16 = jnp.float32, jnp.bfloat16


def dot(a, b):
    return jnp.dot(a, b, preferred_element_type=F32)


def split(values):
    high = values.astype(BF16)
    return jnp.concatenate([high, (values - high.astype(F32)).astype(BF16)], axis=1)


def constants(width):
    rows = lax.broadcasted_iota(jnp.int32, (2 * width, width), 0)
    cols = lax.broadcasted_iota(jnp.int32, (2 * width, width), 1)
    mean = jnp.full((2 * width, width), 1.0 / width, F32)
    center = jnp.where((rows == cols) | (rows == cols + width), 1.0, 0.0) - mean
    return center.astype(BF16), mean.astype(BF16)


def scaled(center, mean, gain, shift):
    spread = dot(split(center * center), mean)
    return (center * lax.rsqrt(spread + 1e-05) * gain + shift).astype(BF16)


def norm_pair(values, consts, gain, shift):
    return scaled(dot(values, consts[0][: values.shape[1]]), consts[1], gain, shift)


def norm_mixed(values, consts, gain, shift):
    return scaled(dot(split(values), consts[0]), consts[1], gain, shift)


def gated(normed, weights, bias, width):
    product = dot(normed, weights) + bias
    return (jnp.tanh(product[:, width:]) + 1.0) * product[:, :width]


def gate(normed, weights, bias):
    return 0.5 * jnp.tanh(dot(normed, weights) + bias) + 0.5


def masked(values, outer, inner):
    t = outer.shape[0]
    grid = jnp.concatenate([outer[k : k + 1] * inner for k in range(t)], axis=0)
    return (values * grid).astype(BF16)


def mix(out_ref, old_ref, lefts, rights, first, last, left_at, right_at, t):
    width = out_ref.shape[1]
    for base in range(0, t, 8):
        if old_ref is None:
            total = (jnp.zeros((t, width), F32),) * 8
        else:
            total = tuple(old_ref[pl.ds((base + i) * t, t), :] for i in range(8))

        def slot(s, total):
            ls, rs = left_at(s), right_at(s)

            def step(q, total):
                for u in range(4):
                    at = pl.multiple_of((q * 4 + u) * t, 8)
                    row = rights[rs, pl.ds(at, t), :]
                    total = tuple(total[i] + lefts[ls, pl.ds(at + base + i, 1), :] * row for i in range(8))
                return total

            return lax.fori_loop(0, t // 4, step, total)

        total = lax.fori_loop(first, last, slot, total)
        for i in range(8):
            out_ref[pl.ds((base + i) * t, t), :] = total[i]


def finish(pair, mixed, gating, consts, gain, shift, weights, bias):
    normout = norm_mixed(mixed, consts, gain, shift)
    return (pair.astype(F32) + gating * (dot(normout, weights) + bias)).astype(BF16)


TABLE_MASK = 24


def in_norm(table, u):
    return table[u : u + 1], table[2 + u : 3 + u]


def out_norm(table, u):
    return table[4 + u : 5 + u], table[6 + u : 7 + u]


def half_bias(table, u, first, last):
    return jnp.concatenate([table[k : k + 1] for k in range(10 + 5 * u + first, 10 + 5 * u + last)], axis=1) * 0.5


def mask_of(table, b, t):
    return table[pl.ds(pl.multiple_of(TABLE_MASK + b * t, 8), t), :]


def sides(values_ref, wide, left_at, right_at, outer, inner, consts, table, weights):
    t, width = outer.shape
    wide[...] = values_ref[...].astype(F32)
    values = jnp.concatenate([wide[pl.ds(k, t, stride=t), :] for k in range(t)], axis=0).astype(BF16)
    normed = norm_pair(values, consts, *in_norm(table, 0))
    for k, target in enumerate((left_at, right_at)):
        span = slice(2 * k * width, 2 * (k + 1) * width)
        side = gated(normed, weights[0, :, span], half_bias(table, 0, 2 * k, 2 * k + 2), width)
        target[...] = masked(side, outer, inner).astype(F32)


def gate_of(values, consts, table, weights, u):
    normed = norm_pair(values, consts, *in_norm(table, u))
    return gate(normed, weights[u, :, 4 * values.shape[1] :], half_bias(table, u, 4, 5))


def place(b, n):
    return b // 2 + lax.rem(b, 2) * (n // 2)


def placed_at(r, n):
    return lax.rem(r, n // 2) * 2 + r // (n // 2)


def own_kernel(t, pair, table, w_in, weights, row_l, row_r, gating, wide):
    r, c = lax.axis_index("row"), lax.axis_index("col")
    consts = constants(wide.shape[1])
    weights[...] = w_in[...] * 0.5
    outer, inner = mask_of(table, c, t), mask_of(table, r, t)
    sides(pair, wide, row_l.at[0], row_r.at[0], outer, inner, consts, table, weights)
    gating[...] = gate_of(pair[...], consts, table, weights, 0)


def rows_kernel(t, count, *refs):
    blocks, (col_block, table, weights) = refs[:count], refs[count : count + 3]
    row_l, row_r, col_l, col_r, wide = refs[count + 5 :]
    r, c = lax.axis_index("row"), lax.axis_index("col")
    consts = constants(wide.shape[1])
    here, there = mask_of(table, r, t), mask_of(table, c, t)
    outer = mask_of(table, placed_at(r, count + 2), t)
    sides(col_block, wide, col_l.at[0], col_r.at[0], outer, there, consts, table, weights)
    for s, block in enumerate(blocks, 1):
        outer = mask_of(table, c ^ s, t)
        sides(block, wide, row_l.at[s], row_r.at[s], outer, here, consts, table, weights)


def columns_kernel(t, count, *refs):
    blocks, (table, weights) = refs[:count], refs[count : count + 2]
    col_l, col_r, wide = refs[count + 4 :]
    r, c = lax.axis_index("row"), lax.axis_index("col")
    consts = constants(wide.shape[1])
    for s, block in enumerate(blocks, 1):
        outer, inner = mask_of(table, placed_at(r ^ s, count + 2), t), mask_of(table, c, t)
        sides(block, wide, col_l.at[s], col_r.at[s], outer, inner, consts, table, weights)


def mirror_kernel(n, t, *refs):
    row, cols, (table, weights, w_out) = refs[0], refs[1 : n + 1], refs[n + 1 : n + 4]
    left_ref, row_l, row_r, col_l, col_r, mixed, wide, held = refs[n + 8 :]
    width = wide.shape[1]
    r, c = lax.axis_index("row"), lax.axis_index("col")
    consts = constants(width)
    here, there = mask_of(table, r, t), mask_of(table, c, t)
    for block, left, right, outer, inner in (
        (row, row_l, row_r, c ^ (n - 1), here),
        (cols[-1], col_l, col_r, placed_at(r ^ (n - 1), n), there),
    ):
        outer = mask_of(table, outer, t)
        sides(block, wide, left.at[n - 1], right.at[n - 1], outer, inner, consts, table, weights)
    mix(mixed, None, col_l, row_r, 0, n, lambda s: r ^ place(c ^ s, n), lambda s: s, t)
    for s in range(n):
        held[s] = cols[s][...]
    pair = held[r ^ place(r, n)]
    updated = finish(pair, mixed[...], gate_of(pair, consts, table, weights, 0), consts, *out_norm(table, 0), w_out[0], table[8:9])
    normed = norm_pair(updated, consts, *in_norm(table, 1))
    side = gated(normed, weights[1, :, : 2 * width], half_bias(table, 1, 0, 2), width)
    left_ref[...] = masked(side, there, here)


def own_end_kernel(n, t, row_l, col_r, table, weights, pair, gating, w_out, pair_ref, right_ref, mixed):
    width = mixed.shape[1]
    r, c = lax.axis_index("row"), lax.axis_index("col")
    consts = constants(width)
    mix(mixed, None, row_l, col_r, 0, n, lambda s: s, lambda s: r ^ place(c ^ s, n), t)
    updated = finish(pair[...], mixed[...], gating[...], consts, *out_norm(table, 0), w_out[0], table[8:9])
    pair_ref[...] = updated
    normed = norm_pair(updated, consts, *in_norm(table, 1))
    side = gated(normed, weights[1, :, 2 * width : 4 * width], half_bias(table, 1, 2, 4), width)
    right_ref[...] = masked(side, mask_of(table, r, t), mask_of(table, c, t))


def gate_kernel(pair, table, weights, gating):
    gating[...] = gate_of(pair[...], constants(pair.shape[1]), table, weights, 1)


def middle_kernel(n, t, *refs):
    blocks, sources = refs[: n - 1], refs[n - 1 : 2 * n - 1]
    rights, mixed, lefts = refs[2 * n - 1 :]
    r, c = lax.axis_index("row"), lax.axis_index("col")
    for s in range(n - 1):
        lefts[s] = blocks[s][...].astype(F32)
    for s in range(n):
        rights[s] = sources[s][...].astype(F32)
    mix(mixed, None, lefts, rights, 0, n - 1, lambda s: s, lambda s: r ^ c ^ s, t)


def end_kernel(n, t, block, rights, old, pair, gating, table, w_out, out, mixed, left):
    r, c = lax.axis_index("row"), lax.axis_index("col")
    left[0] = block[...].astype(F32)
    mix(mixed, old, left, rights, 0, 1, lambda s: s, lambda s: r ^ c ^ (n - 1), t)
    consts = constants(mixed.shape[1])
    out[...] = finish(pair[...], mixed[...], gating[...], consts, *out_norm(table, 1), w_out[1], table[9:10])


def solution(mesh):
    n = mesh.shape["col"]

    def gather(block, axis, after=lambda block: block):
        held, step = {0: block}, n // 2
        while step:
            for s, part in list(held.items()):
                part = after(part) if s else part
                held[s ^ step] = lax.ppermute(part, axis, [(k, k ^ step) for k in range(n)])
            step //= 2
        return [held[s] for s in range(n)]

    def mirrored(block):
        pairs = [(a * n + z, (z // 2 + z % 2 * (n // 2)) * n + a) for a in range(n) for z in range(n)]
        return lax.ppermute(block, ("row", "col"), pairs)

    def per_device(pair, token_mask, in_gain, in_shift, w_in, bias_in, out_gain, out_shift, w_out, bias_out):
        t, _, width = pair.shape
        area = (t * t, width)
        narrow, broad = jax.ShapeDtypeStruct(area, BF16), jax.ShapeDtypeStruct(area, F32)
        slots = jax.ShapeDtypeStruct((n,) + area, F32)
        scratch = pltpu.VMEM(area, F32)

        def call(kernel, name, outs, scratches, *operands, alias=None, **specs):
            return pl.pallas_call(
                kernel,
                out_shape=outs,
                scratch_shapes=scratches,
                input_output_aliases=alias or {},

                compiler_params=pltpu.CompilerParams(vmem_limit_bytes=(16 + n) * 1024 * 1024),
                name=name,
            )(*operands)

        pair = pair.reshape(area)
        col_block = mirrored(pair)
        mask = jnp.broadcast_to(token_mask.astype(F32)[:, None], (n * t, width))
        vectors = [in_gain, in_shift, out_gain, out_shift, bias_out, bias_in.reshape(-1, width)]
        table = jnp.concatenate(vectors + [jnp.zeros((TABLE_MASK - 20, width), F32), mask])
        weights, row_l, row_r, gating = call(
            functools.partial(own_kernel, t),
            "own_sides",
            (jax.ShapeDtypeStruct(w_in.shape, BF16), slots, slots, broad),
            [scratch],
            pair,
            table,
            w_in,
        )
        after = lambda block: lax.optimization_barrier((block, row_l))[0]
        rows = gather(pair, "col", after)
        cols = gather(lax.optimization_barrier((col_block, rows[1], rows[n // 2], row_l))[0], "row")
        row_l, row_r, col_l, col_r = call(
            functools.partial(rows_kernel, t, n - 2),
            "row_sides",
            (slots,) * 4,
            [scratch],
            *rows[1:-1],
            col_block,
            table,
            weights,
            row_l,
            row_r,
            alias={n + 1: 0, n + 2: 1},
        )
        col_l, col_r = call(
            functools.partial(columns_kernel, t, n - 2),
            "column_sides",
            (slots, slots),
            [scratch],
            *cols[1:-1],
            table,
            weights,
            col_l,
            col_r,
            alias={n: 0, n + 1: 1},
        )
        left, row_l, _, _, col_r = call(
            functools.partial(mirror_kernel, n, t),
            "mirror_end",
            (narrow, slots, slots, slots, slots),
            [scratch] * 2 + [pltpu.VMEM((n,) + area, BF16)],
            rows[-1],
            *cols,
            table,
            weights,
            w_out,
            row_l,
            row_r,
            col_l,
            col_r,
            alias={n + 4: 1, n + 5: 2, n + 6: 3, n + 7: 4},
        )
        pair, right = call(
            functools.partial(own_end_kernel, n, t),
            "own_end",
            (narrow, narrow),
            [scratch],
            row_l,
            col_r,
            table,
            weights,
            pair,
            gating,
            w_out,
        )
        lefts = gather(left, "col")
        right = lax.optimization_barrier((right, lefts[1]))[0]
        rights = [right] + [lax.ppermute(right, "row", [(k, k ^ s) for k in range(n)]) for s in range(1, n)]
        gating = call(gate_kernel, "gate", broad, [], pair, table, weights)
        rights, mixed = call(
            functools.partial(middle_kernel, n, t),
            "middle_slots",
            (slots, broad),
            [pltpu.VMEM((n - 1,) + area, F32)],
            *lefts[:-1],
            *rights,
        )
        out = call(
            functools.partial(end_kernel, n, t),
            "end",
            narrow,
            [scratch, pltpu.VMEM((1,) + area, F32)],
            lefts[-1],
            rights,
            mixed,
            pair,
            gating,
            table,
            w_out,
        )
        return out.reshape(t, t, width)

    placed = (P(("groups", "row"), "col", None), P("groups")) + (P(),) * 8
    return jax.shard_map(
        per_device, mesh=mesh, in_specs=placed, out_specs=P(("groups", "row"), "col", None), check_vma=False
    )
```

```python
import functools

import jax
import jax.numpy as jnp
from jax import lax
from jax.experimental import pallas as pl
from jax.experimental.pallas import tpu as pltpu
from jax.sharding import PartitionSpec as P

F32, BF16 = jnp.float32, jnp.bfloat16


def dot(a, b):
    return jnp.dot(a, b, preferred_element_type=F32)


def split(values):
    high = values.astype(BF16)
    return jnp.concatenate([high, (values - high.astype(F32)).astype(BF16)], axis=1)


def constants(width):
    rows = lax.broadcasted_iota(jnp.int32, (2 * width, width), 0)
    cols = lax.broadcasted_iota(jnp.int32, (2 * width, width), 1)
    mean = jnp.full((2 * width, width), 1.0 / width, F32)
    center = jnp.where((rows == cols) | (rows == cols + width), 1.0, 0.0) - mean
    return center.astype(BF16), mean.astype(BF16)


def scaled(center, mean, gain, shift):
    spread = dot(split(center * center), mean)
    return (center * lax.rsqrt(spread + 1e-05) * gain + shift).astype(BF16)


def norm_pair(values, consts, gain, shift):
    return scaled(dot(values, consts[0][: values.shape[1]]), consts[1], gain, shift)


def norm_mixed(values, consts, gain, shift):
    return scaled(dot(split(values), consts[0]), consts[1], gain, shift)


def gated(normed, weights, bias, width):
    product = dot(normed, weights) + bias
    return (jnp.tanh(product[:, width:]) + 1.0) * product[:, :width]


def gate(normed, weights, bias):
    return 0.5 * jnp.tanh(dot(normed, weights) + bias) + 0.5


def masked(values, outer, inner):
    t = outer.shape[0]
    grid = jnp.concatenate([outer[k : k + 1] * inner for k in range(t)], axis=0)
    return (values * grid).astype(BF16)


def mix(out_ref, old_ref, lefts, rights, first, last, left_at, right_at, t):
    width = out_ref.shape[1]
    for base in range(0, t, 8):
        if old_ref is None:
            total = (jnp.zeros((t, width), F32),) * 8
        else:
            total = tuple(old_ref[pl.ds((base + i) * t, t), :] for i in range(8))

        def slot(s, total):
            ls, rs = left_at(s), right_at(s)

            def step(q, total):
                for u in range(4):
                    at = pl.multiple_of((q * 4 + u) * t, 8)
                    row = rights[rs, pl.ds(at, t), :]
                    total = tuple(total[i] + lefts[ls, pl.ds(at + base + i, 1), :] * row for i in range(8))
                return total

            return lax.fori_loop(0, t // 4, step, total)

        total = lax.fori_loop(first, last, slot, total)
        for i in range(8):
            out_ref[pl.ds((base + i) * t, t), :] = total[i]


def finish(pair, mixed, gating, consts, gain, shift, weights, bias):
    normout = norm_mixed(mixed, consts, gain, shift)
    return (pair.astype(F32) + gating * (dot(normout, weights) + bias)).astype(BF16)


TABLE_MASK = 24


def in_norm(table, u):
    return table[u : u + 1], table[2 + u : 3 + u]


def out_norm(table, u):
    return table[4 + u : 5 + u], table[6 + u : 7 + u]


def half_bias(table, u, first, last):
    return jnp.concatenate([table[k : k + 1] for k in range(10 + 5 * u + first, 10 + 5 * u + last)], axis=1) * 0.5


def mask_of(table, b, t):
    return table[pl.ds(pl.multiple_of(TABLE_MASK + b * t, 8), t), :]


def sides(values_ref, wide, left_at, right_at, outer, inner, consts, table, weights):
    t, width = outer.shape
    wide[...] = values_ref[...].astype(F32)
    values = jnp.concatenate([wide[pl.ds(k, t, stride=t), :] for k in range(t)], axis=0).astype(BF16)
    normed = norm_pair(values, consts, *in_norm(table, 0))
    for k, target in enumerate((left_at, right_at)):
        span = slice(2 * k * width, 2 * (k + 1) * width)
        side = gated(normed, weights[0, :, span], half_bias(table, 0, 2 * k, 2 * k + 2), width)
        target[...] = masked(side, outer, inner).astype(F32)


def gate_of(values, consts, table, weights, u):
    normed = norm_pair(values, consts, *in_norm(table, u))
    return gate(normed, weights[u, :, 4 * values.shape[1] :], half_bias(table, u, 4, 5))


def place(b, n):
    return b // 2 + lax.rem(b, 2) * (n // 2)


def placed_at(r, n):
    return lax.rem(r, n // 2) * 2 + r // (n // 2)


def own_kernel(t, pair, table, w_in, weights, row_l, row_r, gating, wide):
    r, c = lax.axis_index("row"), lax.axis_index("col")
    consts = constants(wide.shape[1])
    weights[...] = w_in[...] * 0.5
    outer, inner = mask_of(table, c, t), mask_of(table, r, t)
    sides(pair, wide, row_l.at[0], row_r.at[0], outer, inner, consts, table, weights)
    gating[...] = gate_of(pair[...], consts, table, weights, 0)


def rows_kernel(t, count, *refs):
    blocks, (col_block, table, weights) = refs[:count], refs[count : count + 3]
    row_l, row_r, col_l, col_r, wide = refs[count + 5 :]
    r, c = lax.axis_index("row"), lax.axis_index("col")
    consts = constants(wide.shape[1])
    here, there = mask_of(table, r, t), mask_of(table, c, t)
    outer = mask_of(table, placed_at(r, count + 2), t)
    sides(col_block, wide, col_l.at[0], col_r.at[0], outer, there, consts, table, weights)
    for s, block in enumerate(blocks, 1):
        outer = mask_of(table, c ^ s, t)
        sides(block, wide, row_l.at[s], row_r.at[s], outer, here, consts, table, weights)


def columns_kernel(t, count, *refs):
    blocks, (table, weights) = refs[:count], refs[count : count + 2]
    col_l, col_r, wide = refs[count + 4 :]
    r, c = lax.axis_index("row"), lax.axis_index("col")
    consts = constants(wide.shape[1])
    for s, block in enumerate(blocks, 1):
        outer, inner = mask_of(table, placed_at(r ^ s, count + 2), t), mask_of(table, c, t)
        sides(block, wide, col_l.at[s], col_r.at[s], outer, inner, consts, table, weights)


def mirror_kernel(n, t, *refs):
    row, cols, (table, weights, w_out) = refs[0], refs[1 : n + 1], refs[n + 1 : n + 4]
    left_ref, row_l, row_r, col_l, col_r, mixed, wide, held = refs[n + 8 :]
    width = wide.shape[1]
    r, c = lax.axis_index("row"), lax.axis_index("col")
    consts = constants(width)
    here, there = mask_of(table, r, t), mask_of(table, c, t)
    for block, left, right, outer, inner in (
        (row, row_l, row_r, c ^ (n - 1), here),
        (cols[-1], col_l, col_r, placed_at(r ^ (n - 1), n), there),
    ):
        outer = mask_of(table, outer, t)
        sides(block, wide, left.at[n - 1], right.at[n - 1], outer, inner, consts, table, weights)
    mix(mixed, None, col_l, row_r, 0, n, lambda s: r ^ place(c ^ s, n), lambda s: s, t)
    for s in range(n):
        held[s] = cols[s][...]
    pair = held[r ^ place(r, n)]
    updated = finish(pair, mixed[...], gate_of(pair, consts, table, weights, 0), consts, *out_norm(table, 0), w_out[0], table[8:9])
    normed = norm_pair(updated, consts, *in_norm(table, 1))
    side = gated(normed, weights[1, :, : 2 * width], half_bias(table, 1, 0, 2), width)
    left_ref[...] = masked(side, there, here)


def own_end_kernel(n, t, row_l, col_r, table, weights, pair, gating, w_out, pair_ref, right_ref, mixed):
    width = mixed.shape[1]
    r, c = lax.axis_index("row"), lax.axis_index("col")
    consts = constants(width)
    mix(mixed, None, row_l, col_r, 0, n, lambda s: s, lambda s: r ^ place(c ^ s, n), t)
    updated = finish(pair[...], mixed[...], gating[...], consts, *out_norm(table, 0), w_out[0], table[8:9])
    pair_ref[...] = updated
    normed = norm_pair(updated, consts, *in_norm(table, 1))
    side = gated(normed, weights[1, :, 2 * width : 4 * width], half_bias(table, 1, 2, 4), width)
    right_ref[...] = masked(side, mask_of(table, r, t), mask_of(table, c, t))


def gate_kernel(pair, table, weights, gating):
    gating[...] = gate_of(pair[...], constants(pair.shape[1]), table, weights, 1)


def middle_kernel(n, t, *refs):
    blocks, sources = refs[: n - 1], refs[n - 1 : 2 * n - 1]
    rights, mixed, lefts = refs[2 * n - 1 :]
    r, c = lax.axis_index("row"), lax.axis_index("col")
    for s in range(n - 1):
        lefts[s] = blocks[s][...].astype(F32)
    for s in range(n):
        rights[s] = sources[s][...].astype(F32)
    mix(mixed, None, lefts, rights, 0, n - 1, lambda s: s, lambda s: r ^ c ^ s, t)


def end_kernel(n, t, block, rights, old, pair, gating, table, w_out, out, mixed, left):
    r, c = lax.axis_index("row"), lax.axis_index("col")
    left[0] = block[...].astype(F32)
    mix(mixed, old, left, rights, 0, 1, lambda s: s, lambda s: r ^ c ^ (n - 1), t)
    consts = constants(mixed.shape[1])
    out[...] = finish(pair[...], mixed[...], gating[...], consts, *out_norm(table, 1), w_out[1], table[9:10])


def solution(mesh):
    n = mesh.shape["col"]

    def gather(block, axis, after=lambda block: block):
        held, step = {0: block}, n // 2
        while step:
            for s, part in list(held.items()):
                part = after(part) if s else part
                held[s ^ step] = lax.ppermute(part, axis, [(k, k ^ step) for k in range(n)])
            step //= 2
        return [held[s] for s in range(n)]

    def mirrored(block):
        pairs = [(a * n + z, (z // 2 + z % 2 * (n // 2)) * n + a) for a in range(n) for z in range(n)]
        return lax.ppermute(block, ("row", "col"), pairs)

    def per_device(pair, token_mask, in_gain, in_shift, w_in, bias_in, out_gain, out_shift, w_out, bias_out):
        t, _, width = pair.shape
        area = (t * t, width)
        narrow, broad = jax.ShapeDtypeStruct(area, BF16), jax.ShapeDtypeStruct(area, F32)
        slots = jax.ShapeDtypeStruct((n,) + area, F32)
        scratch = pltpu.VMEM(area, F32)

        def call(kernel, name, outs, scratches, *operands, alias=None, **specs):
            return pl.pallas_call(
                kernel,
                out_shape=outs,
                scratch_shapes=scratches,
                input_output_aliases=alias or {},

                compiler_params=pltpu.CompilerParams(vmem_limit_bytes=(16 + n) * 1024 * 1024),
                name=name,
            )(*operands)

        pair = pair.reshape(area)
        col_block = mirrored(pair)
        mask = jnp.broadcast_to(token_mask.astype(F32)[:, None], (n * t, width))
        vectors = [in_gain, in_shift, out_gain, out_shift, bias_out, bias_in.reshape(-1, width)]
        table = jnp.concatenate(vectors + [jnp.zeros((TABLE_MASK - 20, width), F32), mask])
        weights, row_l, row_r, gating = call(
            functools.partial(own_kernel, t),
            "own_sides",
            (jax.ShapeDtypeStruct(w_in.shape, BF16), slots, slots, broad),
            [scratch],
            pair,
            table,
            w_in,
        )
        own_l = row_l
        rows = gather(pair, "col", lambda block: lax.optimization_barrier((block, own_l))[0])
        row_l, row_r, col_l, col_r = call(
            functools.partial(rows_kernel, t, n - 2),
            "row_sides",
            (slots,) * 4,
            [scratch],
            *rows[1:-1],
            col_block,
            table,
            weights,
            row_l,
            row_r,
            alias={n + 1: 0, n + 2: 1},
        )
        ready = lax.optimization_barrier((col_block, rows[1], rows[n // 2], own_l))[0]
        cols = gather(ready, "row", lambda block: lax.optimization_barrier((block, row_l))[0])
        col_l, col_r = call(
            functools.partial(columns_kernel, t, n - 2),
            "column_sides",
            (slots, slots),
            [scratch],
            *cols[1:-1],
            table,
            weights,
            col_l,
            col_r,
            alias={n: 0, n + 1: 1},
        )
        left, row_l, _, _, col_r = call(
            functools.partial(mirror_kernel, n, t),
            "mirror_end",
            (narrow, slots, slots, slots, slots),
            [scratch] * 2 + [pltpu.VMEM((n,) + area, BF16)],
            rows[-1],
            *cols,
            table,
            weights,
            w_out,
            row_l,
            row_r,
            col_l,
            col_r,
            alias={n + 4: 1, n + 5: 2, n + 6: 3, n + 7: 4},
        )
        pair, right = call(
            functools.partial(own_end_kernel, n, t),
            "own_end",
            (narrow, narrow),
            [scratch],
            row_l,
            col_r,
            table,
            weights,
            pair,
            gating,
            w_out,
        )
        lefts = gather(left, "col")
        rights = [right] + [lax.ppermute(right, "row", [(k, k ^ s) for k in range(n)]) for s in range(1, n)]
        gating = call(gate_kernel, "gate", broad, [], pair, table, weights)
        rights, mixed = call(
            functools.partial(middle_kernel, n, t),
            "middle_slots",
            (slots, broad),
            [pltpu.VMEM((n - 1,) + area, F32)],
            *lefts[:-1],
            *rights,
        )
        out = call(
            functools.partial(end_kernel, n, t),
            "end",
            narrow,
            [scratch, pltpu.VMEM((1,) + area, F32)],
            lefts[-1],
            rights,
            mixed,
            pair,
            gating,
            table,
            w_out,
        )
        return out.reshape(t, t, width)

    placed = (P(("groups", "row"), "col", None), P("groups")) + (P(),) * 8
    return jax.shard_map(
        per_device, mesh=mesh, in_specs=placed, out_specs=P(("groups", "row"), "col", None), check_vma=False
    )
```

```python
import functools

import jax
import jax.numpy as jnp
from jax import lax
from jax.experimental import pallas as pl
from jax.experimental.pallas import tpu as pltpu
from jax.sharding import PartitionSpec as P

F32, BF16 = jnp.float32, jnp.bfloat16


def dot(a, b):
    return jnp.dot(a, b, preferred_element_type=F32)


def split(values):
    high = values.astype(BF16)
    return jnp.concatenate([high, (values - high.astype(F32)).astype(BF16)], axis=1)


def constants(width):
    rows = lax.broadcasted_iota(jnp.int32, (2 * width, width), 0)
    cols = lax.broadcasted_iota(jnp.int32, (2 * width, width), 1)
    mean = jnp.full((2 * width, width), 1.0 / width, F32)
    center = jnp.where((rows == cols) | (rows == cols + width), 1.0, 0.0) - mean
    return center.astype(BF16), mean.astype(BF16)


def scaled(center, mean, gain, shift):
    spread = dot(split(center * center), mean)
    return (center * lax.rsqrt(spread + 1e-05) * gain + shift).astype(BF16)


def norm_pair(values, consts, gain, shift):
    return scaled(dot(values, consts[0][: values.shape[1]]), consts[1], gain, shift)


def norm_mixed(values, consts, gain, shift):
    return scaled(dot(split(values), consts[0]), consts[1], gain, shift)


def gated(normed, weights, bias, width):
    product = dot(normed, weights) + bias
    return (jnp.tanh(product[:, width:]) + 1.0) * product[:, :width]


def gate(normed, weights, bias):
    return 0.5 * jnp.tanh(dot(normed, weights) + bias) + 0.5


def masked(values, outer, inner):
    t = outer.shape[0]
    grid = jnp.concatenate([outer[k : k + 1] * inner for k in range(t)], axis=0)
    return (values * grid).astype(BF16)


def mix(out_ref, old_ref, lefts, rights, first, last, left_at, right_at, t):
    width = out_ref.shape[1]
    for base in range(0, t, 8):
        if old_ref is None:
            total = (jnp.zeros((t, width), F32),) * 8
        else:
            total = tuple(old_ref[pl.ds((base + i) * t, t), :] for i in range(8))

        def slot(s, total):
            ls, rs = left_at(s), right_at(s)

            def step(q, total):
                for u in range(4):
                    at = pl.multiple_of((q * 4 + u) * t, 8)
                    row = rights[rs, pl.ds(at, t), :]
                    total = tuple(total[i] + lefts[ls, pl.ds(at + base + i, 1), :] * row for i in range(8))
                return total

            return lax.fori_loop(0, t // 4, step, total)

        total = lax.fori_loop(first, last, slot, total)
        for i in range(8):
            out_ref[pl.ds((base + i) * t, t), :] = total[i]


def finish(pair, mixed, gating, consts, gain, shift, weights, bias):
    normout = norm_mixed(mixed, consts, gain, shift)
    return (pair.astype(F32) + gating * (dot(normout, weights) + bias)).astype(BF16)


TABLE_MASK = 24


def in_norm(table, u):
    return table[u : u + 1], table[2 + u : 3 + u]


def out_norm(table, u):
    return table[4 + u : 5 + u], table[6 + u : 7 + u]


def half_bias(table, u, first, last):
    return jnp.concatenate([table[k : k + 1] for k in range(10 + 5 * u + first, 10 + 5 * u + last)], axis=1) * 0.5


def mask_of(table, b, t):
    return table[pl.ds(pl.multiple_of(TABLE_MASK + b * t, 8), t), :]


def sides(values_ref, wide, left_at, right_at, outer, inner, consts, table, weights):
    t, width = outer.shape
    wide[...] = values_ref[...].astype(F32)
    values = jnp.concatenate([wide[pl.ds(k, t, stride=t), :] for k in range(t)], axis=0).astype(BF16)
    normed = norm_pair(values, consts, *in_norm(table, 0))
    for k, target in enumerate((left_at, right_at)):
        span = slice(2 * k * width, 2 * (k + 1) * width)
        side = gated(normed, weights[0, :, span], half_bias(table, 0, 2 * k, 2 * k + 2), width)
        target[...] = masked(side, outer, inner).astype(F32)


def gate_of(values, consts, table, weights, u):
    normed = norm_pair(values, consts, *in_norm(table, u))
    return gate(normed, weights[u, :, 4 * values.shape[1] :], half_bias(table, u, 4, 5))


def place(b, n):
    return b // 2 + lax.rem(b, 2) * (n // 2)


def placed_at(r, n):
    return lax.rem(r, n // 2) * 2 + r // (n // 2)


def own_kernel(t, pair, table, w_in, weights, row_l, row_r, gating, wide):
    r, c = lax.axis_index("row"), lax.axis_index("col")
    consts = constants(wide.shape[1])
    weights[...] = w_in[...] * 0.5
    outer, inner = mask_of(table, c, t), mask_of(table, r, t)
    sides(pair, wide, row_l.at[0], row_r.at[0], outer, inner, consts, table, weights)
    gating[...] = gate_of(pair[...], consts, table, weights, 0)


def rows_kernel(t, count, *refs):
    blocks, (col_block, table, weights) = refs[:count], refs[count : count + 3]
    row_l, row_r, col_l, col_r, wide = refs[count + 5 :]
    r, c = lax.axis_index("row"), lax.axis_index("col")
    consts = constants(wide.shape[1])
    here, there = mask_of(table, r, t), mask_of(table, c, t)
    outer = mask_of(table, placed_at(r, count + 2), t)
    sides(col_block, wide, col_l.at[0], col_r.at[0], outer, there, consts, table, weights)
    for s, block in enumerate(blocks, 1):
        outer = mask_of(table, c ^ s, t)
        sides(block, wide, row_l.at[s], row_r.at[s], outer, here, consts, table, weights)


def columns_kernel(t, count, *refs):
    blocks, (table, weights) = refs[:count], refs[count : count + 2]
    col_l, col_r, wide = refs[count + 4 :]
    r, c = lax.axis_index("row"), lax.axis_index("col")
    consts = constants(wide.shape[1])
    for s, block in enumerate(blocks, 1):
        outer, inner = mask_of(table, placed_at(r ^ s, count + 2), t), mask_of(table, c, t)
        sides(block, wide, col_l.at[s], col_r.at[s], outer, inner, consts, table, weights)


def mirror_kernel(n, t, *refs):
    row, cols, (table, weights, w_out) = refs[0], refs[1 : n + 1], refs[n + 1 : n + 4]
    left_ref, row_l, row_r, col_l, col_r, mixed, wide, held = refs[n + 8 :]
    width = wide.shape[1]
    r, c = lax.axis_index("row"), lax.axis_index("col")
    consts = constants(width)
    here, there = mask_of(table, r, t), mask_of(table, c, t)
    for block, left, right, outer, inner in (
        (row, row_l, row_r, c ^ (n - 1), here),
        (cols[-1], col_l, col_r, placed_at(r ^ (n - 1), n), there),
    ):
        outer = mask_of(table, outer, t)
        sides(block, wide, left.at[n - 1], right.at[n - 1], outer, inner, consts, table, weights)
    mix(mixed, None, col_l, row_r, 0, n, lambda s: r ^ place(c ^ s, n), lambda s: s, t)
    for s in range(n):
        held[s] = cols[s][...]
    pair = held[r ^ place(r, n)]
    updated = finish(pair, mixed[...], gate_of(pair, consts, table, weights, 0), consts, *out_norm(table, 0), w_out[0], table[8:9])
    normed = norm_pair(updated, consts, *in_norm(table, 1))
    side = gated(normed, weights[1, :, : 2 * width], half_bias(table, 1, 0, 2), width)
    left_ref[...] = masked(side, there, here)


def own_end_kernel(n, t, row_l, col_r, table, weights, pair, gating, w_out, pair_ref, right_ref, mixed):
    width = mixed.shape[1]
    r, c = lax.axis_index("row"), lax.axis_index("col")
    consts = constants(width)
    mix(mixed, None, row_l, col_r, 0, n, lambda s: s, lambda s: r ^ place(c ^ s, n), t)
    updated = finish(pair[...], mixed[...], gating[...], consts, *out_norm(table, 0), w_out[0], table[8:9])
    pair_ref[...] = updated
    normed = norm_pair(updated, consts, *in_norm(table, 1))
    side = gated(normed, weights[1, :, 2 * width : 4 * width], half_bias(table, 1, 2, 4), width)
    right_ref[...] = masked(side, mask_of(table, r, t), mask_of(table, c, t))


def gate_kernel(pair, table, weights, gating):
    gating[...] = gate_of(pair[...], constants(pair.shape[1]), table, weights, 1)


def middle_kernel(n, t, *refs):
    blocks, sources = refs[: n - 1], refs[n - 1 : 2 * n - 1]
    rights, mixed, lefts = refs[2 * n - 1 :]
    r, c = lax.axis_index("row"), lax.axis_index("col")
    for s in range(n - 1):
        lefts[s] = blocks[s][...].astype(F32)
    for s in range(n):
        rights[s] = sources[s][...].astype(F32)
    mix(mixed, None, lefts, rights, 0, n - 1, lambda s: s, lambda s: r ^ c ^ s, t)


def end_kernel(n, t, block, rights, old, pair, gating, table, w_out, out, mixed, left):
    r, c = lax.axis_index("row"), lax.axis_index("col")
    left[0] = block[...].astype(F32)
    mix(mixed, old, left, rights, 0, 1, lambda s: s, lambda s: r ^ c ^ (n - 1), t)
    consts = constants(mixed.shape[1])
    out[...] = finish(pair[...], mixed[...], gating[...], consts, *out_norm(table, 1), w_out[1], table[9:10])


def solution(mesh):
    n = mesh.shape["col"]

    def gather(block, axis, after=lambda block: block):
        held, step = {0: block}, n // 2
        while step:
            for s, part in list(held.items()):
                part = after(part) if s else part
                held[s ^ step] = lax.ppermute(part, axis, [(k, k ^ step) for k in range(n)])
            step //= 2
        return [held[s] for s in range(n)]

    def direct(block, near):
        return [block] + [
            lax.ppermute(near if s == 1 else block, "row", [(k, k ^ s) for k in range(n)]) for s in range(1, n)
        ]

    def mirrored(block):
        pairs = [(a * n + z, (z // 2 + z % 2 * (n // 2)) * n + a) for a in range(n) for z in range(n)]
        return lax.ppermute(block, ("row", "col"), pairs)

    def per_device(pair, token_mask, in_gain, in_shift, w_in, bias_in, out_gain, out_shift, w_out, bias_out):
        t, _, width = pair.shape
        area = (t * t, width)
        narrow, broad = jax.ShapeDtypeStruct(area, BF16), jax.ShapeDtypeStruct(area, F32)
        slots = jax.ShapeDtypeStruct((n,) + area, F32)
        scratch = pltpu.VMEM(area, F32)

        def call(kernel, name, outs, scratches, *operands, alias=None, **specs):
            return pl.pallas_call(
                kernel,
                out_shape=outs,
                scratch_shapes=scratches,
                input_output_aliases=alias or {},

                compiler_params=pltpu.CompilerParams(vmem_limit_bytes=(16 + n) * 1024 * 1024),
                name=name,
            )(*operands)

        pair = pair.reshape(area)
        col_block = mirrored(pair)
        mask = jnp.broadcast_to(token_mask.astype(F32)[:, None], (n * t, width))
        vectors = [in_gain, in_shift, out_gain, out_shift, bias_out, bias_in.reshape(-1, width)]
        table = jnp.concatenate(vectors + [jnp.zeros((TABLE_MASK - 20, width), F32), mask])
        weights, row_l, row_r, gating = call(
            functools.partial(own_kernel, t),
            "own_sides",
            (jax.ShapeDtypeStruct(w_in.shape, BF16), slots, slots, broad),
            [scratch],
            pair,
            table,
            w_in,
        )
        own_l = row_l
        rows = gather(pair, "col", lambda block: lax.optimization_barrier((block, own_l))[0])
        row_l, row_r, col_l, col_r = call(
            functools.partial(rows_kernel, t, n - 2),
            "row_sides",
            (slots,) * 4,
            [scratch],
            *rows[1:-1],
            col_block,
            table,
            weights,
            row_l,
            row_r,
            alias={n + 1: 0, n + 2: 1},
        )
        ready = lax.optimization_barrier((col_block, own_l))[0]
        cols = direct(ready, ready)
        col_l, col_r = call(
            functools.partial(columns_kernel, t, n - 2),
            "column_sides",
            (slots, slots),
            [scratch],
            *cols[1:-1],
            table,
            weights,
            col_l,
            col_r,
            alias={n: 0, n + 1: 1},
        )
        left, row_l, _, _, col_r = call(
            functools.partial(mirror_kernel, n, t),
            "mirror_end",
            (narrow, slots, slots, slots, slots),
            [scratch] * 2 + [pltpu.VMEM((n,) + area, BF16)],
            rows[-1],
            *cols,
            table,
            weights,
            w_out,
            row_l,
            row_r,
            col_l,
            col_r,
            alias={n + 4: 1, n + 5: 2, n + 6: 3, n + 7: 4},
        )
        pair, right = call(
            functools.partial(own_end_kernel, n, t),
            "own_end",
            (narrow, narrow),
            [scratch],
            row_l,
            col_r,
            table,
            weights,
            pair,
            gating,
            w_out,
        )
        lefts = gather(left, "col")
        near = lax.optimization_barrier((right, lefts[1]))[0]
        rights = direct(right, lax.optimization_barrier((right, lefts[1]))[0])
        gating = call(gate_kernel, "gate", broad, [], pair, table, weights)
        rights, mixed = call(
            functools.partial(middle_kernel, n, t),
            "middle_slots",
            (slots, broad),
            [pltpu.VMEM((n - 1,) + area, F32)],
            *lefts[:-1],
            *rights,
        )
        out = call(
            functools.partial(end_kernel, n, t),
            "end",
            narrow,
            [scratch, pltpu.VMEM((1,) + area, F32)],
            lefts[-1],
            rights,
            mixed,
            pair,
            gating,
            table,
            w_out,
        )
        return out.reshape(t, t, width)

    placed = (P(("groups", "row"), "col", None), P("groups")) + (P(),) * 8
    return jax.shard_map(
        per_device, mesh=mesh, in_specs=placed, out_specs=P(("groups", "row"), "col", None), check_vma=False
    )
```

```python
import functools

import jax
import jax.numpy as jnp
from jax import lax
from jax.experimental import pallas as pl
from jax.experimental.pallas import tpu as pltpu
from jax.sharding import PartitionSpec as P

F32, BF16 = jnp.float32, jnp.bfloat16


def dot(a, b):
    return jnp.dot(a, b, preferred_element_type=F32)


def split(values):
    high = values.astype(BF16)
    return jnp.concatenate([high, (values - high.astype(F32)).astype(BF16)], axis=1)


def constants(width):
    rows = lax.broadcasted_iota(jnp.int32, (2 * width, width), 0)
    cols = lax.broadcasted_iota(jnp.int32, (2 * width, width), 1)
    mean = jnp.full((2 * width, width), 1.0 / width, F32)
    center = jnp.where((rows == cols) | (rows == cols + width), 1.0, 0.0) - mean
    return center.astype(BF16), mean.astype(BF16)


def scaled(center, mean, gain, shift):
    spread = dot(split(center * center), mean)
    return (center * lax.rsqrt(spread + 1e-05) * gain + shift).astype(BF16)


def norm_pair(values, consts, gain, shift):
    return scaled(dot(values, consts[0][: values.shape[1]]), consts[1], gain, shift)


def norm_mixed(values, consts, gain, shift):
    return scaled(dot(split(values), consts[0]), consts[1], gain, shift)


def gated(normed, weights, bias, width):
    product = dot(normed, weights) + bias
    return (jnp.tanh(product[:, width:]) + 1.0) * product[:, :width]


def gate(normed, weights, bias):
    return 0.5 * jnp.tanh(dot(normed, weights) + bias) + 0.5


def masked(values, outer, inner):
    t = outer.shape[0]
    grid = jnp.concatenate([outer[k : k + 1] * inner for k in range(t)], axis=0)
    return (values * grid).astype(BF16)


def mix(out_ref, old_ref, lefts, rights, first, last, left_at, right_at, t):
    width = out_ref.shape[1]
    for base in range(0, t, 8):
        if old_ref is None:
            total = (jnp.zeros((t, width), F32),) * 8
        else:
            total = tuple(old_ref[pl.ds((base + i) * t, t), :] for i in range(8))

        def slot(s, total):
            ls, rs = left_at(s), right_at(s)

            def step(q, total):
                for u in range(4):
                    at = pl.multiple_of((q * 4 + u) * t, 8)
                    row = rights[rs, pl.ds(at, t), :]
                    total = tuple(total[i] + lefts[ls, pl.ds(at + base + i, 1), :] * row for i in range(8))
                return total

            return lax.fori_loop(0, t // 4, step, total)

        total = lax.fori_loop(first, last, slot, total)
        for i in range(8):
            out_ref[pl.ds((base + i) * t, t), :] = total[i]


def finish(pair, mixed, gating, consts, gain, shift, weights, bias):
    normout = norm_mixed(mixed, consts, gain, shift)
    return (pair.astype(F32) + gating * (dot(normout, weights) + bias)).astype(BF16)


TABLE_MASK = 24


def in_norm(table, u):
    return table[u : u + 1], table[2 + u : 3 + u]


def out_norm(table, u):
    return table[4 + u : 5 + u], table[6 + u : 7 + u]


def half_bias(table, u, first, last):
    return jnp.concatenate([table[k : k + 1] for k in range(10 + 5 * u + first, 10 + 5 * u + last)], axis=1) * 0.5


def mask_of(table, b, t):
    return table[pl.ds(pl.multiple_of(TABLE_MASK + b * t, 8), t), :]


def sides(values_ref, wide, left_at, right_at, outer, inner, consts, table, weights):
    t, width = outer.shape
    wide[...] = values_ref[...].astype(F32)
    values = jnp.concatenate([wide[pl.ds(k, t, stride=t), :] for k in range(t)], axis=0).astype(BF16)
    normed = norm_pair(values, consts, *in_norm(table, 0))
    for k, target in enumerate((left_at, right_at)):
        span = slice(2 * k * width, 2 * (k + 1) * width)
        side = gated(normed, weights[0, :, span], half_bias(table, 0, 2 * k, 2 * k + 2), width)
        target[...] = masked(side, outer, inner).astype(F32)


def gate_of(values, consts, table, weights, u):
    normed = norm_pair(values, consts, *in_norm(table, u))
    return gate(normed, weights[u, :, 4 * values.shape[1] :], half_bias(table, u, 4, 5))


def place(b, n):
    return b // 2 + lax.rem(b, 2) * (n // 2)


def placed_at(r, n):
    return lax.rem(r, n // 2) * 2 + r // (n // 2)


def early_pairs(late, n):
    return jnp.where(late == n - 1, n - 1, n - 2), lambda i: i + jnp.where(i >= late, 1, 0)


def late_pairs(late, n):
    return jnp.where(late == n - 1, 1, 2), lambda i: jnp.where(i == 0, n - 1, late)


def own_kernel(t, pair, table, w_in, weights, row_l, row_r, gating, wide):
    r, c = lax.axis_index("row"), lax.axis_index("col")
    consts = constants(wide.shape[1])
    weights[...] = w_in[...] * 0.5
    outer, inner = mask_of(table, c, t), mask_of(table, r, t)
    sides(pair, wide, row_l.at[0], row_r.at[0], outer, inner, consts, table, weights)
    gating[...] = gate_of(pair[...], consts, table, weights, 0)


def rows_kernel(t, count, *refs):
    blocks, (col_block, table, weights) = refs[:count], refs[count : count + 3]
    row_l, row_r, col_l, col_r, wide = refs[count + 5 :]
    r, c = lax.axis_index("row"), lax.axis_index("col")
    consts = constants(wide.shape[1])
    here, there = mask_of(table, r, t), mask_of(table, c, t)
    outer = mask_of(table, placed_at(r, count + 2), t)
    sides(col_block, wide, col_l.at[0], col_r.at[0], outer, there, consts, table, weights)
    for s, block in enumerate(blocks, 1):
        outer = mask_of(table, c ^ s, t)
        sides(block, wide, row_l.at[s], row_r.at[s], outer, here, consts, table, weights)


def columns_kernel(n, t, *refs):
    blocks, (table, weights, row_r) = refs[: n - 2], refs[n - 2 : n + 1]
    col_l, col_r, mixed, wide = refs[n + 3 :]
    r, c = lax.axis_index("row"), lax.axis_index("col")
    consts = constants(wide.shape[1])
    for s, block in enumerate(blocks, 1):
        outer, inner = mask_of(table, placed_at(r ^ s, n), t), mask_of(table, c, t)
        sides(block, wide, col_l.at[s], col_r.at[s], outer, inner, consts, table, weights)
    count, slot = early_pairs(c ^ placed_at(r ^ (n - 1), n), n)
    mix(mixed, None, col_l, row_r, 0, count, lambda i: r ^ place(c ^ slot(i), n), slot, t)


def mirror_kernel(n, t, *refs):
    row, cols, (table, weights, w_out) = refs[0], refs[1 : n + 1], refs[n + 1 : n + 4]
    old = refs[n + 8]
    left_ref, row_l, row_r, col_l, col_r, mixed, wide, held = refs[n + 9 :]
    width = wide.shape[1]
    r, c = lax.axis_index("row"), lax.axis_index("col")
    consts = constants(width)
    here, there = mask_of(table, r, t), mask_of(table, c, t)
    for block, left, right, outer, inner in (
        (row, row_l, row_r, c ^ (n - 1), here),
        (cols[-1], col_l, col_r, placed_at(r ^ (n - 1), n), there),
    ):
        outer = mask_of(table, outer, t)
        sides(block, wide, left.at[n - 1], right.at[n - 1], outer, inner, consts, table, weights)
    count, slot = late_pairs(c ^ placed_at(r ^ (n - 1), n), n)
    mix(mixed, old, col_l, row_r, 0, count, lambda i: r ^ place(c ^ slot(i), n), slot, t)
    for s in range(n):
        held[s] = cols[s][...]
    pair = held[r ^ place(r, n)]
    updated = finish(pair, mixed[...], gate_of(pair, consts, table, weights, 0), consts, *out_norm(table, 0), w_out[0], table[8:9])
    normed = norm_pair(updated, consts, *in_norm(table, 1))
    side = gated(normed, weights[1, :, : 2 * width], half_bias(table, 1, 0, 2), width)
    left_ref[...] = masked(side, there, here)


def own_end_kernel(n, t, row_l, col_r, table, weights, pair, gating, w_out, pair_ref, right_ref, mixed):
    width = mixed.shape[1]
    r, c = lax.axis_index("row"), lax.axis_index("col")
    consts = constants(width)
    mix(mixed, None, row_l, col_r, 0, n, lambda s: s, lambda s: r ^ place(c ^ s, n), t)
    updated = finish(pair[...], mixed[...], gating[...], consts, *out_norm(table, 0), w_out[0], table[8:9])
    pair_ref[...] = updated
    normed = norm_pair(updated, consts, *in_norm(table, 1))
    side = gated(normed, weights[1, :, 2 * width : 4 * width], half_bias(table, 1, 2, 4), width)
    right_ref[...] = masked(side, mask_of(table, r, t), mask_of(table, c, t))


def gate_kernel(pair, table, weights, gating):
    gating[...] = gate_of(pair[...], constants(pair.shape[1]), table, weights, 1)


def left_kernel(n, *refs):
    for s in range(n - 1):
        refs[n - 1][s] = refs[s][...].astype(F32)


def middle_kernel(n, t, *refs):
    sources, (lefts, rights, mixed) = refs[: n - 1], refs[n - 1 :]
    r, c = lax.axis_index("row"), lax.axis_index("col")
    for s in range(n - 1):
        rights[s] = sources[s][...].astype(F32)
    count, slot = early_pairs(r ^ c ^ (n - 1), n)
    mix(mixed, None, lefts, rights, 0, count, slot, lambda i: r ^ c ^ slot(i), t)


def end_kernel(n, t, left, right, old, pair, gating, table, w_out, left_in, right_in, out, lefts, rights, mixed):
    r, c = lax.axis_index("row"), lax.axis_index("col")
    lefts[n - 1] = left[...].astype(F32)
    rights[n - 1] = right[...].astype(F32)
    count, slot = late_pairs(r ^ c ^ (n - 1), n)
    mix(mixed, old, lefts, rights, 0, count, slot, lambda i: r ^ c ^ slot(i), t)
    consts = constants(mixed.shape[1])
    out[...] = finish(pair[...], mixed[...], gating[...], consts, *out_norm(table, 1), w_out[1], table[9:10])


def solution(mesh):
    n = mesh.shape["col"]

    def gather(block, axis, after):
        held, step = {0: block}, n // 2
        while step:
            for s, part in list(held.items()):
                part = lax.optimization_barrier((part, after(s, step)))[0]
                held[s ^ step] = lax.ppermute(part, axis, [(k, k ^ step) for k in range(n)])
            step //= 2
        return [held[s] for s in range(n)]

    def direct(block):
        return [block] + [lax.ppermute(block, "row", [(k, k ^ s) for k in range(n)]) for s in range(1, n)]

    def mirrored(block):
        pairs = [(a * n + z, (z // 2 + z % 2 * (n // 2)) * n + a) for a in range(n) for z in range(n)]
        return lax.ppermute(block, ("row", "col"), pairs)

    def per_device(pair, token_mask, in_gain, in_shift, w_in, bias_in, out_gain, out_shift, w_out, bias_out):
        t, _, width = pair.shape
        area = (t * t, width)
        narrow, broad = jax.ShapeDtypeStruct(area, BF16), jax.ShapeDtypeStruct(area, F32)
        slots = jax.ShapeDtypeStruct((n,) + area, F32)
        scratch = pltpu.VMEM(area, F32)

        def call(kernel, name, outs, scratches, *operands, alias=None, weight=0):
            return pl.pallas_call(
                kernel,
                out_shape=outs,
                scratch_shapes=scratches,
                input_output_aliases=alias or {},
                cost_estimate=pl.CostEstimate(
                    flops=weight * 10**9, bytes_accessed=weight * 10**6, transcendentals=0
                ) if weight else None,

                compiler_params=pltpu.CompilerParams(vmem_limit_bytes=(16 + n) * 1024 * 1024),
                name=name,
            )(*operands)

        pair = pair.reshape(area)
        col_block = mirrored(pair)
        mask = jnp.broadcast_to(token_mask.astype(F32)[:, None], (n * t, width))
        vectors = [in_gain, in_shift, out_gain, out_shift, bias_out, bias_in.reshape(-1, width)]
        table = jnp.concatenate(vectors + [jnp.zeros((TABLE_MASK - 20, width), F32), mask])
        weights, row_l, row_r, gating = call(
            functools.partial(own_kernel, t),
            "own_sides",
            (jax.ShapeDtypeStruct(w_in.shape, BF16), slots, slots, broad),
            [scratch],
            pair,
            table,
            w_in,
        )
        own_l = row_l
        rows = gather(pair, "col", lambda s, step: own_l if s else ())
        row_l, row_r, col_l, col_r = call(
            functools.partial(rows_kernel, t, n - 2),
            "row_sides",
            (slots,) * 4,
            [scratch],
            *rows[1:-1],
            col_block,
            table,
            weights,
            row_l,
            row_r,
            alias={n + 1: 0, n + 2: 1},
        )
        cols = direct(lax.optimization_barrier((col_block, own_l))[0])
        col_l, col_r, mixed = call(
            functools.partial(columns_kernel, n, t),
            "column_sides",
            (slots, slots, broad),
            [scratch],
            *cols[1:-1],
            table,
            weights,
            row_r,
            col_l,
            col_r,
            alias={n + 1: 0, n + 2: 1},
        )
        left, row_l, _, _, col_r = call(
            functools.partial(mirror_kernel, n, t),
            "mirror_end",
            (narrow, slots, slots, slots, slots),
            [scratch] * 2 + [pltpu.VMEM((n,) + area, BF16)],
            rows[-1],
            *cols,
            table,
            weights,
            w_out,
            row_l,
            row_r,
            col_l,
            col_r,
            mixed,
            alias={n + 4: 1, n + 5: 2, n + 6: 3, n + 7: 4},
        )
        pair, right = call(
            functools.partial(own_end_kernel, n, t),
            "own_end",
            (narrow, narrow),
            [scratch],
            row_l,
            col_r,
            table,
            weights,
            pair,
            gating,
            w_out,
        )
        lefts = gather(left, "col", lambda s, step: ())
        left_slots = call(functools.partial(left_kernel, n), "left_slots", slots, [], *lefts[:-1], weight=20)
        rights = gather(right, "row", lambda s, step: left_slots if s else lefts[1] if step == 1 else ())
        gating = call(gate_kernel, "gate", broad, [], pair, table, weights)
        right_slots, mixed = call(
            functools.partial(middle_kernel, n, t), "middle_slots", (slots, broad), [], *rights[:-1], left_slots
        )
        out, _, _ = call(
            functools.partial(end_kernel, n, t),
            "end",
            (narrow, slots, slots),
            [scratch],
            lefts[-1],
            rights[-1],
            mixed,
            pair,
            gating,
            table,
            w_out,
            left_slots,
            right_slots,
            alias={7: 1, 8: 2},
        )
        return out.reshape(t, t, width)

    placed = (P(("groups", "row"), "col", None), P("groups")) + (P(),) * 8
    return jax.shard_map(
        per_device, mesh=mesh, in_specs=placed, out_specs=P(("groups", "row"), "col", None), check_vma=False
    )
```

```python
import functools

import jax
import jax.numpy as jnp
from jax import lax
from jax.experimental import pallas as pl
from jax.experimental.pallas import tpu as pltpu
from jax.sharding import PartitionSpec as P

F32, BF16 = jnp.float32, jnp.bfloat16


def dot(a, b):
    return jnp.dot(a, b, preferred_element_type=F32)


def split(values):
    high = values.astype(BF16)
    return jnp.concatenate([high, (values - high.astype(F32)).astype(BF16)], axis=1)


def constants(width):
    rows = lax.broadcasted_iota(jnp.int32, (2 * width, width), 0)
    cols = lax.broadcasted_iota(jnp.int32, (2 * width, width), 1)
    mean = jnp.full((2 * width, width), 1.0 / width, F32)
    center = jnp.where((rows == cols) | (rows == cols + width), 1.0, 0.0) - mean
    return center.astype(BF16), mean.astype(BF16)


def scaled(center, mean, gain, shift):
    spread = dot(split(center * center), mean)
    return (center * lax.rsqrt(spread + 1e-05) * gain + shift).astype(BF16)


def norm_pair(values, consts, gain, shift):
    return scaled(dot(values, consts[0][: values.shape[1]]), consts[1], gain, shift)


def norm_mixed(values, consts, gain, shift):
    return scaled(dot(split(values), consts[0]), consts[1], gain, shift)


def gated(normed, weights, bias, width):
    product = dot(normed, weights) + bias
    return (jnp.tanh(product[:, width:]) + 1.0) * product[:, :width]


def gate(normed, weights, bias):
    return 0.5 * jnp.tanh(dot(normed, weights) + bias) + 0.5


def masked(values, outer, inner):
    t = outer.shape[0]
    grid = jnp.concatenate([outer[k : k + 1] * inner for k in range(t)], axis=0)
    return (values * grid).astype(BF16)


def mix(out_ref, old_ref, lefts, rights, first, last, left_at, right_at, t):
    width = out_ref.shape[1]
    for base in range(0, t, 8):
        if old_ref is None:
            total = (jnp.zeros((t, width), F32),) * 8
        else:
            total = tuple(old_ref[pl.ds((base + i) * t, t), :] for i in range(8))

        def slot(s, total):
            ls, rs = left_at(s), right_at(s)

            def step(q, total):
                for u in range(4):
                    at = pl.multiple_of((q * 4 + u) * t, 8)
                    row = rights[rs, pl.ds(at, t), :]
                    total = tuple(total[i] + lefts[ls, pl.ds(at + base + i, 1), :] * row for i in range(8))
                return total

            return lax.fori_loop(0, t // 4, step, total)

        total = lax.fori_loop(first, last, slot, total)
        for i in range(8):
            out_ref[pl.ds((base + i) * t, t), :] = total[i]


def finish(pair, mixed, gating, consts, gain, shift, weights, bias):
    normout = norm_mixed(mixed, consts, gain, shift)
    return (pair.astype(F32) + gating * (dot(normout, weights) + bias)).astype(BF16)


TABLE_MASK = 24


def in_norm(table, u):
    return table[u : u + 1], table[2 + u : 3 + u]


def out_norm(table, u):
    return table[4 + u : 5 + u], table[6 + u : 7 + u]


def half_bias(table, u, first, last):
    return jnp.concatenate([table[k : k + 1] for k in range(10 + 5 * u + first, 10 + 5 * u + last)], axis=1) * 0.5


def mask_of(table, b, t):
    return table[pl.ds(pl.multiple_of(TABLE_MASK + b * t, 8), t), :]


def sides(values_ref, wide, left_at, right_at, outer, inner, consts, table, weights):
    t, width = outer.shape
    wide[...] = values_ref[...].astype(F32)
    values = jnp.concatenate([wide[pl.ds(k, t, stride=t), :] for k in range(t)], axis=0).astype(BF16)
    normed = norm_pair(values, consts, *in_norm(table, 0))
    for k, target in enumerate((left_at, right_at)):
        span = slice(2 * k * width, 2 * (k + 1) * width)
        side = gated(normed, weights[0, :, span], half_bias(table, 0, 2 * k, 2 * k + 2), width)
        target[...] = masked(side, outer, inner).astype(F32)


def gate_of(values, consts, table, weights, u):
    normed = norm_pair(values, consts, *in_norm(table, u))
    return gate(normed, weights[u, :, 4 * values.shape[1] :], half_bias(table, u, 4, 5))


def place(b, n):
    return b // 2 + lax.rem(b, 2) * (n // 2)


def placed_at(r, n):
    return lax.rem(r, n // 2) * 2 + r // (n // 2)


def early_pairs(late, n):
    return jnp.where(late == n - 1, n - 1, n - 2), lambda i: i + jnp.where(i >= late, 1, 0)


def late_pairs(late, n):
    return jnp.where(late == n - 1, 1, 2), lambda i: jnp.where(i == 0, n - 1, late)


def own_kernel(t, pair, table, w_in, weights, row_l, row_r, gating, wide):
    r, c = lax.axis_index("row"), lax.axis_index("col")
    consts = constants(wide.shape[1])
    weights[...] = w_in[...] * 0.5
    outer, inner = mask_of(table, c, t), mask_of(table, r, t)
    sides(pair, wide, row_l.at[0], row_r.at[0], outer, inner, consts, table, weights)
    gating[...] = gate_of(pair[...], consts, table, weights, 0)


def early_kernel(n, t, row, col, table, weights, left_in, right_in, row_l, row_r, col_l, col_r, wide):
    r, c = lax.axis_index("row"), lax.axis_index("col")
    consts = constants(wide.shape[1])
    here, there = mask_of(table, r, t), mask_of(table, c, t)
    outer = mask_of(table, placed_at(r, n), t)
    sides(col, wide, col_l.at[0], col_r.at[0], outer, there, consts, table, weights)
    outer = mask_of(table, c ^ 1, t)
    sides(row, wide, row_l.at[1], row_r.at[1], outer, here, consts, table, weights)


def middle_sides_kernel(n, t, *refs):
    rows, cols, (table, weights) = refs[: n - 3], refs[n - 3 : 2 * n - 5], refs[2 * n - 5 : 2 * n - 3]
    row_l, row_r, col_l, col_r, mixed, wide = refs[2 * n + 1 :]
    r, c = lax.axis_index("row"), lax.axis_index("col")
    consts = constants(wide.shape[1])
    here, there = mask_of(table, r, t), mask_of(table, c, t)
    for s, block in enumerate(rows, 2):
        outer = mask_of(table, c ^ s, t)
        sides(block, wide, row_l.at[s], row_r.at[s], outer, here, consts, table, weights)
    for s, block in enumerate(cols, 1):
        outer = mask_of(table, placed_at(r ^ s, n), t)
        sides(block, wide, col_l.at[s], col_r.at[s], outer, there, consts, table, weights)
    count, slot = early_pairs(c ^ placed_at(r ^ (n - 1), n), n)
    mix(mixed, None, col_l, row_r, 0, count, lambda i: r ^ place(c ^ slot(i), n), slot, t)


def mirror_kernel(n, t, *refs):
    row, cols, (table, weights, w_out) = refs[0], refs[1 : n + 1], refs[n + 1 : n + 4]
    old = refs[n + 8]
    left_ref, row_l, row_r, col_l, col_r, mixed, wide, held = refs[n + 9 :]
    width = wide.shape[1]
    r, c = lax.axis_index("row"), lax.axis_index("col")
    consts = constants(width)
    here, there = mask_of(table, r, t), mask_of(table, c, t)
    for block, left, right, outer, inner in (
        (row, row_l, row_r, c ^ (n - 1), here),
        (cols[-1], col_l, col_r, placed_at(r ^ (n - 1), n), there),
    ):
        outer = mask_of(table, outer, t)
        sides(block, wide, left.at[n - 1], right.at[n - 1], outer, inner, consts, table, weights)
    count, slot = late_pairs(c ^ placed_at(r ^ (n - 1), n), n)
    mix(mixed, old, col_l, row_r, 0, count, lambda i: r ^ place(c ^ slot(i), n), slot, t)
    for s in range(n):
        held[s] = cols[s][...]
    pair = held[r ^ place(r, n)]
    updated = finish(pair, mixed[...], gate_of(pair, consts, table, weights, 0), consts, *out_norm(table, 0), w_out[0], table[8:9])
    normed = norm_pair(updated, consts, *in_norm(table, 1))
    side = gated(normed, weights[1, :, : 2 * width], half_bias(table, 1, 0, 2), width)
    left_ref[...] = masked(side, there, here)


def own_end_kernel(n, t, row_l, col_r, table, weights, pair, gating, w_out, pair_ref, right_ref, mixed):
    width = mixed.shape[1]
    r, c = lax.axis_index("row"), lax.axis_index("col")
    consts = constants(width)
    mix(mixed, None, row_l, col_r, 0, n, lambda s: s, lambda s: r ^ place(c ^ s, n), t)
    updated = finish(pair[...], mixed[...], gating[...], consts, *out_norm(table, 0), w_out[0], table[8:9])
    pair_ref[...] = updated
    normed = norm_pair(updated, consts, *in_norm(table, 1))
    side = gated(normed, weights[1, :, 2 * width : 4 * width], half_bias(table, 1, 2, 4), width)
    right_ref[...] = masked(side, mask_of(table, r, t), mask_of(table, c, t))


def gate_kernel(pair, table, weights, gating):
    gating[...] = gate_of(pair[...], constants(pair.shape[1]), table, weights, 1)


def left_kernel(n, *refs):
    for s in range(n - 1):
        refs[n - 1][s] = refs[s][...].astype(F32)


def middle_kernel(n, t, *refs):
    sources, (lefts, rights, mixed) = refs[: n - 1], refs[n - 1 :]
    r, c = lax.axis_index("row"), lax.axis_index("col")
    for s in range(n - 1):
        rights[s] = sources[s][...].astype(F32)
    count, slot = early_pairs(r ^ c ^ (n - 1), n)
    mix(mixed, None, lefts, rights, 0, count, slot, lambda i: r ^ c ^ slot(i), t)


def end_kernel(n, t, left, right, old, pair, gating, table, w_out, left_in, right_in, out, lefts, rights, mixed):
    r, c = lax.axis_index("row"), lax.axis_index("col")
    lefts[n - 1] = left[...].astype(F32)
    rights[n - 1] = right[...].astype(F32)
    count, slot = late_pairs(r ^ c ^ (n - 1), n)
    mix(mixed, old, lefts, rights, 0, count, slot, lambda i: r ^ c ^ slot(i), t)
    consts = constants(mixed.shape[1])
    out[...] = finish(pair[...], mixed[...], gating[...], consts, *out_norm(table, 1), w_out[1], table[9:10])


def solution(mesh):
    n = mesh.shape["col"]

    def gather(block, axis, after):
        held, step = {0: block}, n // 2
        while step:
            for s, part in list(held.items()):
                part = lax.optimization_barrier((part, after(s, step)))[0]
                held[s ^ step] = lax.ppermute(part, axis, [(k, k ^ step) for k in range(n)])
            step //= 2
        return [held[s] for s in range(n)]

    def direct(block):
        return [block] + [lax.ppermute(block, "row", [(k, k ^ s) for k in range(n)]) for s in range(1, n)]

    def mirrored(block):
        pairs = [(a * n + z, (z // 2 + z % 2 * (n // 2)) * n + a) for a in range(n) for z in range(n)]
        return lax.ppermute(block, ("row", "col"), pairs)

    def per_device(pair, token_mask, in_gain, in_shift, w_in, bias_in, out_gain, out_shift, w_out, bias_out):
        t, _, width = pair.shape
        area = (t * t, width)
        narrow, broad = jax.ShapeDtypeStruct(area, BF16), jax.ShapeDtypeStruct(area, F32)
        slots = jax.ShapeDtypeStruct((n,) + area, F32)
        scratch = pltpu.VMEM(area, F32)

        def call(kernel, name, outs, scratches, *operands, alias=None, weight=0):
            return pl.pallas_call(
                kernel,
                out_shape=outs,
                scratch_shapes=scratches,
                input_output_aliases=alias or {},
                cost_estimate=pl.CostEstimate(
                    flops=weight * 10**9, bytes_accessed=weight * 10**6, transcendentals=0
                ) if weight else None,

                compiler_params=pltpu.CompilerParams(vmem_limit_bytes=(16 + n) * 1024 * 1024),
                name=name,
            )(*operands)

        pair = pair.reshape(area)
        col_block = mirrored(pair)
        mask = jnp.broadcast_to(token_mask.astype(F32)[:, None], (n * t, width))
        vectors = [in_gain, in_shift, out_gain, out_shift, bias_out, bias_in.reshape(-1, width)]
        table = jnp.concatenate(vectors + [jnp.zeros((TABLE_MASK - 20, width), F32), mask])
        weights, row_l, row_r, gating = call(
            functools.partial(own_kernel, t),
            "own_sides",
            (jax.ShapeDtypeStruct(w_in.shape, BF16), slots, slots, broad),
            [scratch],
            pair,
            table,
            w_in,
        )
        own_l = row_l
        near = lax.ppermute(pair, "col", [(k, k ^ 1) for k in range(n)])
        row_l, row_r, col_l, col_r = call(
            functools.partial(early_kernel, n, t),
            "early_sides",
            (slots,) * 4,
            [scratch],
            near,
            col_block,
            table,
            weights,
            row_l,
            row_r,
            alias={4: 0, 5: 1},
        )
        rows = gather(pair, "col", lambda s, step: row_l if s else ())
        rows[1] = near
        cols = direct(lax.optimization_barrier((col_block, own_l))[0])
        row_l, row_r, col_l, col_r, mixed = call(
            functools.partial(middle_sides_kernel, n, t),
            "middle_sides",
            (slots,) * 4 + (broad,),
            [scratch],
            *rows[2:-1],
            *cols[1:-1],
            table,
            weights,
            row_l,
            row_r,
            col_l,
            col_r,
            alias={2 * n - 3: 0, 2 * n - 2: 1, 2 * n - 1: 2, 2 * n: 3},
        )
        left, row_l, _, _, col_r = call(
            functools.partial(mirror_kernel, n, t),
            "mirror_end",
            (narrow, slots, slots, slots, slots),
            [scratch] * 2 + [pltpu.VMEM((n,) + area, BF16)],
            rows[-1],
            *cols,
            table,
            weights,
            w_out,
            row_l,
            row_r,
            col_l,
            col_r,
            mixed,
            alias={n + 4: 1, n + 5: 2, n + 6: 3, n + 7: 4},
        )
        pair, right = call(
            functools.partial(own_end_kernel, n, t),
            "own_end",
            (narrow, narrow),
            [scratch],
            row_l,
            col_r,
            table,
            weights,
            pair,
            gating,
            w_out,
        )
        lefts = gather(left, "col", lambda s, step: ())
        left_slots = call(functools.partial(left_kernel, n), "left_slots", slots, [], *lefts[:-1], weight=20)
        rights = gather(right, "row", lambda s, step: left_slots if s else ())
        gating = call(gate_kernel, "gate", broad, [], pair, table, weights)
        right_slots, mixed = call(
            functools.partial(middle_kernel, n, t), "middle_slots", (slots, broad), [], *rights[:-1], left_slots
        )
        out, _, _ = call(
            functools.partial(end_kernel, n, t),
            "end",
            (narrow, slots, slots),
            [scratch],
            lefts[-1],
            rights[-1],
            mixed,
            pair,
            gating,
            table,
            w_out,
            left_slots,
            right_slots,
            alias={7: 1, 8: 2},
        )
        return out.reshape(t, t, width)

    placed = (P(("groups", "row"), "col", None), P("groups")) + (P(),) * 8
    return jax.shard_map(
        per_device, mesh=mesh, in_specs=placed, out_specs=P(("groups", "row"), "col", None), check_vma=False
    )
```

```python
import functools

import jax
import jax.numpy as jnp
from jax import lax
from jax.experimental import pallas as pl
from jax.experimental.pallas import tpu as pltpu
from jax.sharding import PartitionSpec as P

F32, BF16 = jnp.float32, jnp.bfloat16


def dot(a, b):
    return jnp.dot(a, b, preferred_element_type=F32)


def split(values):
    high = values.astype(BF16)
    return jnp.concatenate([high, (values - high.astype(F32)).astype(BF16)], axis=1)


def constants(width):
    rows = lax.broadcasted_iota(jnp.int32, (2 * width, width), 0)
    cols = lax.broadcasted_iota(jnp.int32, (2 * width, width), 1)
    mean = jnp.full((2 * width, width), 1.0 / width, F32)
    center = jnp.where((rows == cols) | (rows == cols + width), 1.0, 0.0) - mean
    return center.astype(BF16), mean.astype(BF16)


def scaled(center, mean, gain, shift):
    spread = dot(split(center * center), mean)
    return (center * lax.rsqrt(spread + 1e-05) * gain + shift).astype(BF16)


def norm_pair(values, consts, gain, shift):
    return scaled(dot(values, consts[0][: values.shape[1]]), consts[1], gain, shift)


def norm_mixed(values, consts, gain, shift):
    return scaled(dot(split(values), consts[0]), consts[1], gain, shift)


def gated(normed, weights, bias, width):
    product = dot(normed, weights) + bias
    return (jnp.tanh(product[:, width:]) + 1.0) * product[:, :width]


def gate(normed, weights, bias):
    return 0.5 * jnp.tanh(dot(normed, weights) + bias) + 0.5


def masked(values, outer, inner):
    t = outer.shape[0]
    grid = jnp.concatenate([outer[k : k + 1] * inner for k in range(t)], axis=0)
    return (values * grid).astype(BF16)


def mix(out_ref, old_ref, lefts, rights, first, last, left_at, right_at, t):
    width = out_ref.shape[1]
    for base in range(0, t, 8):
        if old_ref is None:
            total = (jnp.zeros((t, width), F32),) * 8
        else:
            total = tuple(old_ref[pl.ds((base + i) * t, t), :] for i in range(8))

        def slot(s, total):
            ls, rs = left_at(s), right_at(s)

            def step(q, total):
                for u in range(4):
                    at = pl.multiple_of((q * 4 + u) * t, 8)
                    row = rights[rs, pl.ds(at, t), :]
                    total = tuple(total[i] + lefts[ls, pl.ds(at + base + i, 1), :] * row for i in range(8))
                return total

            return lax.fori_loop(0, t // 4, step, total)

        total = lax.fori_loop(first, last, slot, total)
        for i in range(8):
            out_ref[pl.ds((base + i) * t, t), :] = total[i]


def finish(pair, mixed, gating, consts, gain, shift, weights, bias):
    normout = norm_mixed(mixed, consts, gain, shift)
    return (pair.astype(F32) + gating * (dot(normout, weights) + bias)).astype(BF16)


TABLE_MASK = 24


def in_norm(table, u):
    return table[u : u + 1], table[2 + u : 3 + u]


def out_norm(table, u):
    return table[4 + u : 5 + u], table[6 + u : 7 + u]


def half_bias(table, u, first, last):
    return jnp.concatenate([table[k : k + 1] for k in range(10 + 5 * u + first, 10 + 5 * u + last)], axis=1) * 0.5


def mask_of(table, b, t):
    return table[pl.ds(pl.multiple_of(TABLE_MASK + b * t, 8), t), :]


def sides(values_ref, wide, left_at, right_at, outer, inner, consts, table, weights):
    t, width = outer.shape
    wide[...] = values_ref[...].astype(F32)
    values = jnp.concatenate([wide[pl.ds(k, t, stride=t), :] for k in range(t)], axis=0).astype(BF16)
    normed = norm_pair(values, consts, *in_norm(table, 0))
    for k, target in enumerate((left_at, right_at)):
        span = slice(2 * k * width, 2 * (k + 1) * width)
        side = gated(normed, weights[0, :, span], half_bias(table, 0, 2 * k, 2 * k + 2), width)
        target[...] = masked(side, outer, inner).astype(F32)


def gate_of(values, consts, table, weights, u):
    normed = norm_pair(values, consts, *in_norm(table, u))
    return gate(normed, weights[u, :, 4 * values.shape[1] :], half_bias(table, u, 4, 5))


def place(b, n):
    return b // 2 + lax.rem(b, 2) * (n // 2)


def placed_at(r, n):
    return lax.rem(r, n // 2) * 2 + r // (n // 2)


def early_pairs(late, n):
    return jnp.where(late == n - 1, n - 1, n - 2), lambda i: i + jnp.where(i >= late, 1, 0)


def late_pairs(late, n):
    return jnp.where(late == n - 1, 1, 2), lambda i: jnp.where(i == 0, n - 1, late)


def own_kernel(t, pair, table, w_in, weights, row_l, row_r, gating, wide):
    r, c = lax.axis_index("row"), lax.axis_index("col")
    consts = constants(wide.shape[1])
    weights[...] = w_in[...] * 0.5
    outer, inner = mask_of(table, c, t), mask_of(table, r, t)
    sides(pair, wide, row_l.at[0], row_r.at[0], outer, inner, consts, table, weights)
    gating[...] = gate_of(pair[...], consts, table, weights, 0)


def early_kernel(n, t, col, table, weights, col_l, col_r, wide):
    r, c = lax.axis_index("row"), lax.axis_index("col")
    outer, inner = mask_of(table, placed_at(r, n), t), mask_of(table, c, t)
    sides(col, wide, col_l.at[0], col_r.at[0], outer, inner, constants(wide.shape[1]), table, weights)


def middle_sides_kernel(n, t, *refs):
    rows, cols, (table, weights) = refs[: n - 2], refs[n - 2 : 2 * n - 4], refs[2 * n - 4 : 2 * n - 2]
    row_l, row_r, col_l, col_r, mixed, wide = refs[2 * n + 2 :]
    r, c = lax.axis_index("row"), lax.axis_index("col")
    consts = constants(wide.shape[1])
    here, there = mask_of(table, r, t), mask_of(table, c, t)
    for s, block in enumerate(rows, 1):
        outer = mask_of(table, c ^ s, t)
        sides(block, wide, row_l.at[s], row_r.at[s], outer, here, consts, table, weights)
    for s, block in enumerate(cols, 1):
        outer = mask_of(table, placed_at(r ^ s, n), t)
        sides(block, wide, col_l.at[s], col_r.at[s], outer, there, consts, table, weights)
    count, slot = early_pairs(c ^ placed_at(r ^ (n - 1), n), n)
    mix(mixed, None, col_l, row_r, 0, count, lambda i: r ^ place(c ^ slot(i), n), slot, t)


def mirror_kernel(n, t, *refs):
    row, cols, (table, weights, w_out) = refs[0], refs[1 : n + 1], refs[n + 1 : n + 4]
    old = refs[n + 8]
    left_ref, row_l, row_r, col_l, col_r, mixed, wide, held = refs[n + 9 :]
    width = wide.shape[1]
    r, c = lax.axis_index("row"), lax.axis_index("col")
    consts = constants(width)
    here, there = mask_of(table, r, t), mask_of(table, c, t)
    for block, left, right, outer, inner in (
        (row, row_l, row_r, c ^ (n - 1), here),
        (cols[-1], col_l, col_r, placed_at(r ^ (n - 1), n), there),
    ):
        outer = mask_of(table, outer, t)
        sides(block, wide, left.at[n - 1], right.at[n - 1], outer, inner, consts, table, weights)
    count, slot = late_pairs(c ^ placed_at(r ^ (n - 1), n), n)
    mix(mixed, old, col_l, row_r, 0, count, lambda i: r ^ place(c ^ slot(i), n), slot, t)
    for s in range(n):
        held[s] = cols[s][...]
    pair = held[r ^ place(r, n)]
    updated = finish(pair, mixed[...], gate_of(pair, consts, table, weights, 0), consts, *out_norm(table, 0), w_out[0], table[8:9])
    normed = norm_pair(updated, consts, *in_norm(table, 1))
    side = gated(normed, weights[1, :, : 2 * width], half_bias(table, 1, 0, 2), width)
    left_ref[...] = masked(side, there, here)


def own_end_kernel(n, t, row_l, col_r, table, weights, pair, gating, w_out, pair_ref, right_ref, mixed):
    width = mixed.shape[1]
    r, c = lax.axis_index("row"), lax.axis_index("col")
    consts = constants(width)
    mix(mixed, None, row_l, col_r, 0, n, lambda s: s, lambda s: r ^ place(c ^ s, n), t)
    updated = finish(pair[...], mixed[...], gating[...], consts, *out_norm(table, 0), w_out[0], table[8:9])
    pair_ref[...] = updated
    normed = norm_pair(updated, consts, *in_norm(table, 1))
    side = gated(normed, weights[1, :, 2 * width : 4 * width], half_bias(table, 1, 2, 4), width)
    right_ref[...] = masked(side, mask_of(table, r, t), mask_of(table, c, t))


def gate_kernel(pair, table, weights, gating):
    gating[...] = gate_of(pair[...], constants(pair.shape[1]), table, weights, 1)


def left_kernel(n, *refs):
    for s in range(n - 1):
        refs[n - 1][s] = refs[s][...].astype(F32)


def widen_kernel(block, out):
    out[...] = block[...].astype(F32)


def middle_kernel(n, t, *refs):
    sources, (lefts, rights, mixed) = refs[: n - 1], refs[n - 1 :]
    r, c = lax.axis_index("row"), lax.axis_index("col")
    for s in range(n - 1):
        rights[s] = sources[s][...].astype(F32)
    count, slot = early_pairs(r ^ c ^ (n - 1), n)
    mix(mixed, None, lefts, rights, 0, count, slot, lambda i: r ^ c ^ slot(i), t)


def end_kernel(n, t, left, right, old, pair, gating, table, w_out, left_in, right_in, out, lefts, rights, mixed):
    r, c = lax.axis_index("row"), lax.axis_index("col")
    lefts[n - 1] = left[...]
    rights[n - 1] = right[...].astype(F32)
    count, slot = late_pairs(r ^ c ^ (n - 1), n)
    mix(mixed, old, lefts, rights, 0, count, slot, lambda i: r ^ c ^ slot(i), t)
    consts = constants(mixed.shape[1])
    out[...] = finish(pair[...], mixed[...], gating[...], consts, *out_norm(table, 1), w_out[1], table[9:10])


def solution(mesh):
    n = mesh.shape["col"]

    def gather(block, axis, after):
        held, step = {0: block}, n // 2
        while step:
            for s, part in list(held.items()):
                part = lax.optimization_barrier((part, after(s, step)))[0]
                held[s ^ step] = lax.ppermute(part, axis, [(k, k ^ step) for k in range(n)])
            step //= 2
        return [held[s] for s in range(n)]

    def direct(block):
        return [block] + [lax.ppermute(block, "row", [(k, k ^ s) for k in range(n)]) for s in range(1, n)]

    def mirrored(block):
        pairs = [(a * n + z, (z // 2 + z % 2 * (n // 2)) * n + a) for a in range(n) for z in range(n)]
        return lax.ppermute(block, ("row", "col"), pairs)

    def per_device(pair, token_mask, in_gain, in_shift, w_in, bias_in, out_gain, out_shift, w_out, bias_out):
        t, _, width = pair.shape
        area = (t * t, width)
        narrow, broad = jax.ShapeDtypeStruct(area, BF16), jax.ShapeDtypeStruct(area, F32)
        slots = jax.ShapeDtypeStruct((n,) + area, F32)
        scratch = pltpu.VMEM(area, F32)

        def call(kernel, name, outs, scratches, *operands, alias=None, weight=0):
            return pl.pallas_call(
                kernel,
                out_shape=outs,
                scratch_shapes=scratches,
                input_output_aliases=alias or {},
                cost_estimate=pl.CostEstimate(
                    flops=weight * 10**9, bytes_accessed=weight * 10**6, transcendentals=0
                ) if weight else None,

                compiler_params=pltpu.CompilerParams(vmem_limit_bytes=(16 + n) * 1024 * 1024),
                name=name,
            )(*operands)

        pair = pair.reshape(area)
        col_block = mirrored(pair)
        mask = jnp.broadcast_to(token_mask.astype(F32)[:, None], (n * t, width))
        vectors = [in_gain, in_shift, out_gain, out_shift, bias_out, bias_in.reshape(-1, width)]
        table = jnp.concatenate(vectors + [jnp.zeros((TABLE_MASK - 20, width), F32), mask])
        weights, row_l, row_r, gating = call(
            functools.partial(own_kernel, t),
            "own_sides",
            (jax.ShapeDtypeStruct(w_in.shape, BF16), slots, slots, broad),
            [scratch],
            pair,
            table,
            w_in,
        )
        own_l = row_l
        col_l, col_r = call(
            functools.partial(early_kernel, n, t), "early_sides", (slots,) * 2, [scratch], col_block, table, weights
        )
        rows = gather(pair, "col", lambda s, step: (own_l, col_l) if s else ())
        cols = direct(lax.optimization_barrier((col_block, own_l))[0])
        row_l, row_r, col_l, col_r, mixed = call(
            functools.partial(middle_sides_kernel, n, t),
            "middle_sides",
            (slots,) * 4 + (broad,),
            [scratch],
            *rows[1:-1],
            *cols[1:-1],
            table,
            weights,
            row_l,
            row_r,
            col_l,
            col_r,
            alias={2 * n - 2: 0, 2 * n - 1: 1, 2 * n: 2, 2 * n + 1: 3},
        )
        left, row_l, _, _, col_r = call(
            functools.partial(mirror_kernel, n, t),
            "mirror_end",
            (narrow, slots, slots, slots, slots),
            [scratch] * 2 + [pltpu.VMEM((n,) + area, BF16)],
            rows[-1],
            *cols,
            table,
            weights,
            w_out,
            row_l,
            row_r,
            col_l,
            col_r,
            mixed,
            alias={n + 4: 1, n + 5: 2, n + 6: 3, n + 7: 4},
        )
        pair, right = call(
            functools.partial(own_end_kernel, n, t),
            "own_end",
            (narrow, narrow),
            [scratch],
            row_l,
            col_r,
            table,
            weights,
            pair,
            gating,
            w_out,
        )
        lefts = gather(left, "col", lambda s, step: ())
        left_slots = call(functools.partial(left_kernel, n), "left_slots", slots, [], *lefts[:-1], weight=20)
        rights = gather(right, "row", lambda s, step: left_slots if s else ())
        gating = call(gate_kernel, "gate", broad, [], pair, table, weights)
        right_slots, mixed = call(
            functools.partial(middle_kernel, n, t), "middle_slots", (slots, broad), [], *rights[:-1], left_slots
        )
        left_last = call(widen_kernel, "left_last", broad, [], lefts[-1], weight=30)
        out, _, _ = call(
            functools.partial(end_kernel, n, t),
            "end",
            (narrow, slots, slots),
            [scratch],
            left_last,
            rights[-1],
            mixed,
            pair,
            gating,
            table,
            w_out,
            left_slots,
            right_slots,
            alias={7: 1, 8: 2},
        )
        return out.reshape(t, t, width)

    placed = (P(("groups", "row"), "col", None), P("groups")) + (P(),) * 8
    return jax.shard_map(
        per_device, mesh=mesh, in_specs=placed, out_specs=P(("groups", "row"), "col", None), check_vma=False
    )
```

```python
import functools

import jax
import jax.numpy as jnp
from jax import lax
from jax.experimental import pallas as pl
from jax.experimental.pallas import tpu as pltpu
from jax.sharding import PartitionSpec as P

F32, BF16 = jnp.float32, jnp.bfloat16


def dot(a, b):
    return jnp.dot(a, b, preferred_element_type=F32)


def split(values):
    high = values.astype(BF16)
    return jnp.concatenate([high, (values - high.astype(F32)).astype(BF16)], axis=1)


def constants(width):
    rows = lax.broadcasted_iota(jnp.int32, (2 * width, width), 0)
    cols = lax.broadcasted_iota(jnp.int32, (2 * width, width), 1)
    mean = jnp.full((2 * width, width), 1.0 / width, F32)
    center = jnp.where((rows == cols) | (rows == cols + width), 1.0, 0.0) - mean
    return center.astype(BF16), mean.astype(BF16)


def scaled(center, mean, gain, shift):
    spread = dot(split(center * center), mean)
    return (center * lax.rsqrt(spread + 1e-05) * gain + shift).astype(BF16)


def norm_pair(values, consts, gain, shift):
    return scaled(dot(values, consts[0][: values.shape[1]]), consts[1], gain, shift)


def norm_mixed(values, consts, gain, shift):
    return scaled(dot(split(values), consts[0]), consts[1], gain, shift)


def gated(normed, weights, bias, width):
    product = dot(normed, weights) + bias
    return (jnp.tanh(product[:, width:]) + 1.0) * product[:, :width]


def gate(normed, weights, bias):
    return 0.5 * jnp.tanh(dot(normed, weights) + bias) + 0.5


def masked(values, outer, inner):
    t = outer.shape[0]
    grid = jnp.concatenate([outer[k : k + 1] * inner for k in range(t)], axis=0)
    return (values * grid).astype(BF16)


def mix(out_ref, old_ref, lefts, rights, first, last, left_at, right_at, t):
    width = out_ref.shape[1]
    for base in range(0, t, 8):
        if old_ref is None:
            total = (jnp.zeros((t, width), F32),) * 8
        else:
            total = tuple(old_ref[pl.ds((base + i) * t, t), :] for i in range(8))

        def slot(s, total):
            ls, rs = left_at(s), right_at(s)

            def step(q, total):
                for u in range(4):
                    at = pl.multiple_of((q * 4 + u) * t, 8)
                    row = rights[rs, pl.ds(at, t), :]
                    total = tuple(total[i] + lefts[ls, pl.ds(at + base + i, 1), :] * row for i in range(8))
                return total

            return lax.fori_loop(0, t // 4, step, total)

        total = lax.fori_loop(first, last, slot, total)
        for i in range(8):
            out_ref[pl.ds((base + i) * t, t), :] = total[i]


def finish(pair, mixed, gating, consts, gain, shift, weights, bias):
    normout = norm_mixed(mixed, consts, gain, shift)
    return (pair.astype(F32) + gating * (dot(normout, weights) + bias)).astype(BF16)


TABLE_MASK = 24


def in_norm(table, u):
    return table[u : u + 1], table[2 + u : 3 + u]


def out_norm(table, u):
    return table[4 + u : 5 + u], table[6 + u : 7 + u]


def half_bias(table, u, first, last):
    return jnp.concatenate([table[k : k + 1] for k in range(10 + 5 * u + first, 10 + 5 * u + last)], axis=1) * 0.5


def mask_of(table, b, t):
    return table[pl.ds(pl.multiple_of(TABLE_MASK + b * t, 8), t), :]


def sides(values_ref, wide, left_at, right_at, outer, inner, consts, table, weights):
    t, width = outer.shape
    wide[...] = values_ref[...].astype(F32)
    values = jnp.concatenate([wide[pl.ds(k, t, stride=t), :] for k in range(t)], axis=0).astype(BF16)
    normed = norm_pair(values, consts, *in_norm(table, 0))
    for k, target in enumerate((left_at, right_at)):
        span = slice(2 * k * width, 2 * (k + 1) * width)
        side = gated(normed, weights[0, :, span], half_bias(table, 0, 2 * k, 2 * k + 2), width)
        target[...] = masked(side, outer, inner).astype(F32)


def gate_of(values, consts, table, weights, u):
    normed = norm_pair(values, consts, *in_norm(table, u))
    return gate(normed, weights[u, :, 4 * values.shape[1] :], half_bias(table, u, 4, 5))


def place(b, n):
    return b // 2 + lax.rem(b, 2) * (n // 2)


def placed_at(r, n):
    return lax.rem(r, n // 2) * 2 + r // (n // 2)


def early_pairs(late, n):
    return jnp.where(late == n - 1, n - 1, n - 2), lambda i: i + jnp.where(i >= late, 1, 0)


def late_pairs(late, n):
    return jnp.where(late == n - 1, 1, 2), lambda i: jnp.where(i == 0, n - 1, late)


def own_kernel(t, pair, table, w_in, weights, row_l, row_r, gating, wide):
    r, c = lax.axis_index("row"), lax.axis_index("col")
    consts = constants(wide.shape[1])
    weights[...] = w_in[...] * 0.5
    outer, inner = mask_of(table, c, t), mask_of(table, r, t)
    sides(pair, wide, row_l.at[0], row_r.at[0], outer, inner, consts, table, weights)
    gating[...] = gate_of(pair[...], consts, table, weights, 0)


def early_kernel(n, t, col, table, weights, col_l, col_r, wide):
    r, c = lax.axis_index("row"), lax.axis_index("col")
    outer, inner = mask_of(table, placed_at(r, n), t), mask_of(table, c, t)
    sides(col, wide, col_l.at[0], col_r.at[0], outer, inner, constants(wide.shape[1]), table, weights)


def first_sides_kernel(n, t, *refs):
    rows, (col, table, weights) = refs[: n - 2], refs[n - 2 : n + 1]
    row_l, row_r, col_l, col_r, wide = refs[n + 5 :]
    r, c = lax.axis_index("row"), lax.axis_index("col")
    consts = constants(wide.shape[1])
    here, there = mask_of(table, r, t), mask_of(table, c, t)
    for s, block in enumerate(rows, 1):
        outer = mask_of(table, c ^ s, t)
        sides(block, wide, row_l.at[s], row_r.at[s], outer, here, consts, table, weights)
    outer = mask_of(table, placed_at(r ^ 1, n), t)
    sides(col, wide, col_l.at[1], col_r.at[1], outer, there, consts, table, weights)


def second_sides_kernel(n, t, *refs):
    cols, (table, weights, row_r) = refs[: n - 3], refs[n - 3 : n]
    col_l, col_r, mixed, wide = refs[n + 2 :]
    r, c = lax.axis_index("row"), lax.axis_index("col")
    consts = constants(wide.shape[1])
    there = mask_of(table, c, t)
    for s, block in enumerate(cols, 2):
        outer = mask_of(table, placed_at(r ^ s, n), t)
        sides(block, wide, col_l.at[s], col_r.at[s], outer, there, consts, table, weights)
    count, slot = early_pairs(c ^ placed_at(r ^ (n - 1), n), n)
    mix(mixed, None, col_l, row_r, 0, count, lambda i: r ^ place(c ^ slot(i), n), slot, t)


def mirror_kernel(n, t, *refs):
    row, cols, (table, weights, w_out) = refs[0], refs[1 : n + 1], refs[n + 1 : n + 4]
    old = refs[n + 8]
    left_ref, row_l, row_r, col_l, col_r, mixed, wide, held = refs[n + 9 :]
    width = wide.shape[1]
    r, c = lax.axis_index("row"), lax.axis_index("col")
    consts = constants(width)
    here, there = mask_of(table, r, t), mask_of(table, c, t)
    for block, left, right, outer, inner in (
        (row, row_l, row_r, c ^ (n - 1), here),
        (cols[-1], col_l, col_r, placed_at(r ^ (n - 1), n), there),
    ):
        outer = mask_of(table, outer, t)
        sides(block, wide, left.at[n - 1], right.at[n - 1], outer, inner, consts, table, weights)
    count, slot = late_pairs(c ^ placed_at(r ^ (n - 1), n), n)
    mix(mixed, old, col_l, row_r, 0, count, lambda i: r ^ place(c ^ slot(i), n), slot, t)
    for s in range(n):
        held[s] = cols[s][...]
    pair = held[r ^ place(r, n)]
    updated = finish(pair, mixed[...], gate_of(pair, consts, table, weights, 0), consts, *out_norm(table, 0), w_out[0], table[8:9])
    normed = norm_pair(updated, consts, *in_norm(table, 1))
    side = gated(normed, weights[1, :, : 2 * width], half_bias(table, 1, 0, 2), width)
    left_ref[...] = masked(side, there, here)


def own_end_kernel(n, t, row_l, col_r, table, weights, pair, gating, w_out, pair_ref, right_ref, mixed):
    width = mixed.shape[1]
    r, c = lax.axis_index("row"), lax.axis_index("col")
    consts = constants(width)
    mix(mixed, None, row_l, col_r, 0, n, lambda s: s, lambda s: r ^ place(c ^ s, n), t)
    updated = finish(pair[...], mixed[...], gating[...], consts, *out_norm(table, 0), w_out[0], table[8:9])
    pair_ref[...] = updated
    normed = norm_pair(updated, consts, *in_norm(table, 1))
    side = gated(normed, weights[1, :, 2 * width : 4 * width], half_bias(table, 1, 2, 4), width)
    right_ref[...] = masked(side, mask_of(table, r, t), mask_of(table, c, t))


def gate_kernel(pair, table, weights, gating):
    gating[...] = gate_of(pair[...], constants(pair.shape[1]), table, weights, 1)


def left_kernel(n, *refs):
    for s in range(n - 1):
        refs[n - 1][s] = refs[s][...].astype(F32)


def widen_kernel(block, out):
    out[...] = block[...].astype(F32)


def right_lot(late, first, last):
    skips = (late >= first) & (late < last)
    count = last - first - jnp.where(skips, 1, 0)
    return count, lambda i: first + i + jnp.where(skips & (first + i >= late), 1, 0)


def near_kernel(n, t, own, core, lefts, rights, mixed):
    r, c = lax.axis_index("row"), lax.axis_index("col")
    rights[0] = own[...].astype(F32)
    rights[1] = core[...].astype(F32)
    count, slot = right_lot(r ^ c ^ (n - 1), 0, 2)
    mix(mixed, None, lefts, rights, 0, count, lambda i: r ^ c ^ slot(i), slot, t)


def far_kernel(n, t, *refs):
    sources, (lefts, _, old, rights, mixed) = refs[: n - 3], refs[n - 3 :]
    r, c = lax.axis_index("row"), lax.axis_index("col")
    for s, source in enumerate(sources, 2):
        rights[s] = source[...].astype(F32)
    count, slot = right_lot(r ^ c ^ (n - 1), 2, n - 1)
    mix(mixed, old, lefts, rights, 0, count, lambda i: r ^ c ^ slot(i), slot, t)


def end_kernel(n, t, left, right, old, pair, gating, table, w_out, left_in, right_in, out, lefts, rights, mixed):
    r, c = lax.axis_index("row"), lax.axis_index("col")
    lefts[n - 1] = left[...]
    rights[n - 1] = right[...].astype(F32)
    count, slot = late_pairs(r ^ c ^ (n - 1), n)
    mix(mixed, old, lefts, rights, 0, count, slot, lambda i: r ^ c ^ slot(i), t)
    consts = constants(mixed.shape[1])
    out[...] = finish(pair[...], mixed[...], gating[...], consts, *out_norm(table, 1), w_out[1], table[9:10])


def solution(mesh):
    n = mesh.shape["col"]

    def gather(block, axis, after):
        held, step = {0: block}, n // 2
        while step:
            for s, part in list(held.items()):
                part = lax.optimization_barrier((part, after(s, step)))[0]
                held[s ^ step] = lax.ppermute(part, axis, [(k, k ^ step) for k in range(n)])
            step //= 2
        return [held[s] for s in range(n)]

    def direct(block, last):
        return [block] + [
            lax.ppermute(last if s == n - 1 else block, "row", [(k, k ^ s) for k in range(n)]) for s in range(1, n)
        ]

    def mirrored(block):
        pairs = [(a * n + z, (z // 2 + z % 2 * (n // 2)) * n + a) for a in range(n) for z in range(n)]
        return lax.ppermute(block, ("row", "col"), pairs)

    def per_device(pair, token_mask, in_gain, in_shift, w_in, bias_in, out_gain, out_shift, w_out, bias_out):
        t, _, width = pair.shape
        area = (t * t, width)
        narrow, broad = jax.ShapeDtypeStruct(area, BF16), jax.ShapeDtypeStruct(area, F32)
        slots = jax.ShapeDtypeStruct((n,) + area, F32)
        scratch = pltpu.VMEM(area, F32)

        def call(kernel, name, outs, scratches, *operands, alias=None, weight=0):
            return pl.pallas_call(
                kernel,
                out_shape=outs,
                scratch_shapes=scratches,
                input_output_aliases=alias or {},
                cost_estimate=pl.CostEstimate(
                    flops=weight * 10**9, bytes_accessed=weight * 10**6, transcendentals=0
                ) if weight else None,

                compiler_params=pltpu.CompilerParams(vmem_limit_bytes=(16 + n) * 1024 * 1024),
                name=name,
            )(*operands)

        pair = pair.reshape(area)
        col_block = mirrored(pair)
        mask = jnp.broadcast_to(token_mask.astype(F32)[:, None], (n * t, width))
        vectors = [in_gain, in_shift, out_gain, out_shift, bias_out, bias_in.reshape(-1, width)]
        table = jnp.concatenate(vectors + [jnp.zeros((TABLE_MASK - 20, width), F32), mask])
        weights, row_l, row_r, gating = call(
            functools.partial(own_kernel, t),
            "own_sides",
            (jax.ShapeDtypeStruct(w_in.shape, BF16), slots, slots, broad),
            [scratch],
            pair,
            table,
            w_in,
        )
        own_l = row_l
        col_l, col_r = call(
            functools.partial(early_kernel, n, t), "early_sides", (slots,) * 2, [scratch], col_block, table, weights
        )
        rows = gather(pair, "col", lambda s, step: (own_l, col_l) if s else ())
        cols = direct(*(lax.optimization_barrier((col_block, after))[0] for after in (own_l, col_l)))
        row_l, row_r, col_l, col_r = call(
            functools.partial(first_sides_kernel, n, t),
            "first_sides",
            (slots,) * 4,
            [scratch],
            *rows[1:-1],
            cols[1],
            table,
            weights,
            row_l,
            row_r,
            col_l,
            col_r,
            alias={n + 1: 0, n + 2: 1, n + 3: 2, n + 4: 3},
        )
        col_l, col_r, mixed = call(
            functools.partial(second_sides_kernel, n, t),
            "second_sides",
            (slots, slots, broad),
            [scratch],
            *cols[2:-1],
            table,
            weights,
            row_r,
            col_l,
            col_r,
            alias={n: 0, n + 1: 1},
        )
        left, row_l, _, _, col_r = call(
            functools.partial(mirror_kernel, n, t),
            "mirror_end",
            (narrow, slots, slots, slots, slots),
            [scratch] * 2 + [pltpu.VMEM((n,) + area, BF16)],
            rows[-1],
            *cols,
            table,
            weights,
            w_out,
            row_l,
            row_r,
            col_l,
            col_r,
            mixed,
            alias={n + 4: 1, n + 5: 2, n + 6: 3, n + 7: 4},
        )
        pair, right = call(
            functools.partial(own_end_kernel, n, t),
            "own_end",
            (narrow, narrow),
            [scratch],
            row_l,
            col_r,
            table,
            weights,
            pair,
            gating,
            w_out,
        )
        lefts = gather(left, "col", lambda s, step: ())
        left_slots = call(functools.partial(left_kernel, n), "left_slots", slots, [], *lefts[:-1], weight=20)
        core = lax.ppermute(right, "row", [(k, k ^ 1) for k in range(n)])
        right_slots, mixed = call(
            functools.partial(near_kernel, n, t), "near_slots", (slots, broad), [], right, core, left_slots
        )
        rights = gather(right, "row", lambda s, step: mixed if s else ())
        settled = lax.optimization_barrier((pair, left_slots))[0]
        gating = call(gate_kernel, "gate", broad, [], settled, table, weights)
        right_slots, mixed = call(
            functools.partial(far_kernel, n, t),
            "far_slots",
            (slots, broad),
            [],
            *rights[2:-1],
            left_slots,
            right_slots,
            mixed,
            alias={n - 2: 0, n - 1: 1},
        )
        left_last = call(widen_kernel, "left_last", broad, [], lefts[-1], weight=30)
        out, _, _ = call(
            functools.partial(end_kernel, n, t),
            "end",
            (narrow, slots, slots),
            [scratch],
            left_last,
            rights[-1],
            mixed,
            pair,
            gating,
            table,
            w_out,
            left_slots,
            right_slots,
            alias={7: 1, 8: 2},
        )
        return out.reshape(t, t, width)

    placed = (P(("groups", "row"), "col", None), P("groups")) + (P(),) * 8
    return jax.shard_map(
        per_device, mesh=mesh, in_specs=placed, out_specs=P(("groups", "row"), "col", None), check_vma=False
    )
```

```python
import functools

import jax
import jax.numpy as jnp
from jax import lax
from jax.experimental import pallas as pl
from jax.experimental.pallas import tpu as pltpu
from jax.sharding import PartitionSpec as P

F32, BF16 = jnp.float32, jnp.bfloat16


def dot(a, b):
    return jnp.dot(a, b, preferred_element_type=F32)


def split(values):
    high = values.astype(BF16)
    return jnp.concatenate([high, (values - high.astype(F32)).astype(BF16)], axis=1)


def constants(width):
    rows = lax.broadcasted_iota(jnp.int32, (2 * width, width), 0)
    cols = lax.broadcasted_iota(jnp.int32, (2 * width, width), 1)
    mean = jnp.full((2 * width, width), 1.0 / width, F32)
    center = jnp.where((rows == cols) | (rows == cols + width), 1.0, 0.0) - mean
    return center.astype(BF16), mean.astype(BF16)


def scaled(center, mean, gain, shift):
    spread = dot(split(center * center), mean)
    return (center * lax.rsqrt(spread + 1e-05) * gain + shift).astype(BF16)


def norm_pair(values, consts, gain, shift):
    return scaled(dot(values, consts[0][: values.shape[1]]), consts[1], gain, shift)


def norm_mixed(values, consts, gain, shift):
    return scaled(dot(split(values), consts[0]), consts[1], gain, shift)


def gated(normed, weights, bias, width):
    product = dot(normed, weights) + bias
    return (jnp.tanh(product[:, width:]) + 1.0) * product[:, :width]


def gate(normed, weights, bias):
    return 0.5 * jnp.tanh(dot(normed, weights) + bias) + 0.5


def masked(values, outer, inner):
    t = outer.shape[0]
    grid = jnp.concatenate([outer[k : k + 1] * inner for k in range(t)], axis=0)
    return (values * grid).astype(BF16)


def mix(out_ref, old_ref, lefts, rights, first, last, left_at, right_at, t):
    width = out_ref.shape[1]
    for base in range(0, t, 8):
        if old_ref is None:
            total = (jnp.zeros((t, width), F32),) * 8
        else:
            total = tuple(old_ref[pl.ds((base + i) * t, t), :] for i in range(8))

        def slot(s, total):
            ls, rs = left_at(s), right_at(s)

            def step(q, total):
                for u in range(4):
                    at = pl.multiple_of((q * 4 + u) * t, 8)
                    row = rights[rs, pl.ds(at, t), :]
                    total = tuple(total[i] + lefts[ls, pl.ds(at + base + i, 1), :] * row for i in range(8))
                return total

            return lax.fori_loop(0, t // 4, step, total)

        total = lax.fori_loop(first, last, slot, total)
        for i in range(8):
            out_ref[pl.ds((base + i) * t, t), :] = total[i]


def finish(pair, mixed, gating, consts, gain, shift, weights, bias):
    normout = norm_mixed(mixed, consts, gain, shift)
    return (pair.astype(F32) + gating * (dot(normout, weights) + bias)).astype(BF16)


TABLE_MASK = 24


def in_norm(table, u):
    return table[u : u + 1], table[2 + u : 3 + u]


def out_norm(table, u):
    return table[4 + u : 5 + u], table[6 + u : 7 + u]


def half_bias(table, u, first, last):
    return jnp.concatenate([table[k : k + 1] for k in range(10 + 5 * u + first, 10 + 5 * u + last)], axis=1) * 0.5


def mask_of(table, b, t):
    return table[pl.ds(pl.multiple_of(TABLE_MASK + b * t, 8), t), :]


def sides(values_ref, wide, left_at, right_at, outer, inner, consts, table, weights):
    t, width = outer.shape
    wide[...] = values_ref[...].astype(F32)
    values = jnp.concatenate([wide[pl.ds(k, t, stride=t), :] for k in range(t)], axis=0).astype(BF16)
    normed = norm_pair(values, consts, *in_norm(table, 0))
    for k, target in enumerate((left_at, right_at)):
        span = slice(2 * k * width, 2 * (k + 1) * width)
        side = gated(normed, weights[0, :, span], half_bias(table, 0, 2 * k, 2 * k + 2), width)
        target[...] = masked(side, outer, inner).astype(F32)


def gate_of(values, consts, table, weights, u):
    normed = norm_pair(values, consts, *in_norm(table, u))
    return gate(normed, weights[u, :, 4 * values.shape[1] :], half_bias(table, u, 4, 5))


def place(b, n):
    return b // 2 + lax.rem(b, 2) * (n // 2)


def placed_at(r, n):
    return lax.rem(r, n // 2) * 2 + r // (n // 2)


def early_pairs(late, n):
    return jnp.where(late == n - 1, n - 1, n - 2), lambda i: i + jnp.where(i >= late, 1, 0)


def late_pairs(late, n):
    return jnp.where(late == n - 1, 1, 2), lambda i: jnp.where(i == 0, n - 1, late)


def own_kernel(t, pair, table, w_in, weights, row_l, row_r, gating, wide):
    r, c = lax.axis_index("row"), lax.axis_index("col")
    consts = constants(wide.shape[1])
    weights[...] = w_in[...] * 0.5
    outer, inner = mask_of(table, c, t), mask_of(table, r, t)
    sides(pair, wide, row_l.at[0], row_r.at[0], outer, inner, consts, table, weights)
    gating[...] = gate_of(pair[...], consts, table, weights, 0)


def early_kernel(n, t, col, table, weights, col_l, col_r, wide):
    r, c = lax.axis_index("row"), lax.axis_index("col")
    outer, inner = mask_of(table, placed_at(r, n), t), mask_of(table, c, t)
    sides(col, wide, col_l.at[0], col_r.at[0], outer, inner, constants(wide.shape[1]), table, weights)


def first_sides_kernel(n, t, *refs):
    rows, (col, table, weights) = refs[: n - 2], refs[n - 2 : n + 1]
    row_l, row_r, col_l, col_r, wide = refs[n + 5 :]
    r, c = lax.axis_index("row"), lax.axis_index("col")
    consts = constants(wide.shape[1])
    here, there = mask_of(table, r, t), mask_of(table, c, t)
    for s, block in enumerate(rows, 1):
        outer = mask_of(table, c ^ s, t)
        sides(block, wide, row_l.at[s], row_r.at[s], outer, here, consts, table, weights)
    outer = mask_of(table, placed_at(r ^ 1, n), t)
    sides(col, wide, col_l.at[1], col_r.at[1], outer, there, consts, table, weights)


def second_sides_kernel(n, t, *refs):
    cols, (table, weights, row_r) = refs[: n - 3], refs[n - 3 : n]
    col_l, col_r, mixed, wide = refs[n + 2 :]
    r, c = lax.axis_index("row"), lax.axis_index("col")
    consts = constants(wide.shape[1])
    there = mask_of(table, c, t)
    for s, block in enumerate(cols, 2):
        outer = mask_of(table, placed_at(r ^ s, n), t)
        sides(block, wide, col_l.at[s], col_r.at[s], outer, there, consts, table, weights)
    count, slot = early_pairs(c ^ placed_at(r ^ (n - 1), n), n)
    mix(mixed, None, col_l, row_r, 0, count, lambda i: r ^ place(c ^ slot(i), n), slot, t)


def last_column_kernel(n, t, col, table, weights, left_in, right_in, col_l, col_r, wide):
    r, c = lax.axis_index("row"), lax.axis_index("col")
    outer, inner = mask_of(table, placed_at(r ^ (n - 1), n), t), mask_of(table, c, t)
    consts = constants(wide.shape[1])
    sides(col, wide, col_l.at[n - 1], col_r.at[n - 1], outer, inner, consts, table, weights)


def mirror_kernel(n, t, *refs):
    row, cols, (table, weights, w_out) = refs[0], refs[1 : n + 1], refs[n + 1 : n + 4]
    col_l, old = refs[n + 6 : n + 8]
    left_ref, row_l, row_r, mixed, wide, held = refs[n + 8 :]
    width = wide.shape[1]
    r, c = lax.axis_index("row"), lax.axis_index("col")
    consts = constants(width)
    here, there = mask_of(table, r, t), mask_of(table, c, t)
    outer = mask_of(table, c ^ (n - 1), t)
    sides(row, wide, row_l.at[n - 1], row_r.at[n - 1], outer, here, consts, table, weights)
    count, slot = late_pairs(c ^ placed_at(r ^ (n - 1), n), n)
    mix(mixed, old, col_l, row_r, 0, count, lambda i: r ^ place(c ^ slot(i), n), slot, t)
    for s in range(n):
        held[s] = cols[s][...]
    pair = held[r ^ place(r, n)]
    updated = finish(pair, mixed[...], gate_of(pair, consts, table, weights, 0), consts, *out_norm(table, 0), w_out[0], table[8:9])
    normed = norm_pair(updated, consts, *in_norm(table, 1))
    side = gated(normed, weights[1, :, : 2 * width], half_bias(table, 1, 0, 2), width)
    left_ref[...] = masked(side, there, here)


def own_end_kernel(n, t, row_l, col_r, table, weights, pair, gating, w_out, pair_ref, right_ref, mixed):
    width = mixed.shape[1]
    r, c = lax.axis_index("row"), lax.axis_index("col")
    consts = constants(width)
    mix(mixed, None, row_l, col_r, 0, n, lambda s: s, lambda s: r ^ place(c ^ s, n), t)
    updated = finish(pair[...], mixed[...], gating[...], consts, *out_norm(table, 0), w_out[0], table[8:9])
    pair_ref[...] = updated
    normed = norm_pair(updated, consts, *in_norm(table, 1))
    side = gated(normed, weights[1, :, 2 * width : 4 * width], half_bias(table, 1, 2, 4), width)
    right_ref[...] = masked(side, mask_of(table, r, t), mask_of(table, c, t))


def gate_kernel(pair, table, weights, gating):
    gating[...] = gate_of(pair[...], constants(pair.shape[1]), table, weights, 1)


def left_kernel(n, *refs):
    for s in range(n - 1):
        refs[n - 1][s] = refs[s][...].astype(F32)


def widen_kernel(block, out):
    out[...] = block[...].astype(F32)


def right_lot(late, first, last):
    skips = (late >= first) & (late < last)
    count = last - first - jnp.where(skips, 1, 0)
    return count, lambda i: first + i + jnp.where(skips & (first + i >= late), 1, 0)


def near_kernel(n, t, own, core, lefts, rights, mixed):
    r, c = lax.axis_index("row"), lax.axis_index("col")
    rights[0] = own[...].astype(F32)
    rights[1] = core[...].astype(F32)
    count, slot = right_lot(r ^ c ^ (n - 1), 0, 2)
    mix(mixed, None, lefts, rights, 0, count, lambda i: r ^ c ^ slot(i), slot, t)


def far_kernel(n, t, *refs):
    sources, (lefts, _, old, rights, mixed) = refs[: n - 3], refs[n - 3 :]
    r, c = lax.axis_index("row"), lax.axis_index("col")
    for s, source in enumerate(sources, 2):
        rights[s] = source[...].astype(F32)
    count, slot = right_lot(r ^ c ^ (n - 1), 2, n - 1)
    mix(mixed, old, lefts, rights, 0, count, lambda i: r ^ c ^ slot(i), slot, t)


def end_kernel(n, t, left, right, old, pair, gating, table, w_out, left_in, right_in, out, lefts, rights, mixed):
    r, c = lax.axis_index("row"), lax.axis_index("col")
    lefts[n - 1] = left[...]
    rights[n - 1] = right[...].astype(F32)
    count, slot = late_pairs(r ^ c ^ (n - 1), n)
    mix(mixed, old, lefts, rights, 0, count, slot, lambda i: r ^ c ^ slot(i), t)
    consts = constants(mixed.shape[1])
    out[...] = finish(pair[...], mixed[...], gating[...], consts, *out_norm(table, 1), w_out[1], table[9:10])


def solution(mesh):
    n = mesh.shape["col"]

    def gather(block, axis, after):
        held, step = {0: block}, n // 2
        while step:
            for s, part in list(held.items()):
                part = lax.optimization_barrier((part, after(s, step)))[0]
                held[s ^ step] = lax.ppermute(part, axis, [(k, k ^ step) for k in range(n)])
            step //= 2
        return [held[s] for s in range(n)]

    def direct(block, last):
        return [block] + [
            lax.ppermute(last if s == n - 1 else block, "row", [(k, k ^ s) for k in range(n)]) for s in range(1, n)
        ]

    def mirrored(block):
        pairs = [(a * n + z, (z // 2 + z % 2 * (n // 2)) * n + a) for a in range(n) for z in range(n)]
        return lax.ppermute(block, ("row", "col"), pairs)

    def per_device(pair, token_mask, in_gain, in_shift, w_in, bias_in, out_gain, out_shift, w_out, bias_out):
        t, _, width = pair.shape
        area = (t * t, width)
        narrow, broad = jax.ShapeDtypeStruct(area, BF16), jax.ShapeDtypeStruct(area, F32)
        slots = jax.ShapeDtypeStruct((n,) + area, F32)
        scratch = pltpu.VMEM(area, F32)

        def call(kernel, name, outs, scratches, *operands, alias=None, weight=0):
            return pl.pallas_call(
                kernel,
                out_shape=outs,
                scratch_shapes=scratches,
                input_output_aliases=alias or {},
                cost_estimate=pl.CostEstimate(
                    flops=weight * 10**9, bytes_accessed=weight * 10**6, transcendentals=0
                ) if weight else None,

                compiler_params=pltpu.CompilerParams(vmem_limit_bytes=(16 + n) * 1024 * 1024),
                name=name,
            )(*operands)

        pair = pair.reshape(area)
        col_block = mirrored(pair)
        mask = jnp.broadcast_to(token_mask.astype(F32)[:, None], (n * t, width))
        vectors = [in_gain, in_shift, out_gain, out_shift, bias_out, bias_in.reshape(-1, width)]
        table = jnp.concatenate(vectors + [jnp.zeros((TABLE_MASK - 20, width), F32), mask])
        weights, row_l, row_r, gating = call(
            functools.partial(own_kernel, t),
            "own_sides",
            (jax.ShapeDtypeStruct(w_in.shape, BF16), slots, slots, broad),
            [scratch],
            pair,
            table,
            w_in,
        )
        own_l = row_l
        col_l, col_r = call(
            functools.partial(early_kernel, n, t), "early_sides", (slots,) * 2, [scratch], col_block, table, weights
        )
        rows = gather(pair, "col", lambda s, step: (own_l, col_l) if s else ())
        cols = direct(*(lax.optimization_barrier((col_block, after))[0] for after in (own_l, own_l)))
        row_l, row_r, col_l, col_r = call(
            functools.partial(first_sides_kernel, n, t),
            "first_sides",
            (slots,) * 4,
            [scratch],
            *rows[1:-1],
            cols[1],
            table,
            weights,
            row_l,
            row_r,
            col_l,
            col_r,
            alias={n + 1: 0, n + 2: 1, n + 3: 2, n + 4: 3},
        )
        col_l, col_r, mixed = call(
            functools.partial(second_sides_kernel, n, t),
            "second_sides",
            (slots, slots, broad),
            [scratch],
            *cols[2:-1],
            table,
            weights,
            row_r,
            col_l,
            col_r,
            alias={n: 0, n + 1: 1},
        )
        col_l, col_r = call(
            functools.partial(last_column_kernel, n, t),
            "last_column",
            (slots, slots),
            [scratch],
            cols[-1],
            table,
            weights,
            col_l,
            col_r,
            alias={3: 0, 4: 1},
            weight=30,
        )
        left, row_l, _ = call(
            functools.partial(mirror_kernel, n, t),
            "mirror_end",
            (narrow, slots, slots),
            [scratch] * 2 + [pltpu.VMEM((n,) + area, BF16)],
            rows[-1],
            *cols,
            table,
            weights,
            w_out,
            row_l,
            row_r,
            col_l,
            mixed,
            alias={n + 4: 1, n + 5: 2},
        )
        pair, right = call(
            functools.partial(own_end_kernel, n, t),
            "own_end",
            (narrow, narrow),
            [scratch],
            row_l,
            col_r,
            table,
            weights,
            pair,
            gating,
            w_out,
        )
        lefts = gather(left, "col", lambda s, step: ())
        left_slots = call(functools.partial(left_kernel, n), "left_slots", slots, [], *lefts[:-1], weight=20)
        core = lax.ppermute(right, "row", [(k, k ^ 1) for k in range(n)])
        right_slots, mixed = call(
            functools.partial(near_kernel, n, t), "near_slots", (slots, broad), [], right, core, left_slots
        )
        rights = gather(right, "row", lambda s, step: mixed if s else ())
        settled = lax.optimization_barrier((pair, left_slots))[0]
        gating = call(gate_kernel, "gate", broad, [], settled, table, weights)
        right_slots, mixed = call(
            functools.partial(far_kernel, n, t),
            "far_slots",
            (slots, broad),
            [],
            *rights[2:-1],
            left_slots,
            right_slots,
            mixed,
            alias={n - 2: 0, n - 1: 1},
        )
        left_last = call(widen_kernel, "left_last", broad, [], lefts[-1], weight=30)
        out, _, _ = call(
            functools.partial(end_kernel, n, t),
            "end",
            (narrow, slots, slots),
            [scratch],
            left_last,
            rights[-1],
            mixed,
            pair,
            gating,
            table,
            w_out,
            left_slots,
            right_slots,
            alias={7: 1, 8: 2},
        )
        return out.reshape(t, t, width)

    placed = (P(("groups", "row"), "col", None), P("groups")) + (P(),) * 8
    return jax.shard_map(
        per_device, mesh=mesh, in_specs=placed, out_specs=P(("groups", "row"), "col", None), check_vma=False
    )
```

```python
import functools

import jax
import jax.numpy as jnp
from jax import lax
from jax.experimental import pallas as pl
from jax.experimental.pallas import tpu as pltpu
from jax.sharding import PartitionSpec as P

F32, BF16 = jnp.float32, jnp.bfloat16


def dot(a, b):
    return jnp.dot(a, b, preferred_element_type=F32)


def split(values):
    high = values.astype(BF16)
    return jnp.concatenate([high, (values - high.astype(F32)).astype(BF16)], axis=1)


def constants(width):
    rows = lax.broadcasted_iota(jnp.int32, (2 * width, width), 0)
    cols = lax.broadcasted_iota(jnp.int32, (2 * width, width), 1)
    mean = jnp.full((2 * width, width), 1.0 / width, F32)
    center = jnp.where((rows == cols) | (rows == cols + width), 1.0, 0.0) - mean
    return center.astype(BF16), mean.astype(BF16)


def scaled(center, mean, gain, shift):
    spread = dot(split(center * center), mean)
    return (center * lax.rsqrt(spread + 1e-05) * gain + shift).astype(BF16)


def norm_pair(values, consts, gain, shift):
    return scaled(dot(values, consts[0][: values.shape[1]]), consts[1], gain, shift)


def norm_mixed(values, consts, gain, shift):
    return scaled(dot(split(values), consts[0]), consts[1], gain, shift)


def gated(normed, weights, bias, width):
    product = dot(normed, weights) + bias
    return (jnp.tanh(product[:, width:]) + 1.0) * product[:, :width]


def gate(normed, weights, bias):
    return 0.5 * jnp.tanh(dot(normed, weights) + bias) + 0.5


def masked(values, outer, inner):
    t = outer.shape[0]
    grid = jnp.concatenate([outer[k : k + 1] * inner for k in range(t)], axis=0)
    return (values * grid).astype(BF16)


def mix(out_ref, old_ref, lefts, rights, first, last, left_at, right_at, t):
    width = out_ref.shape[1]
    for base in range(0, t, 8):
        if old_ref is None:
            total = (jnp.zeros((t, width), F32),) * 8
        else:
            total = tuple(old_ref[pl.ds((base + i) * t, t), :] for i in range(8))

        def slot(s, total):
            ls, rs = left_at(s), right_at(s)

            def step(q, total):
                for u in range(4):
                    at = pl.multiple_of((q * 4 + u) * t, 8)
                    row = rights[rs, pl.ds(at, t), :]
                    total = tuple(total[i] + lefts[ls, pl.ds(at + base + i, 1), :] * row for i in range(8))
                return total

            return lax.fori_loop(0, t // 4, step, total)

        total = lax.fori_loop(first, last, slot, total)
        for i in range(8):
            out_ref[pl.ds((base + i) * t, t), :] = total[i]


def finish(pair, mixed, gating, consts, gain, shift, weights, bias):
    normout = norm_mixed(mixed, consts, gain, shift)
    return (pair.astype(F32) + gating * (dot(normout, weights) + bias)).astype(BF16)


TABLE_MASK = 24


def in_norm(table, u):
    return table[u : u + 1], table[2 + u : 3 + u]


def out_norm(table, u):
    return table[4 + u : 5 + u], table[6 + u : 7 + u]


def half_bias(table, u, first, last):
    return jnp.concatenate([table[k : k + 1] for k in range(10 + 5 * u + first, 10 + 5 * u + last)], axis=1) * 0.5


def mask_of(table, b, t):
    return table[pl.ds(pl.multiple_of(TABLE_MASK + b * t, 8), t), :]


def sides(values_ref, wide, left_at, right_at, outer, inner, consts, table, weights):
    t, width = outer.shape
    wide[...] = values_ref[...].astype(F32)
    values = jnp.concatenate([wide[pl.ds(k, t, stride=t), :] for k in range(t)], axis=0).astype(BF16)
    normed = norm_pair(values, consts, *in_norm(table, 0))
    for k, target in enumerate((left_at, right_at)):
        span = slice(2 * k * width, 2 * (k + 1) * width)
        side = gated(normed, weights[0, :, span], half_bias(table, 0, 2 * k, 2 * k + 2), width)
        target[...] = masked(side, outer, inner).astype(F32)


def gate_of(values, consts, table, weights, u):
    normed = norm_pair(values, consts, *in_norm(table, u))
    return gate(normed, weights[u, :, 4 * values.shape[1] :], half_bias(table, u, 4, 5))


def place(b, n):
    return b // 2 + lax.rem(b, 2) * (n // 2)


def placed_at(r, n):
    return lax.rem(r, n // 2) * 2 + r // (n // 2)


def early_pairs(late, n):
    return jnp.where(late == n - 1, n - 1, n - 2), lambda i: i + jnp.where(i >= late, 1, 0)


def late_pairs(late, n):
    return jnp.where(late == n - 1, 1, 2), lambda i: jnp.where(i == 0, n - 1, late)


def own_kernel(t, pair, table, w_in, weights, row_l, row_r, gating, wide):
    r, c = lax.axis_index("row"), lax.axis_index("col")
    consts = constants(wide.shape[1])
    weights[...] = w_in[...] * 0.5
    outer, inner = mask_of(table, c, t), mask_of(table, r, t)
    sides(pair, wide, row_l.at[0], row_r.at[0], outer, inner, consts, table, weights)
    gating[...] = gate_of(pair[...], consts, table, weights, 0)


def early_kernel(n, t, col, table, weights, col_l, col_r, wide):
    r, c = lax.axis_index("row"), lax.axis_index("col")
    outer, inner = mask_of(table, placed_at(r, n), t), mask_of(table, c, t)
    sides(col, wide, col_l.at[0], col_r.at[0], outer, inner, constants(wide.shape[1]), table, weights)


def first_sides_kernel(n, t, *refs):
    rows, (col, table, weights) = refs[: n - 2], refs[n - 2 : n + 1]
    row_l, row_r, col_l, col_r, wide = refs[n + 5 :]
    r, c = lax.axis_index("row"), lax.axis_index("col")
    consts = constants(wide.shape[1])
    here, there = mask_of(table, r, t), mask_of(table, c, t)
    for s, block in enumerate(rows, 1):
        outer = mask_of(table, c ^ s, t)
        sides(block, wide, row_l.at[s], row_r.at[s], outer, here, consts, table, weights)
    outer = mask_of(table, placed_at(r ^ 1, n), t)
    sides(col, wide, col_l.at[1], col_r.at[1], outer, there, consts, table, weights)


def second_sides_kernel(n, t, *refs):
    cols, (table, weights, row_r) = refs[: n - 3], refs[n - 3 : n]
    col_l, col_r, mixed, wide = refs[n + 2 :]
    r, c = lax.axis_index("row"), lax.axis_index("col")
    consts = constants(wide.shape[1])
    there = mask_of(table, c, t)
    for s, block in enumerate(cols, 2):
        outer = mask_of(table, placed_at(r ^ s, n), t)
        sides(block, wide, col_l.at[s], col_r.at[s], outer, there, consts, table, weights)
    count, slot = early_pairs(c ^ placed_at(r ^ (n - 1), n), n)
    mix(mixed, None, col_l, row_r, 0, count, lambda i: r ^ place(c ^ slot(i), n), slot, t)


def last_row_kernel(n, t, row, table, weights, left_in, right_in, row_l, row_r, wide):
    r, c = lax.axis_index("row"), lax.axis_index("col")
    outer, inner = mask_of(table, c ^ (n - 1), t), mask_of(table, r, t)
    consts = constants(wide.shape[1])
    sides(row, wide, row_l.at[n - 1], row_r.at[n - 1], outer, inner, consts, table, weights)


def mirror_kernel(n, t, *refs):
    cols, (table, weights, w_out, row_r) = refs[:n], refs[n : n + 4]
    old = refs[n + 6]
    left_ref, col_l, col_r, mixed, wide, held = refs[n + 7 :]
    width = wide.shape[1]
    r, c = lax.axis_index("row"), lax.axis_index("col")
    consts = constants(width)
    here, there = mask_of(table, r, t), mask_of(table, c, t)
    outer = mask_of(table, placed_at(r ^ (n - 1), n), t)
    sides(cols[-1], wide, col_l.at[n - 1], col_r.at[n - 1], outer, there, consts, table, weights)
    count, slot = late_pairs(c ^ placed_at(r ^ (n - 1), n), n)
    mix(mixed, old, col_l, row_r, 0, count, lambda i: r ^ place(c ^ slot(i), n), slot, t)
    for s in range(n):
        held[s] = cols[s][...]
    pair = held[r ^ place(r, n)]
    updated = finish(pair, mixed[...], gate_of(pair, consts, table, weights, 0), consts, *out_norm(table, 0), w_out[0], table[8:9])
    normed = norm_pair(updated, consts, *in_norm(table, 1))
    side = gated(normed, weights[1, :, : 2 * width], half_bias(table, 1, 0, 2), width)
    left_ref[...] = masked(side, there, here)


def own_end_kernel(n, t, row_l, col_r, table, weights, pair, gating, w_out, pair_ref, right_ref, mixed):
    width = mixed.shape[1]
    r, c = lax.axis_index("row"), lax.axis_index("col")
    consts = constants(width)
    mix(mixed, None, row_l, col_r, 0, n, lambda s: s, lambda s: r ^ place(c ^ s, n), t)
    updated = finish(pair[...], mixed[...], gating[...], consts, *out_norm(table, 0), w_out[0], table[8:9])
    pair_ref[...] = updated
    normed = norm_pair(updated, consts, *in_norm(table, 1))
    side = gated(normed, weights[1, :, 2 * width : 4 * width], half_bias(table, 1, 2, 4), width)
    right_ref[...] = masked(side, mask_of(table, r, t), mask_of(table, c, t))


def gate_kernel(pair, table, weights, gating):
    gating[...] = gate_of(pair[...], constants(pair.shape[1]), table, weights, 1)


def left_kernel(n, *refs):
    for s in range(n - 1):
        refs[n - 1][s] = refs[s][...].astype(F32)


def widen_kernel(block, out):
    out[...] = block[...].astype(F32)


def right_lot(late, first, last):
    skips = (late >= first) & (late < last)
    count = last - first - jnp.where(skips, 1, 0)
    return count, lambda i: first + i + jnp.where(skips & (first + i >= late), 1, 0)


def near_kernel(n, t, own, core, lefts, rights, mixed):
    r, c = lax.axis_index("row"), lax.axis_index("col")
    rights[0] = own[...].astype(F32)
    rights[1] = core[...].astype(F32)
    count, slot = right_lot(r ^ c ^ (n - 1), 0, 2)
    mix(mixed, None, lefts, rights, 0, count, lambda i: r ^ c ^ slot(i), slot, t)


def far_kernel(n, t, *refs):
    sources, (lefts, _, old, rights, mixed) = refs[: n - 3], refs[n - 3 :]
    r, c = lax.axis_index("row"), lax.axis_index("col")
    for s, source in enumerate(sources, 2):
        rights[s] = source[...].astype(F32)
    count, slot = right_lot(r ^ c ^ (n - 1), 2, n - 1)
    mix(mixed, old, lefts, rights, 0, count, lambda i: r ^ c ^ slot(i), slot, t)


def end_kernel(n, t, left, right, old, pair, gating, table, w_out, left_in, right_in, out, lefts, rights, mixed):
    r, c = lax.axis_index("row"), lax.axis_index("col")
    lefts[n - 1] = left[...]
    rights[n - 1] = right[...].astype(F32)
    count, slot = late_pairs(r ^ c ^ (n - 1), n)
    mix(mixed, old, lefts, rights, 0, count, slot, lambda i: r ^ c ^ slot(i), t)
    consts = constants(mixed.shape[1])
    out[...] = finish(pair[...], mixed[...], gating[...], consts, *out_norm(table, 1), w_out[1], table[9:10])


def solution(mesh):
    n = mesh.shape["col"]

    def gather(block, axis, after):
        held, step = {0: block}, n // 2
        while step:
            for s, part in list(held.items()):
                part = lax.optimization_barrier((part, after(s, step)))[0]
                held[s ^ step] = lax.ppermute(part, axis, [(k, k ^ step) for k in range(n)])
            step //= 2
        return [held[s] for s in range(n)]

    def mirrored(block):
        pairs = [(a * n + z, (z // 2 + z % 2 * (n // 2)) * n + a) for a in range(n) for z in range(n)]
        return lax.ppermute(block, ("row", "col"), pairs)

    def per_device(pair, token_mask, in_gain, in_shift, w_in, bias_in, out_gain, out_shift, w_out, bias_out):
        t, _, width = pair.shape
        area = (t * t, width)
        narrow, broad = jax.ShapeDtypeStruct(area, BF16), jax.ShapeDtypeStruct(area, F32)
        slots = jax.ShapeDtypeStruct((n,) + area, F32)
        scratch = pltpu.VMEM(area, F32)

        def call(kernel, name, outs, scratches, *operands, alias=None, weight=0):
            return pl.pallas_call(
                kernel,
                out_shape=outs,
                scratch_shapes=scratches,
                input_output_aliases=alias or {},
                cost_estimate=pl.CostEstimate(
                    flops=weight * 10**9, bytes_accessed=weight * 10**6, transcendentals=0
                ) if weight else None,

                compiler_params=pltpu.CompilerParams(vmem_limit_bytes=(16 + n) * 1024 * 1024),
                name=name,
            )(*operands)

        pair = pair.reshape(area)
        col_block = mirrored(pair)
        mask = jnp.broadcast_to(token_mask.astype(F32)[:, None], (n * t, width))
        vectors = [in_gain, in_shift, out_gain, out_shift, bias_out, bias_in.reshape(-1, width)]
        table = jnp.concatenate(vectors + [jnp.zeros((TABLE_MASK - 20, width), F32), mask])
        weights, row_l, row_r, gating = call(
            functools.partial(own_kernel, t),
            "own_sides",
            (jax.ShapeDtypeStruct(w_in.shape, BF16), slots, slots, broad),
            [scratch],
            pair,
            table,
            w_in,
        )
        own_l = row_l
        col_l, col_r = call(
            functools.partial(early_kernel, n, t), "early_sides", (slots,) * 2, [scratch], col_block, table, weights
        )
        rows = gather(pair, "col", lambda s, step: (own_l, col_l) if s else ())
        ready = lax.optimization_barrier((col_block, own_l))[0]
        core = lax.ppermute(ready, "row", [(k, k ^ 1) for k in range(n)])
        row_l, row_r, col_l, col_r = call(
            functools.partial(first_sides_kernel, n, t),
            "first_sides",
            (slots,) * 4,
            [scratch],
            *rows[1:-1],
            core,
            table,
            weights,
            row_l,
            row_r,
            col_l,
            col_r,
            alias={n + 1: 0, n + 2: 1, n + 3: 2, n + 4: 3},
        )
        cols = gather(ready, "row", lambda s, step: row_l if s else ())
        cols[1] = core
        col_l, col_r, mixed = call(
            functools.partial(second_sides_kernel, n, t),
            "second_sides",
            (slots, slots, broad),
            [scratch],
            *cols[2:-1],
            table,
            weights,
            row_r,
            col_l,
            col_r,
            alias={n: 0, n + 1: 1},
        )
        row_l, row_r = call(
            functools.partial(last_row_kernel, n, t),
            "last_row",
            (slots, slots),
            [scratch],
            rows[-1],
            table,
            weights,
            row_l,
            lax.optimization_barrier((row_r, mixed))[0],
            alias={3: 0, 4: 1},
            weight=1,
        )
        left, _, col_r = call(
            functools.partial(mirror_kernel, n, t),
            "mirror_end",
            (narrow, slots, slots),
            [scratch] * 2 + [pltpu.VMEM((n,) + area, BF16)],
            *cols,
            table,
            weights,
            w_out,
            row_r,
            col_l,
            col_r,
            mixed,
            alias={n + 4: 1, n + 5: 2},
        )
        pair, right = call(
            functools.partial(own_end_kernel, n, t),
            "own_end",
            (narrow, narrow),
            [scratch],
            row_l,
            col_r,
            table,
            weights,
            pair,
            gating,
            w_out,
        )
        lefts = gather(left, "col", lambda s, step: ())
        left_slots = call(functools.partial(left_kernel, n), "left_slots", slots, [], *lefts[:-1], weight=20)
        core = lax.ppermute(right, "row", [(k, k ^ 1) for k in range(n)])
        right_slots, mixed = call(
            functools.partial(near_kernel, n, t), "near_slots", (slots, broad), [], right, core, left_slots
        )
        rights = gather(right, "row", lambda s, step: mixed if s else ())
        settled = lax.optimization_barrier((pair, left_slots))[0]
        gating = call(gate_kernel, "gate", broad, [], settled, table, weights)
        right_slots, mixed = call(
            functools.partial(far_kernel, n, t),
            "far_slots",
            (slots, broad),
            [],
            *rights[2:-1],
            left_slots,
            right_slots,
            mixed,
            alias={n - 2: 0, n - 1: 1},
        )
        left_last = call(widen_kernel, "left_last", broad, [], lefts[-1], weight=30)
        out, _, _ = call(
            functools.partial(end_kernel, n, t),
            "end",
            (narrow, slots, slots),
            [scratch],
            left_last,
            rights[-1],
            mixed,
            pair,
            gating,
            table,
            w_out,
            left_slots,
            right_slots,
            alias={7: 1, 8: 2},
        )
        return out.reshape(t, t, width)

    placed = (P(("groups", "row"), "col", None), P("groups")) + (P(),) * 8
    return jax.shard_map(
        per_device, mesh=mesh, in_specs=placed, out_specs=P(("groups", "row"), "col", None), check_vma=False
    )
```

```python
import functools

import jax
import jax.numpy as jnp
from jax import lax
from jax.experimental import pallas as pl
from jax.experimental.pallas import tpu as pltpu
from jax.sharding import PartitionSpec as P

F32, BF16 = jnp.float32, jnp.bfloat16


def dot(a, b):
    return jnp.dot(a, b, preferred_element_type=F32)


def split(values):
    high = values.astype(BF16)
    return jnp.concatenate([high, (values - high.astype(F32)).astype(BF16)], axis=1)


def constants(width):
    rows = lax.broadcasted_iota(jnp.int32, (2 * width, width), 0)
    cols = lax.broadcasted_iota(jnp.int32, (2 * width, width), 1)
    mean = jnp.full((2 * width, width), 1.0 / width, F32)
    center = jnp.where((rows == cols) | (rows == cols + width), 1.0, 0.0) - mean
    return center.astype(BF16), mean.astype(BF16)


def scaled(center, mean, gain, shift):
    spread = dot(split(center * center), mean)
    return (center * lax.rsqrt(spread + 1e-05) * gain + shift).astype(BF16)


def norm_pair(values, consts, gain, shift):
    return scaled(dot(values, consts[0][: values.shape[1]]), consts[1], gain, shift)


def norm_mixed(values, consts, gain, shift):
    return scaled(dot(split(values), consts[0]), consts[1], gain, shift)


def gated(normed, weights, bias, width):
    product = dot(normed, weights) + bias
    return (jnp.tanh(product[:, width:]) + 1.0) * product[:, :width]


def gate(normed, weights, bias):
    return 0.5 * jnp.tanh(dot(normed, weights) + bias) + 0.5


def masked(values, outer, inner):
    t = outer.shape[0]
    grid = jnp.concatenate([outer[k : k + 1] * inner for k in range(t)], axis=0)
    return (values * grid).astype(BF16)


def mix(out_ref, old_ref, lefts, rights, first, last, left_at, right_at, t):
    width = out_ref.shape[1]
    for base in range(0, t, 8):
        if old_ref is None:
            total = (jnp.zeros((t, width), F32),) * 8
        else:
            total = tuple(old_ref[pl.ds((base + i) * t, t), :] for i in range(8))

        def slot(s, total):
            ls, rs = left_at(s), right_at(s)

            def step(q, total):
                for u in range(4):
                    at = pl.multiple_of((q * 4 + u) * t, 8)
                    row = rights[rs, pl.ds(at, t), :]
                    total = tuple(total[i] + lefts[ls, pl.ds(at + base + i, 1), :] * row for i in range(8))
                return total

            return lax.fori_loop(0, t // 4, step, total)

        total = lax.fori_loop(first, last, slot, total)
        for i in range(8):
            out_ref[pl.ds((base + i) * t, t), :] = total[i]


def finish(pair, mixed, gating, consts, gain, shift, weights, bias):
    normout = norm_mixed(mixed, consts, gain, shift)
    return (pair.astype(F32) + gating * (dot(normout, weights) + bias)).astype(BF16)


TABLE_MASK = 24


def in_norm(table, u):
    return table[u : u + 1], table[2 + u : 3 + u]


def out_norm(table, u):
    return table[4 + u : 5 + u], table[6 + u : 7 + u]


def half_bias(table, u, first, last):
    return jnp.concatenate([table[k : k + 1] for k in range(10 + 5 * u + first, 10 + 5 * u + last)], axis=1) * 0.5


def mask_of(table, b, t):
    return table[pl.ds(pl.multiple_of(TABLE_MASK + b * t, 8), t), :]


def sides(values_ref, wide, left_at, right_at, outer, inner, consts, table, weights):
    t, width = outer.shape
    wide[...] = values_ref[...].astype(F32)
    values = jnp.concatenate([wide[pl.ds(k, t, stride=t), :] for k in range(t)], axis=0).astype(BF16)
    normed = norm_pair(values, consts, *in_norm(table, 0))
    for k, target in enumerate((left_at, right_at)):
        span = slice(2 * k * width, 2 * (k + 1) * width)
        side = gated(normed, weights[0, :, span], half_bias(table, 0, 2 * k, 2 * k + 2), width)
        target[...] = masked(side, outer, inner).astype(F32)


def gate_of(values, consts, table, weights, u):
    normed = norm_pair(values, consts, *in_norm(table, u))
    return gate(normed, weights[u, :, 4 * values.shape[1] :], half_bias(table, u, 4, 5))


def place(b, n):
    return b // 2 + lax.rem(b, 2) * (n // 2)


def placed_at(r, n):
    return lax.rem(r, n // 2) * 2 + r // (n // 2)


def early_pairs(late, n):
    return jnp.where(late == n - 1, n - 1, n - 2), lambda i: i + jnp.where(i >= late, 1, 0)


def late_pairs(late, n):
    return jnp.where(late == n - 1, 1, 2), lambda i: jnp.where(i == 0, n - 1, late)


def own_kernel(t, pair, table, w_in, weights, row_l, row_r, gating, wide):
    r, c = lax.axis_index("row"), lax.axis_index("col")
    consts = constants(wide.shape[1])
    weights[...] = w_in[...] * 0.5
    outer, inner = mask_of(table, c, t), mask_of(table, r, t)
    sides(pair, wide, row_l.at[0], row_r.at[0], outer, inner, consts, table, weights)
    gating[...] = gate_of(pair[...], consts, table, weights, 0)


def early_kernel(n, t, col, table, weights, col_l, col_r, wide):
    r, c = lax.axis_index("row"), lax.axis_index("col")
    outer, inner = mask_of(table, placed_at(r, n), t), mask_of(table, c, t)
    sides(col, wide, col_l.at[0], col_r.at[0], outer, inner, constants(wide.shape[1]), table, weights)


def first_sides_kernel(n, t, *refs):
    rows, (col, table, weights) = refs[: n - 2], refs[n - 2 : n + 1]
    row_l, row_r, col_l, col_r, wide = refs[n + 5 :]
    r, c = lax.axis_index("row"), lax.axis_index("col")
    consts = constants(wide.shape[1])
    here, there = mask_of(table, r, t), mask_of(table, c, t)
    for s, block in enumerate(rows, 1):
        outer = mask_of(table, c ^ s, t)
        sides(block, wide, row_l.at[s], row_r.at[s], outer, here, consts, table, weights)
    outer = mask_of(table, placed_at(r ^ 1, n), t)
    sides(col, wide, col_l.at[1], col_r.at[1], outer, there, consts, table, weights)


def second_sides_kernel(n, t, *refs):
    cols, (table, weights, row_r) = refs[: n - 3], refs[n - 3 : n]
    col_l, col_r, mixed, wide = refs[n + 2 :]
    r, c = lax.axis_index("row"), lax.axis_index("col")
    consts = constants(wide.shape[1])
    there = mask_of(table, c, t)
    for s, block in enumerate(cols, 2):
        outer = mask_of(table, placed_at(r ^ s, n), t)
        sides(block, wide, col_l.at[s], col_r.at[s], outer, there, consts, table, weights)
    count, slot = early_pairs(c ^ placed_at(r ^ (n - 1), n), n)
    mix(mixed, None, col_l, row_r, 0, count, lambda i: r ^ place(c ^ slot(i), n), slot, t)


def last_row_kernel(n, t, row, table, weights, left_in, right_in, row_l, row_r, wide):
    r, c = lax.axis_index("row"), lax.axis_index("col")
    outer, inner = mask_of(table, c ^ (n - 1), t), mask_of(table, r, t)
    consts = constants(wide.shape[1])
    sides(row, wide, row_l.at[n - 1], row_r.at[n - 1], outer, inner, consts, table, weights)


def mirror_kernel(n, t, *refs):
    cols, (table, weights, w_out, row_r) = refs[:n], refs[n : n + 4]
    old = refs[n + 6]
    left_ref, col_l, col_r, mixed, wide, held = refs[n + 7 :]
    width = wide.shape[1]
    r, c = lax.axis_index("row"), lax.axis_index("col")
    consts = constants(width)
    here, there = mask_of(table, r, t), mask_of(table, c, t)
    outer = mask_of(table, placed_at(r ^ (n - 1), n), t)
    sides(cols[-1], wide, col_l.at[n - 1], col_r.at[n - 1], outer, there, consts, table, weights)
    count, slot = late_pairs(c ^ placed_at(r ^ (n - 1), n), n)
    mix(mixed, old, col_l, row_r, 0, count, lambda i: r ^ place(c ^ slot(i), n), slot, t)
    for s in range(n):
        held[s] = cols[s][...]
    pair = held[r ^ place(r, n)]
    updated = finish(pair, mixed[...], gate_of(pair, consts, table, weights, 0), consts, *out_norm(table, 0), w_out[0], table[8:9])
    normed = norm_pair(updated, consts, *in_norm(table, 1))
    side = gated(normed, weights[1, :, : 2 * width], half_bias(table, 1, 0, 2), width)
    left_ref[...] = masked(side, there, here)


def own_end_kernel(n, t, row_l, col_r, table, weights, pair, gating, w_out, pair_ref, right_ref, mixed):
    width = mixed.shape[1]
    r, c = lax.axis_index("row"), lax.axis_index("col")
    consts = constants(width)
    mix(mixed, None, row_l, col_r, 0, n, lambda s: s, lambda s: r ^ place(c ^ s, n), t)
    updated = finish(pair[...], mixed[...], gating[...], consts, *out_norm(table, 0), w_out[0], table[8:9])
    pair_ref[...] = updated
    normed = norm_pair(updated, consts, *in_norm(table, 1))
    side = gated(normed, weights[1, :, 2 * width : 4 * width], half_bias(table, 1, 2, 4), width)
    right_ref[...] = masked(side, mask_of(table, r, t), mask_of(table, c, t))


def gate_kernel(pair, table, weights, gating):
    gating[...] = gate_of(pair[...], constants(pair.shape[1]), table, weights, 1)


def left_kernel(n, *refs):
    for s in range(n - 1):
        refs[n - 1][s] = refs[s][...].astype(F32)


def widen_kernel(block, out):
    out[...] = block[...].astype(F32)


def right_lot(late, first, last):
    skips = (late >= first) & (late < last)
    count = last - first - jnp.where(skips, 1, 0)
    return count, lambda i: first + i + jnp.where(skips & (first + i >= late), 1, 0)


def near_kernel(n, t, own, core, lefts, rights, mixed):
    r, c = lax.axis_index("row"), lax.axis_index("col")
    rights[0] = own[...].astype(F32)
    rights[1] = core[...].astype(F32)
    count, slot = right_lot(r ^ c ^ (n - 1), 0, 2)
    mix(mixed, None, lefts, rights, 0, count, lambda i: r ^ c ^ slot(i), slot, t)


def far_kernel(n, t, *refs):
    sources, (lefts, _, old, rights, mixed) = refs[: n - 3], refs[n - 3 :]
    r, c = lax.axis_index("row"), lax.axis_index("col")
    for s, source in enumerate(sources, 2):
        rights[s] = source[...].astype(F32)
    count, slot = right_lot(r ^ c ^ (n - 1), 2, n - 1)
    mix(mixed, old, lefts, rights, 0, count, lambda i: r ^ c ^ slot(i), slot, t)


def end_kernel(n, t, left, right, old, pair, gating, table, w_out, left_in, right_in, out, lefts, rights, mixed):
    r, c = lax.axis_index("row"), lax.axis_index("col")
    lefts[n - 1] = left[...]
    rights[n - 1] = right[...].astype(F32)
    count, slot = late_pairs(r ^ c ^ (n - 1), n)
    mix(mixed, old, lefts, rights, 0, count, slot, lambda i: r ^ c ^ slot(i), t)
    consts = constants(mixed.shape[1])
    out[...] = finish(pair[...], mixed[...], gating[...], consts, *out_norm(table, 1), w_out[1], table[9:10])


def solution(mesh):
    n = mesh.shape["col"]

    def gather(block, axis, after):
        held, step = {0: block}, n // 2
        while step:
            for s, part in list(held.items()):
                part = lax.optimization_barrier((part, after(s, step)))[0]
                held[s ^ step] = lax.ppermute(part, axis, [(k, k ^ step) for k in range(n)])
            step //= 2
        return [held[s] for s in range(n)]

    def mirrored(block):
        pairs = [(a * n + z, (z // 2 + z % 2 * (n // 2)) * n + a) for a in range(n) for z in range(n)]
        return lax.ppermute(block, ("row", "col"), pairs)

    def per_device(pair, token_mask, in_gain, in_shift, w_in, bias_in, out_gain, out_shift, w_out, bias_out):
        t, _, width = pair.shape
        area = (t * t, width)
        narrow, broad = jax.ShapeDtypeStruct(area, BF16), jax.ShapeDtypeStruct(area, F32)
        slots = jax.ShapeDtypeStruct((n,) + area, F32)
        scratch = pltpu.VMEM(area, F32)

        def call(kernel, name, outs, scratches, *operands, alias=None, weight=0):
            return pl.pallas_call(
                kernel,
                out_shape=outs,
                scratch_shapes=scratches,
                input_output_aliases=alias or {},
                cost_estimate=pl.CostEstimate(
                    flops=weight * 10**9, bytes_accessed=weight * 10**6, transcendentals=0
                ) if weight else None,

                compiler_params=pltpu.CompilerParams(vmem_limit_bytes=(16 + n) * 1024 * 1024),
                name=name,
            )(*operands)

        pair = pair.reshape(area)
        col_block = mirrored(pair)
        mask = jnp.broadcast_to(token_mask.astype(F32)[:, None], (n * t, width))
        vectors = [in_gain, in_shift, out_gain, out_shift, bias_out, bias_in.reshape(-1, width)]
        table = jnp.concatenate(vectors + [jnp.zeros((TABLE_MASK - 20, width), F32), mask])
        weights, row_l, row_r, gating = call(
            functools.partial(own_kernel, t),
            "own_sides",
            (jax.ShapeDtypeStruct(w_in.shape, BF16), slots, slots, broad),
            [scratch],
            pair,
            table,
            w_in,
        )
        own_l = row_l
        col_l, col_r = call(
            functools.partial(early_kernel, n, t), "early_sides", (slots,) * 2, [scratch], col_block, table, weights
        )
        rows = gather(pair, "col", lambda s, step: (own_l, col_l) if s else ())
        ready = lax.optimization_barrier((col_block, own_l))[0]
        core = lax.optimization_barrier((col_block, col_l))[0]
        core = lax.ppermute(core, "row", [(k, k ^ 1) for k in range(n)])
        row_l, row_r, col_l, col_r = call(
            functools.partial(first_sides_kernel, n, t),
            "first_sides",
            (slots,) * 4,
            [scratch],
            *rows[1:-1],
            core,
            table,
            weights,
            row_l,
            row_r,
            col_l,
            col_r,
            alias={n + 1: 0, n + 2: 1, n + 3: 2, n + 4: 3},
        )
        cols = gather(ready, "row", lambda s, step: row_l if s else ())
        cols[1] = core
        col_l, col_r, mixed = call(
            functools.partial(second_sides_kernel, n, t),
            "second_sides",
            (slots, slots, broad),
            [scratch],
            *cols[2:-1],
            table,
            weights,
            row_r,
            col_l,
            col_r,
            alias={n: 0, n + 1: 1},
        )
        row_l, row_r = call(
            functools.partial(last_row_kernel, n, t),
            "last_row",
            (slots, slots),
            [scratch],
            rows[-1],
            table,
            weights,
            row_l,
            lax.optimization_barrier((row_r, mixed))[0],
            alias={3: 0, 4: 1},
            weight=1,
        )
        left, _, col_r = call(
            functools.partial(mirror_kernel, n, t),
            "mirror_end",
            (narrow, slots, slots),
            [scratch] * 2 + [pltpu.VMEM((n,) + area, BF16)],
            *cols,
            table,
            weights,
            w_out,
            row_r,
            col_l,
            col_r,
            mixed,
            alias={n + 4: 1, n + 5: 2},
        )
        pair, right = call(
            functools.partial(own_end_kernel, n, t),
            "own_end",
            (narrow, narrow),
            [scratch],
            row_l,
            col_r,
            table,
            weights,
            pair,
            gating,
            w_out,
        )
        lefts = gather(left, "col", lambda s, step: ())
        left_slots = call(functools.partial(left_kernel, n), "left_slots", slots, [], *lefts[:-1], weight=20)
        core = lax.ppermute(right, "row", [(k, k ^ 1) for k in range(n)])
        right_slots, mixed = call(
            functools.partial(near_kernel, n, t), "near_slots", (slots, broad), [], right, core, left_slots
        )
        rights = gather(right, "row", lambda s, step: mixed if s else ())
        settled = lax.optimization_barrier((pair, left_slots))[0]
        gating = call(gate_kernel, "gate", broad, [], settled, table, weights)
        right_slots, mixed = call(
            functools.partial(far_kernel, n, t),
            "far_slots",
            (slots, broad),
            [],
            *rights[2:-1],
            left_slots,
            right_slots,
            mixed,
            alias={n - 2: 0, n - 1: 1},
        )
        left_last = call(widen_kernel, "left_last", broad, [], lefts[-1], weight=30)
        out, _, _ = call(
            functools.partial(end_kernel, n, t),
            "end",
            (narrow, slots, slots),
            [scratch],
            left_last,
            rights[-1],
            mixed,
            pair,
            gating,
            table,
            w_out,
            left_slots,
            right_slots,
            alias={7: 1, 8: 2},
        )
        return out.reshape(t, t, width)

    placed = (P(("groups", "row"), "col", None), P("groups")) + (P(),) * 8
    return jax.shard_map(
        per_device, mesh=mesh, in_specs=placed, out_specs=P(("groups", "row"), "col", None), check_vma=False
    )
```
